32 devices in a mesh: fsdp: 8 (over y, x, core), tensor: 4 (over z).
Axes of the slice: x: 2, y: 2, z: 4, core: 2. Of those that a mesh axis runs over, the one named last changes fastest.
Arguments:
- momentum: bfloat16 [3, 2, 4096, 1536], P(None, None, 'fsdp', 'tensor'), may hold values from -6 to 6
- gradient: bfloat16 [3, 2, 4096, 1536], P(None, None, 'fsdp', 'tensor'), may hold values from -4.2 to 4.2
- right_in: bfloat16 [3, 2, 1536, 128], P(None, None, 'tensor'), may hold values from -6 to 6
- owners: int32 [3], replicated, may hold values from 0 to 3, as said below
Outputs:
- state_out: bfloat16 [8, 2, 4096, 1536], P('tensor', None, 'fsdp')
- left_out: float32 [8, 2, 4096, 128], P('tensor', None, 'fsdp')
- right_out: float32 [3, 2, 1536, 128], P(None, None, 'tensor')
The draws below stay inside these ranges and needn't reach their ends.
Inputs may be any that keep to these rules, and one draw needn't show every extreme that they name: `owners`: each entry is a tensor index. No tensor index takes more than 2 experts, and some index takes exactly 2.
All inputs are finite; a program needn't handle non-finite values.
Results may differ from the reference program's by a relative error of at most 0.0072.
Values may be sent and summed in bfloat16 or wider, within the bound.
A program may use at most 64 MiB of HBM per device.

```python
import math
import jax
import jax.numpy as jnp
from jax import lax

D = 4096
HID = 1536
RANK = 128
KINDS = 2
CAP = 2
EXPERTS = 3
SLOTS = 8


def draw_owners(key, part):
    key = jax.random.fold_in(key, 5)
    first, second, third = jax.random.split(key, 3)
    groups = SLOTS // CAP
    order = jax.random.permutation(first, SLOTS)
    rank_of = order // CAP
    upper_end = jax.random.randint(second, (), 0, 2)
    full_rank = upper_end * (groups - 1)
    other_rank = groups - 1 - full_rank
    level = jnp.where(rank_of == full_rank, 0, jnp.where(order == other_rank * CAP, 1, 2))
    score = level * SLOTS + jnp.arange(SLOTS)
    picked = order[jnp.argsort(score, stable=True)][:EXPERTS]
    chosen = (picked // CAP).astype(jnp.int32)
    return jax.random.permutation(third, chosen).astype(jnp.int32)


def mixed_field(left_part, right_part, noise_part, scale, limit):
    inner = left_part.shape[-1]
    product = jnp.einsum('ekdl,eklh->ekdh', left_part, right_part, precision=lax.Precision.HIGHEST)
    product = product / math.sqrt(inner)
    value = math.sqrt(0.85) * product + math.sqrt(0.15) * noise_part
    value = jnp.clip(value, -limit, limit) * scale
    return value.astype(jnp.bfloat16)


def draw_momentum(key, part):
    key = jax.random.fold_in(key, 11)
    first, second, third = jax.random.split(key, 3)
    inner = max(RANK // 4, 1)
    left_part = jax.random.normal(first, (EXPERTS, KINDS, D, inner), jnp.float32)
    right_part = jax.random.normal(second, (EXPERTS, KINDS, inner, HID), jnp.float32)
    noise_part = jax.random.normal(third, (EXPERTS, KINDS, D, HID), jnp.float32)
    return mixed_field(left_part, right_part, noise_part, 1.0, 6.0)


def draw_gradient(key, part):
    key = jax.random.fold_in(key, 17)
    first, second, third = jax.random.split(key, 3)
    inner = max(RANK // 4, 1)
    left_part = jax.random.normal(first, (EXPERTS, KINDS, D, inner), jnp.float32)
    right_part = jax.random.normal(second, (EXPERTS, KINDS, inner, HID), jnp.float32)
    noise_part = jax.random.normal(third, (EXPERTS, KINDS, D, HID), jnp.float32)
    return mixed_field(left_part, right_part, noise_part, 0.7, 6.0)


def level_of(rng, dims, pieces, smallest, high):
    gain = 1.0
    for dim, parts in pieces:
        steps = jax.random.uniform(jax.random.fold_in(jax.random.fold_in(rng, 6), dim), (parts,), jnp.float32, smallest / len(pieces), high / len(pieces))
        gain = gain * jnp.repeat(jnp.exp(steps), dims[dim] // parts).reshape((-1,) + (1,) * (len(dims) - 1 - dim))
    return gain


def normal_values(rng, shape, deviation, most, cuts=(), kind=jnp.bfloat16):
    entries = deviation * jax.random.normal(rng, shape, jnp.float32)
    if cuts:
        entries = entries * level_of(rng, shape, cuts, -0.22, 0.18)
    return jnp.clip(entries, -most, most).astype(kind)


def setup_inputs(seed: int = 0) -> dict:
    seeds = jax.random.split(jax.random.key(seed), 5)
    return {
        "momentum": draw_momentum(jax.random.fold_in(seeds[4], 71), 0),
        "gradient": draw_gradient(jax.random.fold_in(seeds[4], 71), 0),
        "right_in": normal_values(seeds[2], (EXPERTS, KINDS, HID, RANK), 1.0, 6.0, ((2, 4),)),
        "owners": draw_owners(jax.random.fold_in(seeds[4], 71), 0),
    }


ridge_term = 0.001
feedback = 0.1
epsilon = 1e-06

def orthonormal(panel, gram_total):
    eye_matrix = jnp.eye(gram_total.shape[-1], dtype=jnp.float32)
    lower_factor = jnp.linalg.cholesky(gram_total + ridge_term * eye_matrix)
    solved = jax.scipy.linalg.solve_triangular(lower_factor, jnp.swapaxes(panel, -1, -2), lower=True)
    return jnp.swapaxes(solved, -1, -2)

def reference(momentum, gradient, right_in, owners):
    highest = lax.Precision.HIGHEST
    summed = (momentum.astype(jnp.float32) + gradient.astype(jnp.float32)).astype(jnp.bfloat16)
    summed_wide = summed.astype(jnp.float32)
    panel = jnp.einsum('emrk,emkq->emrq', summed_wide, right_in.astype(jnp.float32), precision=highest)
    gram_total = jnp.einsum('emrq,emrs->emqs', panel, panel, precision=highest)
    ortho = orthonormal(panel, gram_total)
    ortho_low = ortho.astype(jnp.bfloat16).astype(jnp.float32)
    factor = jnp.einsum('emrk,emrq->emkq', summed_wide, ortho_low, precision=highest)
    mean_square = lax.optimization_barrier(jnp.mean(factor * factor, axis=2))
    right_out = factor * lax.rsqrt(mean_square + epsilon)[:, :, None, :]
    corrected = summed_wide - feedback * jnp.einsum('emrq,emkq->emrk', ortho, factor, precision=highest)
    fresh = corrected.astype(jnp.bfloat16)
    index_line = jnp.arange(EXPERTS, dtype=jnp.int32)
    same_owner = owners[:, None] == owners[None, :]
    earlier = index_line[None, :] < index_line[:, None]
    position = lax.optimization_barrier(jnp.sum((same_owner & earlier).astype(jnp.int32), axis=1)).astype(jnp.int32)
    slot = (owners * CAP + position).astype(jnp.int32)
    state_out = jnp.zeros((SLOTS, KINDS, D, HID), jnp.bfloat16).at[slot].set(fresh)
    left_out = jnp.zeros((SLOTS, KINDS, D, RANK), jnp.float32).at[slot].set(ortho * math.sqrt(D))
    return (state_out, left_out, right_out)
```

```python
import functools
import math

import jax
import jax.numpy as jnp
from jax import lax
from jax.experimental import pallas as pl
from jax.experimental.pallas import tpu as pltpu
from jax.sharding import PartitionSpec as P

D = 4096
CAP = 2


ridge_term = 0.001
feedback = 0.1
epsilon = 1e-06


def orthonormal(panel, gram_total):
    eye_matrix = jnp.eye(gram_total.shape[-1], dtype=jnp.float32)
    lower_factor = jnp.linalg.cholesky(gram_total + ridge_term * eye_matrix)
    solved = jax.scipy.linalg.solve_triangular(
        lower_factor, jnp.swapaxes(panel, -1, -2), lower=True
    )
    return jnp.swapaxes(solved, -1, -2)


def slot_table(owners, groups, capacity):
    count = owners.shape[0]
    index_line = jnp.arange(count, dtype=jnp.int32)
    same_owner = owners[:, None] == owners[None, :]
    earlier = index_line[None, :] < index_line[:, None]
    position = jnp.sum((same_owner & earlier).astype(jnp.int32), axis=1)
    owner_hit = owners[:, None, None] == jnp.arange(groups, dtype=jnp.int32)[None, :, None]
    slot_hit = position[:, None, None] == jnp.arange(capacity, dtype=jnp.int32)[None, None, :]
    return (owner_hit & slot_hit).astype(jnp.float32)


def general_shards(momentum, gradient, right_in, owners):
    highest = lax.Precision.HIGHEST
    groups = lax.axis_size("tensor")
    rows = momentum.shape[2]
    columns = momentum.shape[3]
    owner_table = slot_table(owners, groups, CAP)
    table_low = owner_table.astype(jnp.bfloat16)
    summed = (momentum.astype(jnp.float32) + gradient.astype(jnp.float32)).astype(jnp.bfloat16)
    scale = math.sqrt(D)
    send_state = jnp.einsum(
        "edc,emrk->cmrdk", table_low, summed, preferred_element_type=jnp.float32
    ).astype(jnp.bfloat16)
    send_right = jnp.einsum(
        "edc,emkq->cmkdq", table_low, right_in, preferred_element_type=jnp.float32
    ).astype(jnp.bfloat16)
    got_state, got_right = (
        lax.all_to_all(send_state, "tensor", split_axis=3, concat_axis=3, tiled=True),
        lax.all_to_all(send_right, "tensor", split_axis=3, concat_axis=3, tiled=True),
    )
    panel = jnp.einsum(
        "cmrtk,cmktq->cmrq", got_state, got_right, preferred_element_type=jnp.float32
    )
    gram_part = jnp.einsum("cmrq,cmrs->cmqs", panel, panel, precision=highest)
    gram_total = lax.psum(gram_part, "fsdp")
    ortho = orthonormal(panel, gram_total)
    ortho_low = ortho.astype(jnp.bfloat16)
    factor_part = jnp.einsum(
        "cmrtk,cmrq->cmktq", got_state, ortho_low, preferred_element_type=jnp.float32
    )
    factor = lax.psum(factor_part, "fsdp")
    mean_square = jnp.mean(factor * factor, axis=(2, 3))
    right_new = factor * lax.rsqrt(mean_square + epsilon)[:, :, None, None, :]
    update = jnp.einsum("cmrq,cmktq->cmrtk", ortho, factor, precision=highest)
    fresh = (got_state.astype(jnp.float32) - feedback * update).astype(jnp.bfloat16)
    state_out = fresh.reshape(CAP, fresh.shape[1], rows, groups * columns)
    left_out = ortho * scale
    returned = lax.all_to_all(right_new, "tensor", split_axis=3, concat_axis=3, tiled=True)
    right_out = jnp.einsum("edc,cmkdq->emkq", owner_table, returned, precision=highest)
    return (state_out, left_out, right_out)


MESH = pl.DeviceIdType.MESH
HIGHEST = lax.Precision.HIGHEST
VMEM_BYTES = 56 * 1024 * 1024


def greet(shards_f, groups):
    f = lax.axis_index("fsdp")
    z = lax.axis_index("tensor")
    barrier = pltpu.get_barrier_semaphore()
    for j in range(1, shards_f):
        pl.semaphore_signal(
            barrier, inc=1, device_id={"fsdp": lax.rem(f + j, shards_f), "tensor": z}, device_id_type=MESH
        )
    for j in range(1, groups):
        pl.semaphore_signal(
            barrier, inc=1, device_id={"fsdp": f, "tensor": lax.rem(z + j, groups)}, device_id_type=MESH
        )
    pl.semaphore_wait(barrier, shards_f - 1 + groups - 1)
    return f, z


def remote(src, dst, send_sem, recv_sem, f, z):
    return pltpu.make_async_remote_copy(
        src_ref=src,
        dst_ref=dst,
        send_sem=send_sem,
        recv_sem=recv_sem,
        device_id={"fsdp": f, "tensor": z},
        device_id_type=MESH,
    )


def exchange_kernel(
    shards_f, groups, kinds,
    sel_ref, m_ref, g_ref, r_ref,
    got_out, panel_ref, gram_ref,
    sendbuf, got, rfull, gpart, gpair, ghalf, gfour, gfin,
    s_send, s_recv, rz_send, rz_recv, rf_send, rf_recv, g_send, g_recv, out_sem,
):
    rows, columns = m_ref.shape[2], m_ref.shape[3]
    piece = columns // shards_f
    f, z = greet(shards_f, groups)
    mine = pl.ds(pl.multiple_of(f * piece, piece), piece)

    rfull[z, :, mine, :] = r_ref[:, mine, :]
    right_z = []
    for j in range(1, groups):
        part = rfull.at[z, :, mine, :]
        copy = remote(part, part, rz_send.at[j - 1], rz_recv.at[j - 1], f, lax.rem(z + j, groups))
        copy.start()
        right_z.append(copy)

    step = 128
    here = pl.ds(pl.multiple_of(z * columns, columns), columns)
    sends = []
    for j in (2, 3, 1):
        d = lax.rem(z + j, groups)
        for c in range(CAP):
            expert = sel_ref[d * CAP + c]
            slot = (j - 1) * CAP + c
            for k in range(kinds):
                @pl.loop(0, rows // step)
                def _(i):
                    at = pl.ds(pl.multiple_of(i * step, step), step)
                    total = m_ref[expert, k, at, :].astype(jnp.float32) + g_ref[expert, k, at, :].astype(jnp.float32)
                    sendbuf[slot, k, at, :] = total.astype(jnp.bfloat16)
            copy = remote(
                sendbuf.at[slot],
                got.at[pl.ds(c * kinds, kinds), :, here],
                s_send.at[slot],
                s_recv.at[slot],
                f,
                d,
            )
            copy.start()
            sends.append(copy)
    for c in range(CAP):
        expert = sel_ref[z * CAP + c]
        for k in range(kinds):
            @pl.loop(0, rows // step)
            def _(i):
                at = pl.ds(pl.multiple_of(i * step, step), step)
                total = m_ref[expert, k, at, :].astype(jnp.float32) + g_ref[expert, k, at, :].astype(jnp.float32)
                got[c * kinds + k, at, here] = total.astype(jnp.bfloat16)

    for j in range(1, groups):
        part = rfull.at[lax.rem(z + groups - j, groups), :, mine, :]
        remote(part, part, rz_send.at[j - 1], rz_recv.at[j - 1], f, z).wait_recv()
    right_f = []
    for j in range(1, shards_f):
        part = rfull.at[:, :, mine, :]
        copy = remote(part, part, rf_send.at[j - 1], rf_recv.at[j - 1], lax.rem(f + j, shards_f), z)
        copy.start()
        right_f.append(copy)
    for j in range(1, shards_f):
        theirs = pl.ds(pl.multiple_of(lax.rem(f + shards_f - j, shards_f) * piece, piece), piece)
        part = rfull.at[:, :, theirs, :]
        remote(part, part, rf_send.at[j - 1], rf_recv.at[j - 1], f, z).wait_recv()

    outs = []
    order = (0, 1, 2, 3)
    for j in order:
        source = lax.rem(z + groups - j, groups)
        there = pl.ds(pl.multiple_of(source * columns, columns), columns)
        for c in range(CAP):
            slot = (j - 1) * CAP + c
            block = got.at[pl.ds(c * kinds, kinds), :, there]
            if j:
                remote(sendbuf.at[slot], block, s_send.at[slot], s_recv.at[slot], f, z).wait_recv()
            copy = pltpu.make_async_copy(
                block, got_out.at[pl.ds(c * kinds, kinds), :, there], out_sem.at[j * CAP + c]
            )
            copy.start()
            outs.append(copy)
            expert = sel_ref[z * CAP + c]
            for k in range(kinds):
                term = jnp.dot(
                    got[c * kinds + k, :, there],
                    rfull[source, expert * kinds + k],
                    preferred_element_type=jnp.float32,
                )
                if j:
                    panel_ref[c * kinds + k] += term
                else:
                    panel_ref[c * kinds + k] = term

    mats = CAP * kinds
    half = mats // 2
    core = lax.rem(f, 2)
    chip = f // 2
    chips = shards_f // 2
    pair = chip * 2 + 1 - core
    for m in range(mats):
        panel = panel_ref[m]
        gpart[m] = jnp.dot(panel.T, panel, precision=HIGHEST, preferred_element_type=jnp.float32)
    first = remote(gpart.at[pl.ds((1 - core) * half, half)], gpair, g_send.at[0], g_recv.at[0], pair, z)
    first.start()
    first.wait_recv()
    ghalf[...] = gpart[pl.ds(core * half, half)] + gpair[...]
    second = []
    for j in range(1, chips):
        copy = remote(
            ghalf, gfour.at[j - 1], g_send.at[j], g_recv.at[j], lax.rem(chip + j, chips) * 2 + core, z
        )
        copy.start()
        second.append(copy)
    for copy in second:
        copy.wait_recv()
    total = ghalf[...]
    for j in range(1, chips):
        total = total + gfour[j - 1]
    gfin[pl.ds(core * half, half)] = total
    part = gfin.at[pl.ds(core * half, half)]
    third = remote(part, part, g_send.at[chips], g_recv.at[chips], pair, z)
    third.start()
    part = gfin.at[pl.ds((1 - core) * half, half)]
    remote(part, part, g_send.at[chips], g_recv.at[chips], pair, z).wait_recv()
    gram_ref[...] = gfin[...]

    for copy in right_z + sends + right_f + [first] + second + [third]:
        copy.wait_send()
    for copy in outs:
        copy.wait()


def factor_kernel(used_ref, gram_ref, panel_ref, got_ref, left_ref, low_ref, fact_ref, aug):
    mats, rank = gram_ref.shape[0], gram_ref.shape[1]
    block = 32
    row_at = lax.broadcasted_iota(jnp.int32, (rank, rank), 0)
    col_at = lax.broadcasted_iota(jnp.int32, (rank, rank), 1)
    eye = (row_at == col_at).astype(jnp.float32)
    for m in range(mats):
        aug[m, :, :rank] = gram_ref[m] + ridge_term * eye
        aug[m, :, rank:] = eye
    small_row = lax.broadcasted_iota(jnp.int32, (mats, block, block), 1)
    small_col = lax.broadcasted_iota(jnp.int32, (mats, block, block), 2)
    small_eye = (small_row == small_col).astype(jnp.float32)
    for start in range(0, rank, block):
        stop = start + block

        def eliminate(k, carry):
            left, right = carry
            on_row = small_row == k
            left_row = jnp.sum(jnp.where(on_row, left, 0.0), axis=1, keepdims=True)
            right_row = jnp.sum(jnp.where(on_row, right, 0.0), axis=1, keepdims=True)
            column = jnp.sum(jnp.where(small_col == k, left, 0.0), axis=2, keepdims=True)
            pivot = jnp.sum(jnp.where(small_col[:, :1] == k, left_row, 0.0), axis=2, keepdims=True)
            ratio = jnp.where(small_row > k, column / pivot, 0.0)
            return left - ratio * left_row, right - ratio * right_row

        left, right = lax.fori_loop(
            0, block, eliminate, (aug[:, start:stop, start:stop], small_eye)
        )
        diagonal = jnp.sum(left * small_eye, axis=2, keepdims=True)
        inverse = right * lax.rsqrt(diagonal)
        for m in range(mats):
            top = jnp.dot(inverse[m], aug[m, start:stop, :], precision=HIGHEST, preferred_element_type=jnp.float32)
            aug[m, start:stop, :] = top
            if stop < rank:
                below = top[:, :rank].T[stop:]
                aug[m, stop:, :] -= jnp.dot(below, top, precision=HIGHEST, preferred_element_type=jnp.float32)
    scale = math.sqrt(D)
    for m in range(mats):
        ortho = jnp.dot(
            panel_ref[m], aug[m, :, rank:].T, precision=HIGHEST, preferred_element_type=jnp.float32
        )
        left_ref[m] = jnp.where(used_ref[m] > 0, ortho * scale, 0.0)
        low = ortho.astype(jnp.bfloat16)
        low_ref[m] = low
        fact_ref[m] = jnp.dot(low.T, got_ref[m], preferred_element_type=jnp.float32)


def reduce_kernel(
    shards_f, groups, kinds, experts,
    slot_ref, part_ref,
    fact_out, right_out,
    pairbuf, halfbuf, chipbuf, lowbuf, newbuf, retbuf, pickbuf, rightbuf,
    a_send, a_recv, b_send, b_recv, c_send, c_recv, d_send, d_recv, e_send, e_recv,
):
    mats, rank, hidden = part_ref.shape
    f, z = greet(shards_f, groups)
    core = lax.rem(f, 2)
    chip = f // 2
    chips = shards_f // 2
    pair = chip * 2 + 1 - core
    half = rank // 2
    piece = rank // shards_f
    columns = hidden // groups

    first = []
    for m in range(mats):
        src = part_ref.at[m, pl.ds(pl.multiple_of((1 - core) * half, half), half), :]
        copy = remote(src, pairbuf.at[m], a_send.at[m], a_recv.at[m], pair, z)
        copy.start()
        first.append(copy)
    second = []
    own = pl.ds(pl.multiple_of(core * half, half), half)
    for m in range(mats):
        first[m].wait_recv()
        halfbuf[m] = part_ref[m, own, :] + pairbuf[m]
        for j in (2, 1, 3):
            other = lax.rem(chip + j, chips)
            copy = remote(
                halfbuf.at[m, pl.ds(pl.multiple_of(other * piece, piece), piece), :],
                chipbuf.at[j - 1, m],
                b_send.at[j - 1, m],
                b_recv.at[j - 1, m],
                other * 2 + core,
                z,
            )
            copy.start()
            second.append(copy)
    chunk = core * half + chip * piece
    at = pl.ds(pl.multiple_of(chunk, piece), piece)
    mine = pl.ds(pl.multiple_of(chip * piece, piece), piece)
    third = []
    for copy in second:
        copy.wait_recv()
    for m in range(mats):
        total = halfbuf[m, mine, :]
        for j in range(1, chips):
            total = total + chipbuf[j - 1, m]
        lowbuf[m, at, :] = total.astype(jnp.bfloat16)
        mean_square = jnp.mean(total * total, axis=1, keepdims=True)
        fresh = total * lax.rsqrt(mean_square + epsilon)
        for t in range(groups):
            newbuf[t, m] = fresh[:, t * columns : (t + 1) * columns]
    fourth = []
    for j in range(1, groups):
        d = lax.rem(z + j, groups)
        copy = remote(newbuf.at[d], retbuf.at[z], d_send.at[j - 1], d_recv.at[j - 1], f, d)
        copy.start()
        fourth.append(copy)
    for j in range(1, shards_f):
        part = lowbuf.at[:, at, :]
        copy = remote(part, part, c_send.at[j - 1], c_recv.at[j - 1], lax.rem(f + j, shards_f), z)
        copy.start()
        third.append(copy)
    retbuf[z] = newbuf[z]
    for j in range(1, groups):
        source = lax.rem(z + groups - j, groups)
        remote(newbuf.at[source], retbuf.at[source], d_send.at[j - 1], d_recv.at[j - 1], f, z).wait_recv()
    for e in range(experts):
        slot = slot_ref[e]
        owner = slot // CAP
        position = lax.rem(slot, CAP)
        for k in range(kinds):
            rightbuf[e * kinds + k, at, :] = retbuf[owner, position * kinds + k]
    fifth = []
    for j in range(1, shards_f):
        part = rightbuf.at[:, at, :]
        copy = remote(part, part, e_send.at[j - 1], e_recv.at[j - 1], lax.rem(f + j, shards_f), z)
        copy.start()
        fifth.append(copy)
    for buffer, send, recv in ((lowbuf, c_send, c_recv), (rightbuf, e_send, e_recv)):
        for j in range(1, shards_f):
            source = lax.rem(f + shards_f - j, shards_f)
            place = lax.rem(source, 2) * half + (source // 2) * piece
            part = buffer.at[:, pl.ds(pl.multiple_of(place, piece), piece), :]
            remote(part, part, send.at[j - 1], recv.at[j - 1], f, z).wait_recv()
    fact_out[...] = lowbuf[...]
    right_out[...] = rightbuf[...]
    for copy in first + second + third + fourth + fifth:
        copy.wait_send()


def fresh_kernel(used_ref, got_ref, low_ref, fact_ref, state_ref):
    m = pl.program_id(0)
    update = jnp.dot(low_ref[0], fact_ref[0], preferred_element_type=jnp.float32)
    fresh = got_ref[0].astype(jnp.float32) - feedback * update
    state_ref[0] = jnp.where(used_ref[m] > 0, fresh, 0.0).astype(jnp.bfloat16)


def shards(momentum, gradient, right_in, owners):
    groups = lax.axis_size("tensor")
    shards_f = lax.axis_size("fsdp")
    experts, kinds, rows, columns = momentum.shape
    rank = right_in.shape[-1]
    hidden = groups * columns
    mats = CAP * kinds
    z = lax.axis_index("tensor")
    index_line = jnp.arange(experts, dtype=jnp.int32)
    same_owner = owners[:, None] == owners[None, :]
    earlier = index_line[None, :] < index_line[:, None]
    position = jnp.sum((same_owner & earlier).astype(jnp.int32), axis=1)
    slot = owners * CAP + position
    hit = slot[:, None] == jnp.arange(groups * CAP, dtype=jnp.int32)[None, :]
    sel = jnp.sum(jnp.where(hit, index_line[:, None], 0), axis=0).astype(jnp.int32)
    here = slot[:, None] == (z * CAP + jnp.arange(mats, dtype=jnp.int32) // kinds)[None, :]
    used = jnp.sum(here.astype(jnp.int32), axis=0)

    smem = pl.BlockSpec(memory_space=pltpu.SMEM)
    vmem = pl.BlockSpec(memory_space=pltpu.VMEM)
    hbm = pl.BlockSpec(memory_space=pl.ANY)
    f32, bf16 = jnp.float32, jnp.bfloat16
    shape = jax.ShapeDtypeStruct
    dma = pltpu.SemaphoreType.DMA
    remote_slots = (groups - 1) * CAP
    chips = shards_f // 2

    got, panel, gram = pl.pallas_call(
        functools.partial(exchange_kernel, shards_f, groups, kinds),
        out_shape=(shape((mats, rows, hidden), bf16), shape((mats, rows, rank), f32), shape((mats, rank, rank), f32)),
        in_specs=[smem, vmem, vmem, vmem],
        out_specs=(hbm, vmem, vmem),
        scratch_shapes=[
            pltpu.VMEM((remote_slots, kinds, rows, columns), bf16),
            pltpu.VMEM((mats, rows, hidden), bf16),
            pltpu.VMEM((groups, experts * kinds, columns, rank), bf16),
            pltpu.VMEM((mats, rank, rank), f32),
            pltpu.VMEM((mats // 2, rank, rank), f32),
            pltpu.VMEM((mats // 2, rank, rank), f32),
            pltpu.VMEM((chips - 1, mats // 2, rank, rank), f32),
            pltpu.VMEM((mats, rank, rank), f32),
            dma((remote_slots,)), dma((remote_slots,)),
            dma((groups - 1,)), dma((groups - 1,)),
            dma((shards_f - 1,)), dma((shards_f - 1,)),
            dma((chips + 1,)), dma((chips + 1,)),
            dma((groups * CAP,)),
        ],
        compiler_params=pltpu.CompilerParams(
            collective_id=0, has_side_effects=True, vmem_limit_bytes=VMEM_BYTES
        ),
        name="exchange",
    )(sel, momentum, gradient, right_in.reshape(experts * kinds, columns, rank))

    left, low, part = pl.pallas_call(
        factor_kernel,
        out_shape=(shape((mats, rows, rank), f32), shape((mats, rows, rank), bf16), shape((mats, rank, hidden), f32)),
        in_specs=[smem, vmem, vmem, vmem],
        out_specs=(vmem, vmem, vmem),
        scratch_shapes=[pltpu.VMEM((mats, rank, 2 * rank), f32)],
        compiler_params=pltpu.CompilerParams(vmem_limit_bytes=VMEM_BYTES),
        name="factors",
    )(used, gram, panel, got)

    piece = rank // shards_f
    fact, right = pl.pallas_call(
        functools.partial(reduce_kernel, shards_f, groups, kinds, experts),
        out_shape=(shape((mats, rank, hidden), bf16), shape((experts * kinds, rank, columns), f32)),
        in_specs=[smem, vmem],
        out_specs=(vmem, vmem),
        scratch_shapes=[
            pltpu.VMEM((mats, rank // 2, hidden), f32),
            pltpu.VMEM((mats, rank // 2, hidden), f32),
            pltpu.VMEM((chips - 1, mats, piece, hidden), f32),
            pltpu.VMEM((mats, rank, hidden), bf16),
            pltpu.VMEM((groups, mats, piece, columns), f32),
            pltpu.VMEM((groups, mats, piece, columns), f32),
            pltpu.VMEM((8, 128), f32),
            pltpu.VMEM((experts * kinds, rank, columns), f32),
            dma((mats,)), dma((mats,)),
            dma((chips - 1, mats)), dma((chips - 1, mats)),
            dma((shards_f - 1,)), dma((shards_f - 1,)),
            dma((groups - 1,)), dma((groups - 1,)),
            dma((shards_f - 1,)), dma((shards_f - 1,)),
        ],
        compiler_params=pltpu.CompilerParams(
            collective_id=1, has_side_effects=True, vmem_limit_bytes=VMEM_BYTES
        ),
        name="reduce",
    )(slot, part)

    band = min(rows, 256)
    state = pl.pallas_call(
        fresh_kernel,
        grid=(mats, rows // band),
        out_shape=shape((mats, rows, hidden), bf16),
        in_specs=[
            smem,
            pl.BlockSpec((1, band, hidden), lambda m, i: (m, i, 0)),
            pl.BlockSpec((1, band, rank), lambda m, i: (m, i, 0)),
            pl.BlockSpec((1, rank, hidden), lambda m, i: (m, 0, 0)),
        ],
        out_specs=pl.BlockSpec((1, band, hidden), lambda m, i: (m, i, 0)),
        name="fresh",
    )(used, got, low, fact)
    right_new = jnp.swapaxes(right, 1, 2).reshape(experts, kinds, columns, rank)
    return (
        state.reshape(CAP, kinds, rows, hidden),
        left.reshape(CAP, kinds, rows, rank),
        right_new,
    )


def solution(mesh):
    fits = mesh.shape["fsdp"] == 8 and mesh.shape["tensor"] == 4
    return jax.shard_map(
        shards if fits else general_shards,
        mesh=mesh,
        in_specs=(
            P(None, None, "fsdp", "tensor"),
            P(None, None, "fsdp", "tensor"),
            P(None, None, "tensor", None),
            P(),
        ),
        out_specs=(
            P("tensor", None, "fsdp", None),
            P("tensor", None, "fsdp", None),
            P(None, None, "tensor", None),
        ),
        check_vma=False,
    )
```

```python
import functools
import math

import jax
import jax.numpy as jnp
from jax import lax
from jax.experimental import pallas as pl
from jax.experimental.pallas import tpu as pltpu
from jax.sharding import PartitionSpec as P

D = 4096
CAP = 2


ridge_term = 0.001
feedback = 0.1
epsilon = 1e-06


def orthonormal(panel, gram_total):
    eye_matrix = jnp.eye(gram_total.shape[-1], dtype=jnp.float32)
    lower_factor = jnp.linalg.cholesky(gram_total + ridge_term * eye_matrix)
    solved = jax.scipy.linalg.solve_triangular(
        lower_factor, jnp.swapaxes(panel, -1, -2), lower=True
    )
    return jnp.swapaxes(solved, -1, -2)


def slot_table(owners, groups, capacity):
    count = owners.shape[0]
    index_line = jnp.arange(count, dtype=jnp.int32)
    same_owner = owners[:, None] == owners[None, :]
    earlier = index_line[None, :] < index_line[:, None]
    position = jnp.sum((same_owner & earlier).astype(jnp.int32), axis=1)
    owner_hit = owners[:, None, None] == jnp.arange(groups, dtype=jnp.int32)[None, :, None]
    slot_hit = position[:, None, None] == jnp.arange(capacity, dtype=jnp.int32)[None, None, :]
    return (owner_hit & slot_hit).astype(jnp.float32)


def general_shards(momentum, gradient, right_in, owners):
    highest = lax.Precision.HIGHEST
    groups = lax.axis_size("tensor")
    rows = momentum.shape[2]
    columns = momentum.shape[3]
    owner_table = slot_table(owners, groups, CAP)
    table_low = owner_table.astype(jnp.bfloat16)
    summed = (momentum.astype(jnp.float32) + gradient.astype(jnp.float32)).astype(jnp.bfloat16)
    scale = math.sqrt(D)
    send_state = jnp.einsum(
        "edc,emrk->cmrdk", table_low, summed, preferred_element_type=jnp.float32
    ).astype(jnp.bfloat16)
    send_right = jnp.einsum(
        "edc,emkq->cmkdq", table_low, right_in, preferred_element_type=jnp.float32
    ).astype(jnp.bfloat16)
    got_state, got_right = (
        lax.all_to_all(send_state, "tensor", split_axis=3, concat_axis=3, tiled=True),
        lax.all_to_all(send_right, "tensor", split_axis=3, concat_axis=3, tiled=True),
    )
    panel = jnp.einsum(
        "cmrtk,cmktq->cmrq", got_state, got_right, preferred_element_type=jnp.float32
    )
    gram_part = jnp.einsum("cmrq,cmrs->cmqs", panel, panel, precision=highest)
    gram_total = lax.psum(gram_part, "fsdp")
    ortho = orthonormal(panel, gram_total)
    ortho_low = ortho.astype(jnp.bfloat16)
    factor_part = jnp.einsum(
        "cmrtk,cmrq->cmktq", got_state, ortho_low, preferred_element_type=jnp.float32
    )
    factor = lax.psum(factor_part, "fsdp")
    mean_square = jnp.mean(factor * factor, axis=(2, 3))
    right_new = factor * lax.rsqrt(mean_square + epsilon)[:, :, None, None, :]
    update = jnp.einsum("cmrq,cmktq->cmrtk", ortho, factor, precision=highest)
    fresh = (got_state.astype(jnp.float32) - feedback * update).astype(jnp.bfloat16)
    state_out = fresh.reshape(CAP, fresh.shape[1], rows, groups * columns)
    left_out = ortho * scale
    returned = lax.all_to_all(right_new, "tensor", split_axis=3, concat_axis=3, tiled=True)
    right_out = jnp.einsum("edc,cmkdq->emkq", owner_table, returned, precision=highest)
    return (state_out, left_out, right_out)


MESH = pl.DeviceIdType.MESH
HIGHEST = lax.Precision.HIGHEST
VMEM_BYTES = 56 * 1024 * 1024


def greet(shards_f, groups):
    f = lax.axis_index("fsdp")
    z = lax.axis_index("tensor")
    barrier = pltpu.get_barrier_semaphore()
    for j in range(1, shards_f):
        pl.semaphore_signal(
            barrier, inc=1, device_id={"fsdp": lax.rem(f + j, shards_f), "tensor": z}, device_id_type=MESH
        )
    for j in range(1, groups):
        pl.semaphore_signal(
            barrier, inc=1, device_id={"fsdp": f, "tensor": lax.rem(z + j, groups)}, device_id_type=MESH
        )
    pl.semaphore_wait(barrier, shards_f - 1 + groups - 1)
    return f, z


def remote(src, dst, send_sem, recv_sem, f, z):
    return pltpu.make_async_remote_copy(
        src_ref=src,
        dst_ref=dst,
        send_sem=send_sem,
        recv_sem=recv_sem,
        device_id={"fsdp": f, "tensor": z},
        device_id_type=MESH,
    )


def inverse_factor(aug, mats, rank):
    block = 32
    small_row = lax.broadcasted_iota(jnp.int32, (mats, block, block), 1)
    small_col = lax.broadcasted_iota(jnp.int32, (mats, block, block), 2)
    small_eye = (small_row == small_col).astype(jnp.float32)
    for start in range(0, rank, block):
        stop = start + block

        def eliminate(k, carry):
            left, right = carry
            on_row = small_row == k
            left_row = jnp.sum(jnp.where(on_row, left, 0.0), axis=1, keepdims=True)
            right_row = jnp.sum(jnp.where(on_row, right, 0.0), axis=1, keepdims=True)
            column = jnp.sum(jnp.where(small_col == k, left, 0.0), axis=2, keepdims=True)
            pivot = jnp.sum(jnp.where(small_col[:, :1] == k, left_row, 0.0), axis=2, keepdims=True)
            ratio = jnp.where(small_row > k, column / pivot, 0.0)
            return left - ratio * left_row, right - ratio * right_row

        left, right = lax.fori_loop(
            0, block, eliminate, (aug[:, start:stop, start:stop], small_eye)
        )
        diagonal = jnp.sum(left * small_eye, axis=2, keepdims=True)
        inverse = right * lax.rsqrt(diagonal)
        for m in range(mats):
            top = jnp.dot(inverse[m], aug[m, start:stop, :], precision=HIGHEST, preferred_element_type=jnp.float32)
            aug[m, start:stop, :] = top
            if stop < rank:
                below = top[:, :rank].T[stop:]
                aug[m, stop:, :] -= jnp.dot(below, top, precision=HIGHEST, preferred_element_type=jnp.float32)


def step_kernel(
    shards_f, groups,
    sel_ref, m_ref, g_ref, r_ref,
    got_out, low_out, fact_out, right_out,
    summed, sendbuf, got, pbuf, precv, pchunk,
    gram, gpair, ghalf, gchip, gpiece, gdepth, gfull, aug, wfull,
    obuf, fpart, fpair, fhalf, fchip, fchunk, fsend, lowbuf, sqbuf, sqrecv, rightbuf,
    p_send, p_recv, ga_send, ga_recv, gb_send, gb_recv, gc_send, gc_recv, gd_send, gd_recv,
    w_send, w_recv, o_send, o_recv, fa_send, fa_recv, fb_send, fb_recv, fz_send, fz_recv,
    sq_send, sq_recv, low_send, low_recv, right_send, right_recv,
    s_send, first_recv, near_recv, second_recv, pass_send, pass_recv, out_sem,
):
    experts, kinds, rows, columns = m_ref.shape
    mats = experts * kinds
    slots = CAP * kinds
    rank = r_ref.shape[-1]
    half_m = mats // 2
    f, z = greet(shards_f, groups)
    core = lax.rem(f, 2)
    chip = f // 2
    chips = shards_f // 2
    pair = chip * 2 + 1 - core
    zrows = rows // groups
    started = []

    def go(src, dst, send_sem, recv_sem, to_f, to_z):
        copy = remote(src, dst, send_sem, recv_sem, to_f, to_z)
        copy.start()
        started.append(copy)
        return copy

    def landed(dst, recv_sem):
        remote(dst, dst, recv_sem, recv_sem, f, z).wait_recv()

    step = 128
    zmine = pl.ds(pl.multiple_of(z * zrows, zrows), zrows)
    for e in range(experts):
        for k in range(kinds):
            @pl.loop(0, rows // step)
            def _(i):
                at = pl.ds(pl.multiple_of(i * step, step), step)
                total = m_ref[e, k, at, :].astype(jnp.float32) + g_ref[e, k, at, :].astype(jnp.float32)
                low = total.astype(jnp.bfloat16)
                summed[e, k, at, :] = low
                pbuf[e * kinds + k, at, :] = jnp.dot(low, r_ref[e * kinds + k], preferred_element_type=jnp.float32)
        for j in (2, 3, 1):
            d = lax.rem(z + j, groups)
            go(
                pbuf.at[pl.ds(e * kinds, kinds), pl.ds(pl.multiple_of(d * zrows, zrows), zrows), :],
                precv.at[j - 1, pl.ds(e * kinds, kinds)],
                p_send.at[j - 1, e],
                p_recv.at[j - 1, e],
                f,
                d,
            )

    near = z + 1 - 2 * lax.rem(z, 2)
    upper = z // 2
    inner = 2 - upper
    outer = 3 - 3 * upper
    picks = (
        sel_ref[groups * CAP + 1 - upper],
        sel_ref[outer * CAP],
        sel_ref[inner * CAP],
        sel_ref[near * CAP],
        sel_ref[near * CAP + 1],
    )
    for unit, expert in enumerate(picks):
        for k in range(kinds):
            @pl.loop(0, rows // step)
            def _(i):
                at = pl.ds(pl.multiple_of(i * step, step), step)
                sendbuf[unit, k, at, :] = summed[expert, k, at, :]
    here = pl.ds(pl.multiple_of(z * columns, columns), columns)
    for c in range(CAP):
        expert = sel_ref[z * CAP + c]
        for k in range(kinds):
            @pl.loop(0, rows // step)
            def _(i):
                at = pl.ds(pl.multiple_of(i * step, step), step)
                got[c * kinds + k, at, here] = summed[expert, k, at, :]

    def place(c, source):
        return got.at[pl.ds(c * kinds, kinds), :, pl.ds(pl.multiple_of(source * columns, columns), columns)]

    for j in range(1, groups):
        for e in range(experts):
            landed(precv.at[j - 1, pl.ds(e * kinds, kinds)], p_recv.at[j - 1, e])
    go(sendbuf.at[0], place(1, z), s_send.at[0], second_recv.at[lax.rem(z, 2)], f, inner)
    go(sendbuf.at[4], place(1, z), s_send.at[4], near_recv, f, near)

    for m in range(mats):
        total = pbuf[m, zmine, :]
        for j in range(1, groups):
            total = total + precv[j - 1, m]
        pchunk[m] = total
        gram[m] = jnp.dot(total.T, total, precision=HIGHEST, preferred_element_type=jnp.float32)
    go(gram.at[pl.ds((1 - core) * half_m, half_m)], gpair, ga_send, ga_recv, pair, z).wait_recv()
    ghalf[...] = gram[pl.ds(core * half_m, half_m)] + gpair[...]
    prows = rank // chips
    cmine = pl.ds(pl.multiple_of(chip * prows, prows), prows)
    for j in (2, 1, 3):
        other = lax.rem(chip + j, chips)
        go(
            ghalf.at[:, pl.ds(pl.multiple_of(other * prows, prows), prows), :],
            gchip.at[j - 1], gb_send.at[j - 1], gb_recv.at[j - 1], other * 2 + core, z,
        )
    total = ghalf[:, cmine, :]
    for j in range(1, chips):
        landed(gchip.at[j - 1], gb_recv.at[j - 1])
        total = total + gchip[j - 1]
    gpiece[...] = total
    for j in (2, 3, 1):
        go(gpiece, gdepth.at[j - 1], gc_send.at[j - 1], gc_recv.at[j - 1], f, lax.rem(z + j, groups))
    for j in range(1, groups):
        landed(gdepth.at[j - 1], gc_recv.at[j - 1])
        total = total + gdepth[j - 1]
    gfull[:, cmine, :] = total
    for j in (2, 1, 3):
        part = gfull.at[:, cmine, :]
        go(part, part, gd_send.at[j - 1], gd_recv.at[j - 1], lax.rem(chip + j, chips) * 2 + core, z)
    go(sendbuf.at[1], place(0, z), s_send.at[1], first_recv.at[z], f, outer)
    go(sendbuf.at[3], place(0, z), s_send.at[3], first_recv.at[z], f, near)
    for j in range(1, chips):
        other = lax.rem(chip + chips - j, chips)
        landed(gfull.at[:, pl.ds(pl.multiple_of(other * prows, prows), prows), :], gd_recv.at[j - 1])

    row_at = lax.broadcasted_iota(jnp.int32, (rank, rank), 0)
    col_at = lax.broadcasted_iota(jnp.int32, (rank, rank), 1)
    eye = (row_at == col_at).astype(jnp.float32)
    for m in range(half_m):
        aug[m, :, :rank] = gfull[m] + ridge_term * eye
        aug[m, :, rank:] = eye
    inverse_factor(aug, half_m, rank)
    wmine = pl.ds(core * half_m, half_m)
    wfull[wmine] = aug[:, :, rank:]
    go(wfull.at[wmine], wfull.at[wmine], w_send, w_recv, pair, z)
    landed(wfull.at[pl.ds((1 - core) * half_m, half_m)], w_recv)

    for m in range(mats):
        ortho = jnp.dot(pchunk[m], wfull[m].T, precision=HIGHEST, preferred_element_type=jnp.float32)
        obuf[m, zmine, :] = ortho.astype(jnp.bfloat16)
    for j in (2, 3, 1):
        part = obuf.at[:, zmine, :]
        go(part, part, o_send.at[j - 1], o_recv.at[j - 1], f, lax.rem(z + j, groups))
    for j in range(1, groups):
        source = lax.rem(z + groups - j, groups)
        landed(obuf.at[:, pl.ds(pl.multiple_of(source * zrows, zrows), zrows), :], o_recv.at[j - 1])

    far = 2 - 2 * upper
    is_inner = (z == 1) | (z == 2)

    @pl.when(is_inner)
    def _():
        for i in range(2):
            block = place(1, far + i)
            landed(block, second_recv.at[i])
            remote(block, block, pass_send.at[i], pass_recv.at[i], f, near).start()

    go(sendbuf.at[2], place(0, z), s_send.at[2], first_recv.at[z], f, inner)

    for m in range(mats):
        fpart[m] = jnp.dot(obuf[m].T, summed[m // kinds, m % kinds], preferred_element_type=jnp.float32)
        low_rows = rank // 2
        go(
            fpart.at[m, pl.ds(pl.multiple_of((1 - core) * low_rows, low_rows), low_rows), :],
            fpair.at[m], fa_send.at[m], fa_recv.at[m], pair, z,
        )
    piece = rank // shards_f
    own = pl.ds(pl.multiple_of(core * low_rows, low_rows), low_rows)
    for m in range(mats):
        landed(fpair.at[m], fa_recv.at[m])
        fhalf[m] = fpart[m, own, :] + fpair[m]
    for j in (2, 1, 3):
        other = lax.rem(chip + j, chips)
        go(
            fhalf.at[:, pl.ds(pl.multiple_of(other * piece, piece), piece), :],
            fchip.at[j - 1], fb_send.at[j - 1], fb_recv.at[j - 1], other * 2 + core, z,
        )
    total = fhalf[:, pl.ds(pl.multiple_of(chip * piece, piece), piece), :]
    for j in range(1, chips):
        landed(fchip.at[j - 1], fb_recv.at[j - 1])
        total = total + fchip[j - 1]
    square = total * total
    part_sum = square[:, :, :128]
    for lane in range(128, columns, 128):
        part_sum = part_sum + square[:, :, lane : lane + 128]
    sqbuf[...] = part_sum
    for j in (2, 3, 1):
        go(sqbuf, sqrecv.at[j - 1], sq_send.at[j - 1], sq_recv.at[j - 1], f, lax.rem(z + j, groups))
    fchunk[...] = total
    chunk = core * low_rows + chip * piece
    at = pl.ds(pl.multiple_of(chunk, piece), piece)
    for j in (2, 3, 1):
        d = lax.rem(z + j, groups)
        for c in range(CAP):
            expert = sel_ref[d * CAP + c]
            for k in range(kinds):
                fsend[j - 1, c * kinds + k] = fchunk[expert * kinds + k].astype(jnp.bfloat16)
        go(fsend.at[j - 1], lowbuf.at[:, at, here], fz_send.at[j - 1], fz_recv.at[j - 1], f, d)
    for c in range(CAP):
        expert = sel_ref[z * CAP + c]
        for k in range(kinds):
            lowbuf[c * kinds + k, at, here] = fchunk[expert * kinds + k].astype(jnp.bfloat16)
    for j in range(1, groups):
        source = lax.rem(z + groups - j, groups)
        there = pl.ds(pl.multiple_of(source * columns, columns), columns)
        landed(lowbuf.at[:, at, there], fz_recv.at[j - 1])
    for j in range(1, shards_f):
        part = lowbuf.at[:, at, :]
        go(part, part, low_send.at[j - 1], low_recv.at[j - 1], lax.rem(f + j, shards_f), z)
    square = sqbuf[...]
    for j in range(1, groups):
        landed(sqrecv.at[j - 1], sq_recv.at[j - 1])
        square = square + sqrecv[j - 1]
    mean_square = jnp.sum(square, axis=2, keepdims=True) / (groups * columns)
    rightbuf[:, at, :] = fchunk[...] * lax.rsqrt(mean_square + epsilon)
    for j in range(1, shards_f):
        part = rightbuf.at[:, at, :]
        go(part, part, right_send.at[j - 1], right_recv.at[j - 1], lax.rem(f + j, shards_f), z)
    for c in range(CAP):
        expert = sel_ref[z * CAP + c]
        for k in range(kinds):
            low_out[c * kinds + k] = obuf[expert * kinds + k]

    def keep(c, source, sem):
        block = place(c, source)
        there = pl.ds(pl.multiple_of(source * columns, columns), columns)
        pltpu.make_async_copy(block, got_out.at[pl.ds(c * kinds, kinds), :, there], out_sem.at[sem]).start()

    keep(0, z, 0)
    keep(1, z, 1)
    landed(place(1, near), near_recv)
    keep(1, near, 2)
    for n, source in enumerate((near, far, far + 1)):
        landed(place(0, source), first_recv.at[source])
        keep(0, source, 3 + n)

    @pl.when(is_inner)
    def _():
        for i in range(2):
            block = place(1, far + i)
            remote(block, block, pass_send.at[i], pass_recv.at[i], f, near).wait_send()

    @pl.when(jnp.logical_not(is_inner))
    def _():
        for i in range(2):
            landed(place(1, far + i), pass_recv.at[i])

    for i in range(2):
        keep(1, far + i, 6 + i)
    for buffer, recv in ((lowbuf, low_recv), (rightbuf, right_recv)):
        for j in range(1, shards_f):
            source = lax.rem(f + shards_f - j, shards_f)
            start = lax.rem(source, 2) * low_rows + (source // 2) * piece
            landed(buffer.at[:, pl.ds(pl.multiple_of(start, piece), piece), :], recv.at[j - 1])
    fact_out[...] = lowbuf[...]
    right_out[...] = rightbuf[...]
    for copy in started:
        copy.wait_send()
    for n, (c, source) in enumerate(
        ((0, z), (1, z), (1, near), (0, near), (0, far), (0, far + 1), (1, far), (1, far + 1))
    ):
        there = pl.ds(pl.multiple_of(source * columns, columns), columns)
        pltpu.make_async_copy(
            place(c, source), got_out.at[pl.ds(c * kinds, kinds), :, there], out_sem.at[n]
        ).wait()


def fresh_kernel(used_ref, got_ref, low_ref, fact_ref, state_ref, left_ref):
    m = pl.program_id(0)
    update = jnp.dot(low_ref[0], fact_ref[0], preferred_element_type=jnp.float32)
    fresh = got_ref[0].astype(jnp.float32) - feedback * update
    state_ref[0] = jnp.where(used_ref[m] > 0, fresh, 0.0).astype(jnp.bfloat16)
    left = low_ref[0].astype(jnp.float32) * math.sqrt(D)
    left_ref[0] = jnp.where(used_ref[m] > 0, left, 0.0)


def shards(momentum, gradient, right_in, owners):
    groups = lax.axis_size("tensor")
    shards_f = lax.axis_size("fsdp")
    experts, kinds, rows, columns = momentum.shape
    rank = right_in.shape[-1]
    hidden = groups * columns
    mats = CAP * kinds
    z = lax.axis_index("tensor")
    index_line = jnp.arange(experts, dtype=jnp.int32)
    same_owner = owners[:, None] == owners[None, :]
    earlier = index_line[None, :] < index_line[:, None]
    position = jnp.sum((same_owner & earlier).astype(jnp.int32), axis=1)
    slot = owners * CAP + position
    hit = slot[:, None] == jnp.arange(groups * CAP, dtype=jnp.int32)[None, :]
    sel = jnp.sum(jnp.where(hit, index_line[:, None], 0), axis=0).astype(jnp.int32)
    second = sel.reshape(groups, CAP)[:, 1] * jnp.sum(hit, axis=0).reshape(groups, CAP)[:, 1]
    sel = jnp.concatenate([sel, second.reshape(2, groups // 2).sum(axis=1).astype(jnp.int32)])
    here = slot[:, None] == (z * CAP + jnp.arange(mats, dtype=jnp.int32) // kinds)[None, :]
    used = jnp.sum(here.astype(jnp.int32), axis=0)

    smem = pl.BlockSpec(memory_space=pltpu.SMEM)
    vmem = pl.BlockSpec(memory_space=pltpu.VMEM)
    hbm = pl.BlockSpec(memory_space=pl.ANY)
    f32, bf16 = jnp.float32, jnp.bfloat16
    shape = jax.ShapeDtypeStruct
    dma = pltpu.SemaphoreType.DMA
    chips = shards_f // 2
    every = experts * kinds
    half_m = every // 2
    zrows = rows // groups
    piece = rank // shards_f
    near_z, near_c, near_f = groups - 1, chips - 1, shards_f - 1
    got, low, fact, right = pl.pallas_call(
        functools.partial(step_kernel, shards_f, groups),
        out_shape=(
            shape((mats, rows, hidden), bf16),
            shape((mats, rows, rank), bf16),
            shape((mats, rank, hidden), bf16),
            shape((every, rank, columns), f32),
        ),
        in_specs=[smem, vmem, vmem, vmem],
        out_specs=(hbm, vmem, vmem, vmem),
        scratch_shapes=[
            pltpu.VMEM((experts, kinds, rows, columns), bf16),
            pltpu.VMEM((5, kinds, rows, columns), bf16),
            pltpu.VMEM((mats, rows, hidden), bf16),
            pltpu.VMEM((every, rows, rank), f32),
            pltpu.VMEM((near_z, every, zrows, rank), f32),
            pltpu.VMEM((every, zrows, rank), f32),
            pltpu.VMEM((every, rank, rank), f32),
            pltpu.VMEM((half_m, rank, rank), f32),
            pltpu.VMEM((half_m, rank, rank), f32),
            pltpu.VMEM((near_c, half_m, rank // chips, rank), f32),
            pltpu.VMEM((half_m, rank // chips, rank), f32),
            pltpu.VMEM((near_z, half_m, rank // chips, rank), f32),
            pltpu.VMEM((half_m, rank, rank), f32),
            pltpu.VMEM((half_m, rank, 2 * rank), f32),
            pltpu.VMEM((every, rank, rank), f32),
            pltpu.VMEM((every, rows, rank), bf16),
            pltpu.VMEM((every, rank, columns), f32),
            pltpu.VMEM((every, rank // 2, columns), f32),
            pltpu.VMEM((every, rank // 2, columns), f32),
            pltpu.VMEM((near_c, every, piece, columns), f32),
            pltpu.VMEM((every, piece, columns), f32),
            pltpu.VMEM((near_z, mats, piece, columns), bf16),
            pltpu.VMEM((mats, rank, hidden), bf16),
            pltpu.VMEM((every, piece, 128), f32),
            pltpu.VMEM((near_z, every, piece, 128), f32),
            pltpu.VMEM((every, rank, columns), f32),
            dma((near_z, experts)), dma((near_z, experts)),
            dma, dma,
            dma((near_c,)), dma((near_c,)),
            dma((near_z,)), dma((near_z,)),
            dma((near_c,)), dma((near_c,)),
            dma, dma,
            dma((near_z,)), dma((near_z,)),
            dma((every,)), dma((every,)),
            dma((near_c,)), dma((near_c,)),
            dma((near_z,)), dma((near_z,)),
            dma((near_z,)), dma((near_z,)),
            dma((near_f,)), dma((near_f,)),
            dma((near_f,)), dma((near_f,)),
            dma((5,)), dma((groups,)), dma, dma((2,)), dma((2,)), dma((2,)), dma((8,)),
        ],
        compiler_params=pltpu.CompilerParams(
            collective_id=0, has_side_effects=True, vmem_limit_bytes=VMEM_BYTES
        ),
        name="step",
    )(sel, momentum, gradient, right_in.reshape(every, columns, rank))

    band = min(rows, 256)
    state, left = pl.pallas_call(
        fresh_kernel,
        grid=(mats, rows // band),
        out_shape=(shape((mats, rows, hidden), bf16), shape((mats, rows, rank), f32)),
        in_specs=[
            smem,
            pl.BlockSpec((1, band, hidden), lambda m, i: (m, i, 0)),
            pl.BlockSpec((1, band, rank), lambda m, i: (m, i, 0)),
            pl.BlockSpec((1, rank, hidden), lambda m, i: (m, 0, 0)),
        ],
        out_specs=(
            pl.BlockSpec((1, band, hidden), lambda m, i: (m, i, 0)),
            pl.BlockSpec((1, band, rank), lambda m, i: (m, i, 0)),
        ),
        name="fresh",
    )(used, got, low, fact)
    right_new = jnp.swapaxes(right, 1, 2).reshape(experts, kinds, columns, rank)
    return (
        state.reshape(CAP, kinds, rows, hidden),
        left.reshape(CAP, kinds, rows, rank),
        right_new,
    )


def solution(mesh):
    fits = mesh.shape["fsdp"] == 8 and mesh.shape["tensor"] == 4
    return jax.shard_map(
        shards if fits else general_shards,
        mesh=mesh,
        in_specs=(
            P(None, None, "fsdp", "tensor"),
            P(None, None, "fsdp", "tensor"),
            P(None, None, "tensor", None),
            P(),
        ),
        out_specs=(
            P("tensor", None, "fsdp", None),
            P("tensor", None, "fsdp", None),
            P(None, None, "tensor", None),
        ),
        check_vma=False,
    )
```

```python
import functools
import math

import jax
import jax.numpy as jnp
from jax import lax
from jax.experimental import pallas as pl
from jax.experimental.pallas import tpu as pltpu
from jax.sharding import PartitionSpec as P

D = 4096
CAP = 2


ridge_term = 0.001
feedback = 0.1
epsilon = 1e-06


def orthonormal(panel, gram_total):
    eye_matrix = jnp.eye(gram_total.shape[-1], dtype=jnp.float32)
    lower_factor = jnp.linalg.cholesky(gram_total + ridge_term * eye_matrix)
    solved = jax.scipy.linalg.solve_triangular(
        lower_factor, jnp.swapaxes(panel, -1, -2), lower=True
    )
    return jnp.swapaxes(solved, -1, -2)


def slot_table(owners, groups, capacity):
    count = owners.shape[0]
    index_line = jnp.arange(count, dtype=jnp.int32)
    same_owner = owners[:, None] == owners[None, :]
    earlier = index_line[None, :] < index_line[:, None]
    position = jnp.sum((same_owner & earlier).astype(jnp.int32), axis=1)
    owner_hit = owners[:, None, None] == jnp.arange(groups, dtype=jnp.int32)[None, :, None]
    slot_hit = position[:, None, None] == jnp.arange(capacity, dtype=jnp.int32)[None, None, :]
    return (owner_hit & slot_hit).astype(jnp.float32)


def general_shards(momentum, gradient, right_in, owners):
    highest = lax.Precision.HIGHEST
    groups = lax.axis_size("tensor")
    rows = momentum.shape[2]
    columns = momentum.shape[3]
    owner_table = slot_table(owners, groups, CAP)
    table_low = owner_table.astype(jnp.bfloat16)
    summed = (momentum.astype(jnp.float32) + gradient.astype(jnp.float32)).astype(jnp.bfloat16)
    scale = math.sqrt(D)
    send_state = jnp.einsum(
        "edc,emrk->cmrdk", table_low, summed, preferred_element_type=jnp.float32
    ).astype(jnp.bfloat16)
    send_right = jnp.einsum(
        "edc,emkq->cmkdq", table_low, right_in, preferred_element_type=jnp.float32
    ).astype(jnp.bfloat16)
    got_state, got_right = (
        lax.all_to_all(send_state, "tensor", split_axis=3, concat_axis=3, tiled=True),
        lax.all_to_all(send_right, "tensor", split_axis=3, concat_axis=3, tiled=True),
    )
    panel = jnp.einsum(
        "cmrtk,cmktq->cmrq", got_state, got_right, preferred_element_type=jnp.float32
    )
    gram_part = jnp.einsum("cmrq,cmrs->cmqs", panel, panel, precision=highest)
    gram_total = lax.psum(gram_part, "fsdp")
    ortho = orthonormal(panel, gram_total)
    ortho_low = ortho.astype(jnp.bfloat16)
    factor_part = jnp.einsum(
        "cmrtk,cmrq->cmktq", got_state, ortho_low, preferred_element_type=jnp.float32
    )
    factor = lax.psum(factor_part, "fsdp")
    mean_square = jnp.mean(factor * factor, axis=(2, 3))
    right_new = factor * lax.rsqrt(mean_square + epsilon)[:, :, None, None, :]
    update = jnp.einsum("cmrq,cmktq->cmrtk", ortho, factor, precision=highest)
    fresh = (got_state.astype(jnp.float32) - feedback * update).astype(jnp.bfloat16)
    state_out = fresh.reshape(CAP, fresh.shape[1], rows, groups * columns)
    left_out = ortho * scale
    returned = lax.all_to_all(right_new, "tensor", split_axis=3, concat_axis=3, tiled=True)
    right_out = jnp.einsum("edc,cmkdq->emkq", owner_table, returned, precision=highest)
    return (state_out, left_out, right_out)


MESH = pl.DeviceIdType.MESH
HIGHEST = lax.Precision.HIGHEST
VMEM_BYTES = 56 * 1024 * 1024


def greet(shards_f, groups):
    f = lax.axis_index("fsdp")
    z = lax.axis_index("tensor")
    barrier = pltpu.get_barrier_semaphore()
    for j in range(1, shards_f):
        pl.semaphore_signal(
            barrier, inc=1, device_id={"fsdp": lax.rem(f + j, shards_f), "tensor": z}, device_id_type=MESH
        )
    for j in range(1, groups):
        pl.semaphore_signal(
            barrier, inc=1, device_id={"fsdp": f, "tensor": lax.rem(z + j, groups)}, device_id_type=MESH
        )
    pl.semaphore_wait(barrier, shards_f - 1 + groups - 1)
    return f, z


def remote(src, dst, send_sem, recv_sem, f, z):
    return pltpu.make_async_remote_copy(
        src_ref=src,
        dst_ref=dst,
        send_sem=send_sem,
        recv_sem=recv_sem,
        device_id={"fsdp": f, "tensor": z},
        device_id_type=MESH,
    )


def inverse_factor(aug, mats, rank):
    block = 32
    wide = (mats, block, 2 * block)
    wide_row = lax.broadcasted_iota(jnp.int32, wide, 1)
    wide_col = lax.broadcasted_iota(jnp.int32, wide, 2)
    on_diagonal = wide_row == wide_col
    small = (mats, block, block)
    small_eye = (lax.broadcasted_iota(jnp.int32, small, 1) == lax.broadcasted_iota(jnp.int32, small, 2)).astype(jnp.float32)
    for start in range(0, rank, block):
        stop = start + block

        def eliminate(k, both):
            row = jnp.sum(jnp.where(wide_row == k, both, 0.0), axis=1, keepdims=True)
            column = jnp.sum(jnp.where(wide_col == k, both, 0.0), axis=2, keepdims=True)
            pivot = jnp.sum(jnp.where(wide_col[:, :1] == k, row, 0.0), axis=2, keepdims=True)
            ratio = jnp.where(wide_row[:, :, :1] > k, column * (1.0 / pivot), 0.0)
            return both - ratio * row

        both = jnp.concatenate([aug[:, start:stop, start:stop], small_eye], axis=2)
        both = lax.fori_loop(0, block, eliminate, both, unroll=4)
        diagonal = jnp.sum(jnp.where(on_diagonal, both, 0.0), axis=2, keepdims=True)
        inverse = both[:, :, block:] * lax.rsqrt(diagonal)
        for m in range(mats):
            top = jnp.dot(inverse[m], aug[m, start:stop, :], precision=HIGHEST, preferred_element_type=jnp.float32)
            aug[m, start:stop, :] = top
            if stop < rank:
                below = top[:, :rank].T[stop:]
                aug[m, stop:, :] -= jnp.dot(below, top, precision=HIGHEST, preferred_element_type=jnp.float32)


def step_kernel(
    shards_f, groups,
    sel_ref, m_ref, g_ref, r_ref,
    got_out, low_out, fact_out, right_out,
    summed, sendbuf, got, pbuf, precv, pchunk,
    gram, gpair, ghalf, gchip, gpiece, gdepth, gfull, aug, wfull,
    obuf, fpart, fpair, fhalf, fchip, fchunk, fsend, lowbuf, sqbuf, sqrecv, rightbuf,
    p_send, p_recv, ga_send, ga_recv, gb_send, gb_recv, gc_send, gc_recv, gd_send, gd_recv,
    w_send, w_recv, o_send, o_recv, fa_send, fa_recv, fb_send, fb_recv, fz_send, fz_recv,
    sq_send, sq_recv, low_send, low_recv, right_send, right_recv,
    s_send, first_recv, near_recv, second_recv, pass_send, pass_recv, out_sem,
):
    experts, kinds, rows, columns = m_ref.shape
    mats = experts * kinds
    slots = CAP * kinds
    rank = r_ref.shape[-1]
    half_m = mats // 2
    f, z = greet(shards_f, groups)
    core = lax.rem(f, 2)
    chip = f // 2
    chips = shards_f // 2
    pair = chip * 2 + 1 - core
    zrows = rows // groups
    started = []

    def go(src, dst, send_sem, recv_sem, to_f, to_z):
        copy = remote(src, dst, send_sem, recv_sem, to_f, to_z)
        copy.start()
        started.append(copy)
        return copy

    def landed(dst, recv_sem):
        remote(dst, dst, recv_sem, recv_sem, f, z).wait_recv()

    step = 128
    zmine = pl.ds(pl.multiple_of(z * zrows, zrows), zrows)
    for e in range(experts):
        for k in range(kinds):
            @pl.loop(0, rows // step)
            def _(i):
                at = pl.ds(pl.multiple_of(i * step, step), step)
                total = m_ref[e, k, at, :].astype(jnp.float32) + g_ref[e, k, at, :].astype(jnp.float32)
                low = total.astype(jnp.bfloat16)
                summed[e, k, at, :] = low
                pbuf[e * kinds + k, at, :] = jnp.dot(low, r_ref[e * kinds + k], preferred_element_type=jnp.float32)
        for j in (2, 3, 1):
            d = lax.rem(z + j, groups)
            go(
                pbuf.at[pl.ds(e * kinds, kinds), pl.ds(pl.multiple_of(d * zrows, zrows), zrows), :],
                precv.at[j - 1, pl.ds(e * kinds, kinds)],
                p_send.at[j - 1, e],
                p_recv.at[j - 1, e],
                f,
                d,
            )

    near = z + 1 - 2 * lax.rem(z, 2)
    upper = z // 2
    inner = 2 - upper
    outer = 3 - 3 * upper
    picks = (
        sel_ref[groups * CAP + 1 - upper],
        sel_ref[outer * CAP],
        sel_ref[inner * CAP],
        sel_ref[near * CAP],
        sel_ref[near * CAP + 1],
    )
    for unit, expert in enumerate(picks):
        for k in range(kinds):
            @pl.loop(0, rows // step)
            def _(i):
                at = pl.ds(pl.multiple_of(i * step, step), step)
                sendbuf[unit, k, at, :] = summed[expert, k, at, :]
    here = pl.ds(pl.multiple_of(z * columns, columns), columns)
    for c in range(CAP):
        expert = sel_ref[z * CAP + c]
        for k in range(kinds):
            @pl.loop(0, rows // step)
            def _(i):
                at = pl.ds(pl.multiple_of(i * step, step), step)
                got[c * kinds + k, at, here] = summed[expert, k, at, :]

    def place(c, source, k):
        return got.at[c * kinds + k, :, pl.ds(pl.multiple_of(source * columns, columns), columns)]

    def send(unit, c, recv, d, k):
        go(sendbuf.at[unit, k], place(c, z, k), s_send.at[unit, k], recv, f, d)

    def far_second(k):
        send(0, 1, second_recv.at[lax.rem(z, 2), k], inner, k)

    def far_outer(k):
        send(1, 0, first_recv.at[z, k], outer, k)

    def far_inner(k):
        send(2, 0, first_recv.at[z, k], inner, k)

    def near_first(k):
        send(3, 0, first_recv.at[z, k], near, k)

    def near_second(k):
        send(4, 1, near_recv.at[k], near, k)

    far = 2 - 2 * upper
    is_inner = (z == 1) | (z == 2)

    def hand_on(k):
        @pl.when(is_inner)
        def _():
            for i in range(2):
                block = place(1, far + i, k)
                landed(block, second_recv.at[i, k])
                remote(block, block, pass_send.at[i, k], pass_recv.at[i, k], f, near).start()

    for j in range(1, groups):
        for e in range(experts):
            landed(precv.at[j - 1, pl.ds(e * kinds, kinds)], p_recv.at[j - 1, e])
    far_second(0)
    near_second(0)

    for m in range(mats):
        total = pbuf[m, zmine, :]
        for j in range(1, groups):
            total = total + precv[j - 1, m]
        pchunk[m] = total
        gram[m] = jnp.dot(total.T, total, precision=HIGHEST, preferred_element_type=jnp.float32)
    go(gram.at[pl.ds((1 - core) * half_m, half_m)], gpair, ga_send, ga_recv, pair, z).wait_recv()
    ghalf[...] = gram[pl.ds(core * half_m, half_m)] + gpair[...]
    prows = rank // chips
    cmine = pl.ds(pl.multiple_of(chip * prows, prows), prows)
    for j in (2, 1, 3):
        other = lax.rem(chip + j, chips)
        go(
            ghalf.at[:, pl.ds(pl.multiple_of(other * prows, prows), prows), :],
            gchip.at[j - 1], gb_send.at[j - 1], gb_recv.at[j - 1], other * 2 + core, z,
        )
    total = ghalf[:, cmine, :]
    for j in range(1, chips):
        landed(gchip.at[j - 1], gb_recv.at[j - 1])
        total = total + gchip[j - 1]
    gpiece[...] = total
    for j in (2, 3, 1):
        go(gpiece, gdepth.at[j - 1], gc_send.at[j - 1], gc_recv.at[j - 1], f, lax.rem(z + j, groups))
    for j in range(1, groups):
        landed(gdepth.at[j - 1], gc_recv.at[j - 1])
        total = total + gdepth[j - 1]
    gfull[:, cmine, :] = total
    for j in (2, 1, 3):
        part = gfull.at[:, cmine, :]
        go(part, part, gd_send.at[j - 1], gd_recv.at[j - 1], lax.rem(chip + j, chips) * 2 + core, z)
    for j in range(1, chips):
        other = lax.rem(chip + chips - j, chips)
        landed(gfull.at[:, pl.ds(pl.multiple_of(other * prows, prows), prows), :], gd_recv.at[j - 1])

    far_second(1)
    far_outer(0)
    near_second(1)
    near_first(0)

    row_at = lax.broadcasted_iota(jnp.int32, (rank, rank), 0)
    col_at = lax.broadcasted_iota(jnp.int32, (rank, rank), 1)
    eye = (row_at == col_at).astype(jnp.float32)
    for m in range(half_m):
        aug[m, :, :rank] = gfull[m] + ridge_term * eye
        aug[m, :, rank:] = eye
    inverse_factor(aug, half_m, rank)
    wmine = pl.ds(core * half_m, half_m)
    wfull[wmine] = aug[:, :, rank:]
    go(wfull.at[wmine], wfull.at[wmine], w_send, w_recv, pair, z)
    landed(wfull.at[pl.ds((1 - core) * half_m, half_m)], w_recv)

    for m in range(mats):
        ortho = jnp.dot(pchunk[m], wfull[m].T, precision=HIGHEST, preferred_element_type=jnp.float32)
        obuf[m, zmine, :] = ortho.astype(jnp.bfloat16)
    for j in (2, 3, 1):
        part = obuf.at[:, zmine, :]
        go(part, part, o_send.at[j - 1], o_recv.at[j - 1], f, lax.rem(z + j, groups))
    for j in range(1, groups):
        source = lax.rem(z + groups - j, groups)
        landed(obuf.at[:, pl.ds(pl.multiple_of(source * zrows, zrows), zrows), :], o_recv.at[j - 1])

    far_outer(1)
    hand_on(0)

    for m in range(mats):
        fpart[m] = jnp.dot(obuf[m].T, summed[m // kinds, m % kinds], preferred_element_type=jnp.float32)
        low_rows = rank // 2
        go(
            fpart.at[m, pl.ds(pl.multiple_of((1 - core) * low_rows, low_rows), low_rows), :],
            fpair.at[m], fa_send.at[m], fa_recv.at[m], pair, z,
        )
    piece = rank // shards_f
    own = pl.ds(pl.multiple_of(core * low_rows, low_rows), low_rows)
    for m in range(mats):
        landed(fpair.at[m], fa_recv.at[m])
        fhalf[m] = fpart[m, own, :] + fpair[m]
    for j in (2, 1, 3):
        other = lax.rem(chip + j, chips)
        go(
            fhalf.at[:, pl.ds(pl.multiple_of(other * piece, piece), piece), :],
            fchip.at[j - 1], fb_send.at[j - 1], fb_recv.at[j - 1], other * 2 + core, z,
        )
    total = fhalf[:, pl.ds(pl.multiple_of(chip * piece, piece), piece), :]
    for j in range(1, chips):
        landed(fchip.at[j - 1], fb_recv.at[j - 1])
        total = total + fchip[j - 1]
    square = total * total
    part_sum = square[:, :, :128]
    for lane in range(128, columns, 128):
        part_sum = part_sum + square[:, :, lane : lane + 128]
    sqbuf[...] = part_sum
    for j in (2, 3, 1):
        go(sqbuf, sqrecv.at[j - 1], sq_send.at[j - 1], sq_recv.at[j - 1], f, lax.rem(z + j, groups))
    fchunk[...] = total
    chunk = core * low_rows + chip * piece
    at = pl.ds(pl.multiple_of(chunk, piece), piece)
    for j in (2, 3, 1):
        d = lax.rem(z + j, groups)
        for c in range(CAP):
            expert = sel_ref[d * CAP + c]
            for k in range(kinds):
                fsend[j - 1, c * kinds + k] = fchunk[expert * kinds + k].astype(jnp.bfloat16)
        go(fsend.at[j - 1], lowbuf.at[:, at, here], fz_send.at[j - 1], fz_recv.at[j - 1], f, d)
    hand_on(1)
    far_inner(0)
    near_first(1)
    far_inner(1)
    for c in range(CAP):
        expert = sel_ref[z * CAP + c]
        for k in range(kinds):
            lowbuf[c * kinds + k, at, here] = fchunk[expert * kinds + k].astype(jnp.bfloat16)
    for j in range(1, groups):
        source = lax.rem(z + groups - j, groups)
        there = pl.ds(pl.multiple_of(source * columns, columns), columns)
        landed(lowbuf.at[:, at, there], fz_recv.at[j - 1])
    for j in range(1, shards_f):
        part = lowbuf.at[:, at, :]
        go(part, part, low_send.at[j - 1], low_recv.at[j - 1], lax.rem(f + j, shards_f), z)
    square = sqbuf[...]
    for j in range(1, groups):
        landed(sqrecv.at[j - 1], sq_recv.at[j - 1])
        square = square + sqrecv[j - 1]
    mean_square = jnp.sum(square, axis=2, keepdims=True) / (groups * columns)
    rightbuf[:, at, :] = fchunk[...] * lax.rsqrt(mean_square + epsilon)
    for j in range(1, shards_f):
        part = rightbuf.at[:, at, :]
        go(part, part, right_send.at[j - 1], right_recv.at[j - 1], lax.rem(f + j, shards_f), z)
    for c in range(CAP):
        expert = sel_ref[z * CAP + c]
        for k in range(kinds):
            low_out[c * kinds + k] = obuf[expert * kinds + k]

    kept = []

    def keep(c, source, k):
        there = pl.ds(pl.multiple_of(source * columns, columns), columns)
        copy = pltpu.make_async_copy(
            place(c, source, k), got_out.at[c * kinds + k, :, there], out_sem.at[len(kept)]
        )
        copy.start()
        kept.append(copy)

    for k in range(kinds):
        keep(0, z, k)
        keep(1, z, k)
    for k in range(kinds):
        landed(place(1, near, k), near_recv.at[k])
        keep(1, near, k)
    for k in range(kinds):
        for source in (near, far, far + 1):
            landed(place(0, source, k), first_recv.at[source, k])
            keep(0, source, k)

    @pl.when(is_inner)
    def _():
        for i in range(2):
            for k in range(kinds):
                block = place(1, far + i, k)
                remote(block, block, pass_send.at[i, k], pass_recv.at[i, k], f, near).wait_send()

    @pl.when(jnp.logical_not(is_inner))
    def _():
        for i in range(2):
            for k in range(kinds):
                landed(place(1, far + i, k), pass_recv.at[i, k])

    for i in range(2):
        for k in range(kinds):
            keep(1, far + i, k)
    for buffer, recv in ((lowbuf, low_recv), (rightbuf, right_recv)):
        for j in range(1, shards_f):
            source = lax.rem(f + shards_f - j, shards_f)
            start = lax.rem(source, 2) * low_rows + (source // 2) * piece
            landed(buffer.at[:, pl.ds(pl.multiple_of(start, piece), piece), :], recv.at[j - 1])
    fact_out[...] = lowbuf[...]
    right_out[...] = rightbuf[...]
    for copy in started:
        copy.wait_send()
    for copy in kept:
        copy.wait()


def fresh_kernel(used_ref, got_ref, low_ref, fact_ref, state_ref, left_ref):
    m = pl.program_id(0)
    update = jnp.dot(low_ref[0], fact_ref[0], preferred_element_type=jnp.float32)
    fresh = got_ref[0].astype(jnp.float32) - feedback * update
    state_ref[0] = jnp.where(used_ref[m] > 0, fresh, 0.0).astype(jnp.bfloat16)
    left = low_ref[0].astype(jnp.float32) * math.sqrt(D)
    left_ref[0] = jnp.where(used_ref[m] > 0, left, 0.0)


def shards(momentum, gradient, right_in, owners):
    groups = lax.axis_size("tensor")
    shards_f = lax.axis_size("fsdp")
    experts, kinds, rows, columns = momentum.shape
    rank = right_in.shape[-1]
    hidden = groups * columns
    mats = CAP * kinds
    z = lax.axis_index("tensor")
    index_line = jnp.arange(experts, dtype=jnp.int32)
    same_owner = owners[:, None] == owners[None, :]
    earlier = index_line[None, :] < index_line[:, None]
    position = jnp.sum((same_owner & earlier).astype(jnp.int32), axis=1)
    slot = owners * CAP + position
    hit = slot[:, None] == jnp.arange(groups * CAP, dtype=jnp.int32)[None, :]
    sel = jnp.sum(jnp.where(hit, index_line[:, None], 0), axis=0).astype(jnp.int32)
    second = sel.reshape(groups, CAP)[:, 1] * jnp.sum(hit, axis=0).reshape(groups, CAP)[:, 1]
    sel = jnp.concatenate([sel, second.reshape(2, groups // 2).sum(axis=1).astype(jnp.int32)])
    here = slot[:, None] == (z * CAP + jnp.arange(mats, dtype=jnp.int32) // kinds)[None, :]
    used = jnp.sum(here.astype(jnp.int32), axis=0)

    smem = pl.BlockSpec(memory_space=pltpu.SMEM)
    vmem = pl.BlockSpec(memory_space=pltpu.VMEM)
    hbm = pl.BlockSpec(memory_space=pl.ANY)
    f32, bf16 = jnp.float32, jnp.bfloat16
    shape = jax.ShapeDtypeStruct
    dma = pltpu.SemaphoreType.DMA
    chips = shards_f // 2
    every = experts * kinds
    half_m = every // 2
    zrows = rows // groups
    piece = rank // shards_f
    near_z, near_c, near_f = groups - 1, chips - 1, shards_f - 1
    got, low, fact, right = pl.pallas_call(
        functools.partial(step_kernel, shards_f, groups),
        out_shape=(
            shape((mats, rows, hidden), bf16),
            shape((mats, rows, rank), bf16),
            shape((mats, rank, hidden), bf16),
            shape((every, rank, columns), f32),
        ),
        in_specs=[smem, vmem, vmem, vmem],
        out_specs=(hbm, vmem, vmem, vmem),
        scratch_shapes=[
            pltpu.VMEM((experts, kinds, rows, columns), bf16),
            pltpu.VMEM((5, kinds, rows, columns), bf16),
            pltpu.VMEM((mats, rows, hidden), bf16),
            pltpu.VMEM((every, rows, rank), f32),
            pltpu.VMEM((near_z, every, zrows, rank), f32),
            pltpu.VMEM((every, zrows, rank), f32),
            pltpu.VMEM((every, rank, rank), f32),
            pltpu.VMEM((half_m, rank, rank), f32),
            pltpu.VMEM((half_m, rank, rank), f32),
            pltpu.VMEM((near_c, half_m, rank // chips, rank), f32),
            pltpu.VMEM((half_m, rank // chips, rank), f32),
            pltpu.VMEM((near_z, half_m, rank // chips, rank), f32),
            pltpu.VMEM((half_m, rank, rank), f32),
            pltpu.VMEM((half_m, rank, 2 * rank), f32),
            pltpu.VMEM((every, rank, rank), f32),
            pltpu.VMEM((every, rows, rank), bf16),
            pltpu.VMEM((every, rank, columns), f32),
            pltpu.VMEM((every, rank // 2, columns), f32),
            pltpu.VMEM((every, rank // 2, columns), f32),
            pltpu.VMEM((near_c, every, piece, columns), f32),
            pltpu.VMEM((every, piece, columns), f32),
            pltpu.VMEM((near_z, mats, piece, columns), bf16),
            pltpu.VMEM((mats, rank, hidden), bf16),
            pltpu.VMEM((every, piece, 128), f32),
            pltpu.VMEM((near_z, every, piece, 128), f32),
            pltpu.VMEM((every, rank, columns), f32),
            dma((near_z, experts)), dma((near_z, experts)),
            dma, dma,
            dma((near_c,)), dma((near_c,)),
            dma((near_z,)), dma((near_z,)),
            dma((near_c,)), dma((near_c,)),
            dma, dma,
            dma((near_z,)), dma((near_z,)),
            dma((every,)), dma((every,)),
            dma((near_c,)), dma((near_c,)),
            dma((near_z,)), dma((near_z,)),
            dma((near_z,)), dma((near_z,)),
            dma((near_f,)), dma((near_f,)),
            dma((near_f,)), dma((near_f,)),
            dma((5, kinds)), dma((groups, kinds)), dma((kinds,)),
            dma((2, kinds)), dma((2, kinds)), dma((2, kinds)), dma((groups * mats,)),
        ],
        compiler_params=pltpu.CompilerParams(
            collective_id=0, has_side_effects=True, vmem_limit_bytes=VMEM_BYTES
        ),
        name="step",
    )(sel, momentum, gradient, right_in.reshape(every, columns, rank))

    band = min(rows, 256)
    state, left = pl.pallas_call(
        fresh_kernel,
        grid=(mats, rows // band),
        out_shape=(shape((mats, rows, hidden), bf16), shape((mats, rows, rank), f32)),
        in_specs=[
            smem,
            pl.BlockSpec((1, band, hidden), lambda m, i: (m, i, 0)),
            pl.BlockSpec((1, band, rank), lambda m, i: (m, i, 0)),
            pl.BlockSpec((1, rank, hidden), lambda m, i: (m, 0, 0)),
        ],
        out_specs=(
            pl.BlockSpec((1, band, hidden), lambda m, i: (m, i, 0)),
            pl.BlockSpec((1, band, rank), lambda m, i: (m, i, 0)),
        ),
        name="fresh",
    )(used, got, low, fact)
    right_new = jnp.swapaxes(right, 1, 2).reshape(experts, kinds, columns, rank)
    return (
        state.reshape(CAP, kinds, rows, hidden),
        left.reshape(CAP, kinds, rows, rank),
        right_new,
    )


def solution(mesh):
    fits = mesh.shape["fsdp"] == 8 and mesh.shape["tensor"] == 4
    return jax.shard_map(
        shards if fits else general_shards,
        mesh=mesh,
        in_specs=(
            P(None, None, "fsdp", "tensor"),
            P(None, None, "fsdp", "tensor"),
            P(None, None, "tensor", None),
            P(),
        ),
        out_specs=(
            P("tensor", None, "fsdp", None),
            P("tensor", None, "fsdp", None),
            P(None, None, "tensor", None),
        ),
        check_vma=False,
    )
```

```python
import functools
import math

import jax
import jax.numpy as jnp
from jax import lax
from jax.experimental import pallas as pl
from jax.experimental.pallas import tpu as pltpu
from jax.sharding import PartitionSpec as P

D = 4096
CAP = 2


ridge_term = 0.001
feedback = 0.1
epsilon = 1e-06


def orthonormal(panel, gram_total):
    eye_matrix = jnp.eye(gram_total.shape[-1], dtype=jnp.float32)
    lower_factor = jnp.linalg.cholesky(gram_total + ridge_term * eye_matrix)
    solved = jax.scipy.linalg.solve_triangular(
        lower_factor, jnp.swapaxes(panel, -1, -2), lower=True
    )
    return jnp.swapaxes(solved, -1, -2)


def slot_table(owners, groups, capacity):
    count = owners.shape[0]
    index_line = jnp.arange(count, dtype=jnp.int32)
    same_owner = owners[:, None] == owners[None, :]
    earlier = index_line[None, :] < index_line[:, None]
    position = jnp.sum((same_owner & earlier).astype(jnp.int32), axis=1)
    owner_hit = owners[:, None, None] == jnp.arange(groups, dtype=jnp.int32)[None, :, None]
    slot_hit = position[:, None, None] == jnp.arange(capacity, dtype=jnp.int32)[None, None, :]
    return (owner_hit & slot_hit).astype(jnp.float32)


def general_shards(momentum, gradient, right_in, owners):
    highest = lax.Precision.HIGHEST
    groups = lax.axis_size("tensor")
    rows = momentum.shape[2]
    columns = momentum.shape[3]
    owner_table = slot_table(owners, groups, CAP)
    table_low = owner_table.astype(jnp.bfloat16)
    summed = (momentum.astype(jnp.float32) + gradient.astype(jnp.float32)).astype(jnp.bfloat16)
    scale = math.sqrt(D)
    send_state = jnp.einsum(
        "edc,emrk->cmrdk", table_low, summed, preferred_element_type=jnp.float32
    ).astype(jnp.bfloat16)
    send_right = jnp.einsum(
        "edc,emkq->cmkdq", table_low, right_in, preferred_element_type=jnp.float32
    ).astype(jnp.bfloat16)
    got_state, got_right = (
        lax.all_to_all(send_state, "tensor", split_axis=3, concat_axis=3, tiled=True),
        lax.all_to_all(send_right, "tensor", split_axis=3, concat_axis=3, tiled=True),
    )
    panel = jnp.einsum(
        "cmrtk,cmktq->cmrq", got_state, got_right, preferred_element_type=jnp.float32
    )
    gram_part = jnp.einsum("cmrq,cmrs->cmqs", panel, panel, precision=highest)
    gram_total = lax.psum(gram_part, "fsdp")
    ortho = orthonormal(panel, gram_total)
    ortho_low = ortho.astype(jnp.bfloat16)
    factor_part = jnp.einsum(
        "cmrtk,cmrq->cmktq", got_state, ortho_low, preferred_element_type=jnp.float32
    )
    factor = lax.psum(factor_part, "fsdp")
    mean_square = jnp.mean(factor * factor, axis=(2, 3))
    right_new = factor * lax.rsqrt(mean_square + epsilon)[:, :, None, None, :]
    update = jnp.einsum("cmrq,cmktq->cmrtk", ortho, factor, precision=highest)
    fresh = (got_state.astype(jnp.float32) - feedback * update).astype(jnp.bfloat16)
    state_out = fresh.reshape(CAP, fresh.shape[1], rows, groups * columns)
    left_out = ortho * scale
    returned = lax.all_to_all(right_new, "tensor", split_axis=3, concat_axis=3, tiled=True)
    right_out = jnp.einsum("edc,cmkdq->emkq", owner_table, returned, precision=highest)
    return (state_out, left_out, right_out)


MESH = pl.DeviceIdType.MESH
HIGHEST = lax.Precision.HIGHEST
VMEM_BYTES = 56 * 1024 * 1024


def greet(shards_f, groups):
    f = lax.axis_index("fsdp")
    z = lax.axis_index("tensor")
    barrier = pltpu.get_barrier_semaphore()
    for j in range(1, shards_f):
        pl.semaphore_signal(
            barrier, inc=1, device_id={"fsdp": lax.rem(f + j, shards_f), "tensor": z}, device_id_type=MESH
        )
    for j in range(1, groups):
        pl.semaphore_signal(
            barrier, inc=1, device_id={"fsdp": f, "tensor": lax.rem(z + j, groups)}, device_id_type=MESH
        )
    pl.semaphore_wait(barrier, shards_f - 1 + groups - 1)
    return f, z


def remote(src, dst, send_sem, recv_sem, f, z):
    return pltpu.make_async_remote_copy(
        src_ref=src,
        dst_ref=dst,
        send_sem=send_sem,
        recv_sem=recv_sem,
        device_id={"fsdp": f, "tensor": z},
        device_id_type=MESH,
    )


def inverse_factor(aug, mats, rank):
    block = 32
    wide = (mats, block, 2 * block)
    wide_row = lax.broadcasted_iota(jnp.int32, wide, 1)
    wide_col = lax.broadcasted_iota(jnp.int32, wide, 2)
    on_diagonal = wide_row == wide_col
    small = (mats, block, block)
    small_eye = (lax.broadcasted_iota(jnp.int32, small, 1) == lax.broadcasted_iota(jnp.int32, small, 2)).astype(jnp.float32)
    for start in range(0, rank, block):
        stop = start + block

        def eliminate(k, both):
            row = jnp.sum(jnp.where(wide_row == k, both, 0.0), axis=1, keepdims=True)
            column = jnp.sum(jnp.where(wide_col == k, both, 0.0), axis=2, keepdims=True)
            pivot = jnp.sum(jnp.where(wide_col[:, :1] == k, row, 0.0), axis=2, keepdims=True)
            ratio = jnp.where(wide_row[:, :, :1] > k, column * (1.0 / pivot), 0.0)
            return both - ratio * row

        both = jnp.concatenate([aug[:, start:stop, start:stop], small_eye], axis=2)
        both = lax.fori_loop(0, block, eliminate, both, unroll=4)
        diagonal = jnp.sum(jnp.where(on_diagonal, both, 0.0), axis=2, keepdims=True)
        inverse = both[:, :, block:] * lax.rsqrt(diagonal)
        for m in range(mats):
            top = jnp.dot(inverse[m], aug[m, start:stop, :], precision=HIGHEST, preferred_element_type=jnp.float32)
            aug[m, start:stop, :] = top
            if stop < rank:
                below = top[:, :rank].T[stop:]
                aug[m, stop:, :] -= jnp.dot(below, top, precision=HIGHEST, preferred_element_type=jnp.float32)


def step_kernel(
    shards_f, groups, kinds,
    sel_ref, m_ref, g_ref, r_ref,
    got_out, low_out, fact_out, right_out,
    summed, sendbuf, got, pbuf, precv, pchunk,
    gram, gnear, gpair, ghalf, gchip, aug, wfull,
    obuf, fpart, fpair, fhalf, fchip, fchunk, fsend, lowbuf, sqbuf, sqrecv, rightbuf,
    p_send, p_recv, ga_send, ga_recv, gb_send, gb_recv,
    w_send, w_recv, o_send, o_recv, fa_send, fa_recv, fb_send, fb_recv, fz_send, fz_recv,
    sq_send, sq_recv, low_send, low_recv, right_send, right_recv,
    s_send, first_recv, near_recv, second_recv, pass_send, pass_recv, out_sem,
):
    mats, rows, columns = m_ref.shape
    experts = mats // kinds
    slots = CAP * kinds
    rank = r_ref.shape[-1]
    units = 2 * mats // groups
    f, z = greet(shards_f, groups)
    core = lax.rem(f, 2)
    chip = f // 2
    chips = shards_f // 2
    pair = chip * 2 + 1 - core
    urows = rows // 2
    started = []

    def go(src, dst, send_sem, recv_sem, to_f, to_z):
        copy = remote(src, dst, send_sem, recv_sem, to_f, to_z)
        copy.start()
        started.append(copy)
        return copy

    def landed(dst, recv_sem):
        remote(dst, dst, recv_sem, recv_sem, f, z).wait_recv()

    for j in (2, 3, 1, 0):
        d = lax.rem(z + j, groups)
        for i in range(units):
            u = d * units + i
            m = u // 2
            top = lax.rem(u, 2) * urows

            @pl.loop(0, urows // 128)
            def _(b):
                at = pl.ds(pl.multiple_of(top + b * 128, 128), 128)
                total = m_ref[m, at, :].astype(jnp.float32) + g_ref[m, at, :].astype(jnp.float32)
                low = total.astype(jnp.bfloat16)
                summed[m, at, :] = low
                pbuf[u, pl.ds(pl.multiple_of(b * 128, 128), 128), :] = jnp.dot(
                    low, r_ref[m], preferred_element_type=jnp.float32
                )
        if j:
            go(pbuf.at[pl.ds(d * units, units)], precv.at[j - 1], p_send.at[j - 1], p_recv.at[j - 1], f, d)

    step = 128
    near = z + 1 - 2 * lax.rem(z, 2)
    upper = z // 2
    inner = 2 - upper
    outer = 3 - 3 * upper
    picks = (
        sel_ref[groups * CAP + 1 - upper],
        sel_ref[outer * CAP],
        sel_ref[inner * CAP],
        sel_ref[near * CAP],
        sel_ref[near * CAP + 1],
    )
    for unit, expert in enumerate(picks):
        for k in range(kinds):
            @pl.loop(0, rows // step)
            def _(i):
                at = pl.ds(pl.multiple_of(i * step, step), step)
                sendbuf[unit, k, at, :] = summed[expert * kinds + k, at, :]
    here = pl.ds(pl.multiple_of(z * columns, columns), columns)
    for c in range(CAP):
        expert = sel_ref[z * CAP + c]
        for k in range(kinds):
            @pl.loop(0, rows // step)
            def _(i):
                at = pl.ds(pl.multiple_of(i * step, step), step)
                got[c * kinds + k, at, here] = summed[expert * kinds + k, at, :]

    def place(c, source, k):
        return got.at[c * kinds + k, :, pl.ds(pl.multiple_of(source * columns, columns), columns)]

    def send(unit, c, recv, d, k):
        go(sendbuf.at[unit, k], place(c, z, k), s_send.at[unit, k], recv, f, d)

    def far_second(k):
        send(0, 1, second_recv.at[lax.rem(z, 2), k], inner, k)

    def far_outer(k):
        send(1, 0, first_recv.at[z, k], outer, k)

    def far_inner(k):
        send(2, 0, first_recv.at[z, k], inner, k)

    def near_first(k):
        send(3, 0, first_recv.at[z, k], near, k)

    def near_second(k):
        send(4, 1, near_recv.at[k], near, k)

    far = 2 - 2 * upper
    is_inner = (z == 1) | (z == 2)

    def hand_on(k):
        @pl.when(is_inner)
        def _():
            for i in range(2):
                block = place(1, far + i, k)
                landed(block, second_recv.at[i, k])
                remote(block, block, pass_send.at[i, k], pass_recv.at[i, k], f, near).start()

    odd = lax.rem(z, 2)
    for j in range(1, groups):
        landed(precv.at[j - 1], p_recv.at[j - 1])
    for i in range(units):
        total = pbuf[z * units + i]
        for j in range(1, groups):
            total = total + precv[j - 1, i]
        pchunk[i] = total

    def gram_of(i):
        panel = pchunk[i]
        return jnp.dot(panel.T, panel, precision=HIGHEST, preferred_element_type=jnp.float32)

    gram[2] = gram_of(2 - 2 * odd)
    shared = go(gram.at[2], gnear, ga_send.at[0], ga_recv.at[0], f, near)
    gram[0] = gram_of(odd) + gram_of(odd + 1)
    shared.wait_recv()
    gram[1] = gram[2] + gnear[...]
    far_second(0)
    near_second(0)
    far_second(1)
    near_second(1)
    near_first(0)
    near_first(1)
    go(gram.at[1 - core], gpair, ga_send.at[1], ga_recv.at[1], pair, z).wait_recv()
    total = gram[core] + gpair[...]
    ghalf[...] = total
    for j in (2, 1, 3):
        go(
            ghalf, gchip.at[j - 1], gb_send.at[j - 1], gb_recv.at[j - 1],
            lax.rem(chip + j, chips) * 2 + core, z,
        )
    for j in range(1, chips):
        landed(gchip.at[j - 1], gb_recv.at[j - 1])
        total = total + gchip[j - 1]

    row_at = lax.broadcasted_iota(jnp.int32, (rank, rank), 0)
    col_at = lax.broadcasted_iota(jnp.int32, (rank, rank), 1)
    eye = (row_at == col_at).astype(jnp.float32)
    aug[0, :, :rank] = total + ridge_term * eye
    aug[0, :, rank:] = eye
    inverse_factor(aug, 1, rank)
    wfull[core] = aug[0, :, rank:]
    go(wfull.at[core], wfull.at[core], w_send, w_recv, pair, z)
    landed(wfull.at[1 - core], w_recv)

    for i, which in enumerate((odd, 0, 1 - odd)):
        ortho = jnp.dot(pchunk[i], wfull[which].T, precision=HIGHEST, preferred_element_type=jnp.float32)
        obuf[z * units + i] = ortho.astype(jnp.bfloat16)
    for j in (2, 3, 1):
        part = obuf.at[pl.ds(z * units, units)]
        go(part, part, o_send.at[j - 1], o_recv.at[j - 1], f, lax.rem(z + j, groups))
    for j in range(1, groups):
        source = lax.rem(z + groups - j, groups)
        landed(obuf.at[pl.ds(source * units, units)], o_recv.at[j - 1])

    far_inner(0)
    hand_on(0)

    for m in range(mats):
        fpart[m] = jnp.dot(
            obuf[2 * m].T, summed[m, :urows], preferred_element_type=jnp.float32
        ) + jnp.dot(obuf[2 * m + 1].T, summed[m, urows:], preferred_element_type=jnp.float32)
        low_rows = rank // 2
        go(
            fpart.at[m, pl.ds(pl.multiple_of((1 - core) * low_rows, low_rows), low_rows), :],
            fpair.at[m], fa_send.at[m], fa_recv.at[m], pair, z,
        )
    piece = rank // shards_f
    own = pl.ds(pl.multiple_of(core * low_rows, low_rows), low_rows)
    for m in range(mats):
        landed(fpair.at[m], fa_recv.at[m])
        fhalf[m] = fpart[m, own, :] + fpair[m]
    for j in (2, 1, 3):
        other = lax.rem(chip + j, chips)
        go(
            fhalf.at[:, pl.ds(pl.multiple_of(other * piece, piece), piece), :],
            fchip.at[j - 1], fb_send.at[j - 1], fb_recv.at[j - 1], other * 2 + core, z,
        )
    total = fhalf[:, pl.ds(pl.multiple_of(chip * piece, piece), piece), :]
    for j in range(1, chips):
        landed(fchip.at[j - 1], fb_recv.at[j - 1])
        total = total + fchip[j - 1]
    square = total * total
    part_sum = square[:, :, :128]
    for lane in range(128, columns, 128):
        part_sum = part_sum + square[:, :, lane : lane + 128]
    sqbuf[...] = part_sum
    for j in (2, 3, 1):
        go(sqbuf, sqrecv.at[j - 1], sq_send.at[j - 1], sq_recv.at[j - 1], f, lax.rem(z + j, groups))
    fchunk[...] = total
    chunk = core * low_rows + chip * piece
    at = pl.ds(pl.multiple_of(chunk, piece), piece)
    for j in (2, 3, 1):
        d = lax.rem(z + j, groups)
        for c in range(CAP):
            expert = sel_ref[d * CAP + c]
            for k in range(kinds):
                fsend[j - 1, c * kinds + k] = fchunk[expert * kinds + k].astype(jnp.bfloat16)
        go(fsend.at[j - 1], lowbuf.at[:, at, here], fz_send.at[j - 1], fz_recv.at[j - 1], f, d)
    hand_on(1)
    far_outer(0)
    far_outer(1)
    far_inner(1)
    for c in range(CAP):
        expert = sel_ref[z * CAP + c]
        for k in range(kinds):
            lowbuf[c * kinds + k, at, here] = fchunk[expert * kinds + k].astype(jnp.bfloat16)
    for j in range(1, groups):
        source = lax.rem(z + groups - j, groups)
        there = pl.ds(pl.multiple_of(source * columns, columns), columns)
        landed(lowbuf.at[:, at, there], fz_recv.at[j - 1])
    for j in (2, 1, 3):
        part = lowbuf.at[:, at, :]
        go(part, part, low_send.at[j - 1], low_recv.at[j - 1], lax.rem(chip + j, chips) * 2 + core, z)
    square = sqbuf[...]
    for j in range(1, groups):
        landed(sqrecv.at[j - 1], sq_recv.at[j - 1])
        square = square + sqrecv[j - 1]
    mean_square = jnp.sum(square, axis=2, keepdims=True) / (groups * columns)
    rightbuf[:, at, :] = fchunk[...] * lax.rsqrt(mean_square + epsilon)
    for j in (2, 1, 3):
        part = rightbuf.at[:, at, :]
        go(part, part, right_send.at[j - 1], right_recv.at[j - 1], lax.rem(chip + j, chips) * 2 + core, z)
    theirs = pl.ds(pl.multiple_of((1 - core) * low_rows, low_rows), low_rows)
    for buffer, sent, recv in ((lowbuf, low_send, low_recv), (rightbuf, right_send, right_recv)):
        for j in range(1, chips):
            start = core * low_rows + lax.rem(chip + chips - j, chips) * piece
            landed(buffer.at[:, pl.ds(pl.multiple_of(start, piece), piece), :], recv.at[j - 1])
        part = buffer.at[:, own, :]
        go(part, part, sent.at[chips - 1], recv.at[chips - 1], pair, z)
    for c in range(CAP):
        expert = sel_ref[z * CAP + c]
        for k in range(kinds):
            low_out[c * kinds + k, :urows] = obuf[(expert * kinds + k) * 2]
            low_out[c * kinds + k, urows:] = obuf[(expert * kinds + k) * 2 + 1]

    kept = []

    def keep(c, source, k):
        there = pl.ds(pl.multiple_of(source * columns, columns), columns)
        copy = pltpu.make_async_copy(
            place(c, source, k), got_out.at[c * kinds + k, :, there], out_sem.at[len(kept)]
        )
        copy.start()
        kept.append(copy)

    for k in range(kinds):
        keep(0, z, k)
        keep(1, z, k)
    for k in range(kinds):
        landed(place(1, near, k), near_recv.at[k])
        keep(1, near, k)
    for k in range(kinds):
        for source in (near, far, far + 1):
            landed(place(0, source, k), first_recv.at[source, k])
            keep(0, source, k)

    @pl.when(is_inner)
    def _():
        for i in range(2):
            for k in range(kinds):
                block = place(1, far + i, k)
                remote(block, block, pass_send.at[i, k], pass_recv.at[i, k], f, near).wait_send()

    @pl.when(jnp.logical_not(is_inner))
    def _():
        for i in range(2):
            for k in range(kinds):
                landed(place(1, far + i, k), pass_recv.at[i, k])

    for i in range(2):
        for k in range(kinds):
            keep(1, far + i, k)
    for buffer, recv in ((lowbuf, low_recv), (rightbuf, right_recv)):
        landed(buffer.at[:, theirs, :], recv.at[chips - 1])
    fact_out[...] = lowbuf[...]
    right_out[...] = rightbuf[...]
    for copy in started:
        copy.wait_send()
    for copy in kept:
        copy.wait()


def fresh_kernel(used_ref, got_ref, low_ref, fact_ref, state_ref, left_ref):
    m = pl.program_id(0)
    update = jnp.dot(low_ref[0], fact_ref[0], preferred_element_type=jnp.float32)
    fresh = got_ref[0].astype(jnp.float32) - feedback * update
    state_ref[0] = jnp.where(used_ref[m] > 0, fresh, 0.0).astype(jnp.bfloat16)
    left = low_ref[0].astype(jnp.float32) * math.sqrt(D)
    left_ref[0] = jnp.where(used_ref[m] > 0, left, 0.0)


def shards(momentum, gradient, right_in, owners):
    groups = lax.axis_size("tensor")
    shards_f = lax.axis_size("fsdp")
    experts, kinds, rows, columns = momentum.shape
    rank = right_in.shape[-1]
    hidden = groups * columns
    mats = CAP * kinds
    z = lax.axis_index("tensor")
    index_line = jnp.arange(experts, dtype=jnp.int32)
    same_owner = owners[:, None] == owners[None, :]
    earlier = index_line[None, :] < index_line[:, None]
    position = jnp.sum((same_owner & earlier).astype(jnp.int32), axis=1)
    slot = owners * CAP + position
    hit = slot[:, None] == jnp.arange(groups * CAP, dtype=jnp.int32)[None, :]
    sel = jnp.sum(jnp.where(hit, index_line[:, None], 0), axis=0).astype(jnp.int32)
    second = sel.reshape(groups, CAP)[:, 1] * jnp.sum(hit, axis=0).reshape(groups, CAP)[:, 1]
    sel = jnp.concatenate([sel, second.reshape(2, groups // 2).sum(axis=1).astype(jnp.int32)])
    here = slot[:, None] == (z * CAP + jnp.arange(mats, dtype=jnp.int32) // kinds)[None, :]
    used = jnp.sum(here.astype(jnp.int32), axis=0)

    smem = pl.BlockSpec(memory_space=pltpu.SMEM)
    vmem = pl.BlockSpec(memory_space=pltpu.VMEM)
    hbm = pl.BlockSpec(memory_space=pl.ANY)
    f32, bf16 = jnp.float32, jnp.bfloat16
    shape = jax.ShapeDtypeStruct
    dma = pltpu.SemaphoreType.DMA
    chips = shards_f // 2
    every = experts * kinds
    units = 2 * every // groups
    piece = rank // shards_f
    near_z, near_c = groups - 1, chips - 1
    got, low, fact, right = pl.pallas_call(
        functools.partial(step_kernel, shards_f, groups, kinds),
        out_shape=(
            shape((mats, rows, hidden), bf16),
            shape((mats, rows, rank), bf16),
            shape((mats, rank, hidden), bf16),
            shape((every, rank, columns), f32),
        ),
        in_specs=[smem, vmem, vmem, vmem],
        out_specs=(hbm, vmem, vmem, vmem),
        scratch_shapes=[
            pltpu.VMEM((every, rows, columns), bf16),
            pltpu.VMEM((5, kinds, rows, columns), bf16),
            pltpu.VMEM((mats, rows, hidden), bf16),
            pltpu.VMEM((2 * every, rows // 2, rank), f32),
            pltpu.VMEM((near_z, units, rows // 2, rank), f32),
            pltpu.VMEM((units, rows // 2, rank), f32),
            pltpu.VMEM((3, rank, rank), f32),
            pltpu.VMEM((rank, rank), f32),
            pltpu.VMEM((rank, rank), f32),
            pltpu.VMEM((rank, rank), f32),
            pltpu.VMEM((near_c, rank, rank), f32),
            pltpu.VMEM((1, rank, 2 * rank), f32),
            pltpu.VMEM((2, rank, rank), f32),
            pltpu.VMEM((2 * every, rows // 2, rank), bf16),
            pltpu.VMEM((every, rank, columns), f32),
            pltpu.VMEM((every, rank // 2, columns), f32),
            pltpu.VMEM((every, rank // 2, columns), f32),
            pltpu.VMEM((near_c, every, piece, columns), f32),
            pltpu.VMEM((every, piece, columns), f32),
            pltpu.VMEM((near_z, mats, piece, columns), bf16),
            pltpu.VMEM((mats, rank, hidden), bf16),
            pltpu.VMEM((every, piece, 128), f32),
            pltpu.VMEM((near_z, every, piece, 128), f32),
            pltpu.VMEM((every, rank, columns), f32),
            dma((near_z,)), dma((near_z,)),
            dma((2,)), dma((2,)),
            dma((near_c,)), dma((near_c,)),
            dma, dma,
            dma((near_z,)), dma((near_z,)),
            dma((every,)), dma((every,)),
            dma((near_c,)), dma((near_c,)),
            dma((near_z,)), dma((near_z,)),
            dma((near_z,)), dma((near_z,)),
            dma((chips,)), dma((chips,)),
            dma((chips,)), dma((chips,)),
            dma((5, kinds)), dma((groups, kinds)), dma((kinds,)),
            dma((2, kinds)), dma((2, kinds)), dma((2, kinds)), dma((groups * mats,)),
        ],
        compiler_params=pltpu.CompilerParams(
            collective_id=0, has_side_effects=True, vmem_limit_bytes=VMEM_BYTES
        ),
        name="step",
    )(
        sel,
        momentum.reshape(every, rows, columns),
        gradient.reshape(every, rows, columns),
        right_in.reshape(every, columns, rank),
    )

    band = min(rows, 256)
    state, left = pl.pallas_call(
        fresh_kernel,
        grid=(mats, rows // band),
        out_shape=(shape((mats, rows, hidden), bf16), shape((mats, rows, rank), f32)),
        in_specs=[
            smem,
            pl.BlockSpec((1, band, hidden), lambda m, i: (m, i, 0)),
            pl.BlockSpec((1, band, rank), lambda m, i: (m, i, 0)),
            pl.BlockSpec((1, rank, hidden), lambda m, i: (m, 0, 0)),
        ],
        out_specs=(
            pl.BlockSpec((1, band, hidden), lambda m, i: (m, i, 0)),
            pl.BlockSpec((1, band, rank), lambda m, i: (m, i, 0)),
        ),
        name="fresh",
    )(used, got, low, fact)
    right_new = jnp.swapaxes(right, 1, 2).reshape(experts, kinds, columns, rank)
    return (
        state.reshape(CAP, kinds, rows, hidden),
        left.reshape(CAP, kinds, rows, rank),
        right_new,
    )


def solution(mesh):
    fits = mesh.shape["fsdp"] == 8 and mesh.shape["tensor"] == 4
    return jax.shard_map(
        shards if fits else general_shards,
        mesh=mesh,
        in_specs=(
            P(None, None, "fsdp", "tensor"),
            P(None, None, "fsdp", "tensor"),
            P(None, None, "tensor", None),
            P(),
        ),
        out_specs=(
            P("tensor", None, "fsdp", None),
            P("tensor", None, "fsdp", None),
            P(None, None, "tensor", None),
        ),
        check_vma=False,
    )
```

```python
import functools
import math

import jax
import jax.numpy as jnp
from jax import lax
from jax.experimental import pallas as pl
from jax.experimental.pallas import tpu as pltpu
from jax.sharding import PartitionSpec as P

D = 4096
CAP = 2


ridge_term = 0.001
feedback = 0.1
epsilon = 1e-06


def orthonormal(panel, gram_total):
    eye_matrix = jnp.eye(gram_total.shape[-1], dtype=jnp.float32)
    lower_factor = jnp.linalg.cholesky(gram_total + ridge_term * eye_matrix)
    solved = jax.scipy.linalg.solve_triangular(
        lower_factor, jnp.swapaxes(panel, -1, -2), lower=True
    )
    return jnp.swapaxes(solved, -1, -2)


def slot_table(owners, groups, capacity):
    count = owners.shape[0]
    index_line = jnp.arange(count, dtype=jnp.int32)
    same_owner = owners[:, None] == owners[None, :]
    earlier = index_line[None, :] < index_line[:, None]
    position = jnp.sum((same_owner & earlier).astype(jnp.int32), axis=1)
    owner_hit = owners[:, None, None] == jnp.arange(groups, dtype=jnp.int32)[None, :, None]
    slot_hit = position[:, None, None] == jnp.arange(capacity, dtype=jnp.int32)[None, None, :]
    return (owner_hit & slot_hit).astype(jnp.float32)


def general_shards(momentum, gradient, right_in, owners):
    highest = lax.Precision.HIGHEST
    groups = lax.axis_size("tensor")
    rows = momentum.shape[2]
    columns = momentum.shape[3]
    owner_table = slot_table(owners, groups, CAP)
    table_low = owner_table.astype(jnp.bfloat16)
    summed = (momentum.astype(jnp.float32) + gradient.astype(jnp.float32)).astype(jnp.bfloat16)
    scale = math.sqrt(D)
    send_state = jnp.einsum(
        "edc,emrk->cmrdk", table_low, summed, preferred_element_type=jnp.float32
    ).astype(jnp.bfloat16)
    send_right = jnp.einsum(
        "edc,emkq->cmkdq", table_low, right_in, preferred_element_type=jnp.float32
    ).astype(jnp.bfloat16)
    got_state, got_right = (
        lax.all_to_all(send_state, "tensor", split_axis=3, concat_axis=3, tiled=True),
        lax.all_to_all(send_right, "tensor", split_axis=3, concat_axis=3, tiled=True),
    )
    panel = jnp.einsum(
        "cmrtk,cmktq->cmrq", got_state, got_right, preferred_element_type=jnp.float32
    )
    gram_part = jnp.einsum("cmrq,cmrs->cmqs", panel, panel, precision=highest)
    gram_total = lax.psum(gram_part, "fsdp")
    ortho = orthonormal(panel, gram_total)
    ortho_low = ortho.astype(jnp.bfloat16)
    factor_part = jnp.einsum(
        "cmrtk,cmrq->cmktq", got_state, ortho_low, preferred_element_type=jnp.float32
    )
    factor = lax.psum(factor_part, "fsdp")
    mean_square = jnp.mean(factor * factor, axis=(2, 3))
    right_new = factor * lax.rsqrt(mean_square + epsilon)[:, :, None, None, :]
    update = jnp.einsum("cmrq,cmktq->cmrtk", ortho, factor, precision=highest)
    fresh = (got_state.astype(jnp.float32) - feedback * update).astype(jnp.bfloat16)
    state_out = fresh.reshape(CAP, fresh.shape[1], rows, groups * columns)
    left_out = ortho * scale
    returned = lax.all_to_all(right_new, "tensor", split_axis=3, concat_axis=3, tiled=True)
    right_out = jnp.einsum("edc,cmkdq->emkq", owner_table, returned, precision=highest)
    return (state_out, left_out, right_out)


MESH = pl.DeviceIdType.MESH
HIGHEST = lax.Precision.HIGHEST
VMEM_BYTES = 56 * 1024 * 1024


def greet(shards_f, groups):
    f = lax.axis_index("fsdp")
    z = lax.axis_index("tensor")
    barrier = pltpu.get_barrier_semaphore()
    for j in range(1, shards_f):
        pl.semaphore_signal(
            barrier, inc=1, device_id={"fsdp": lax.rem(f + j, shards_f), "tensor": z}, device_id_type=MESH
        )
    for j in range(1, groups):
        pl.semaphore_signal(
            barrier, inc=1, device_id={"fsdp": f, "tensor": lax.rem(z + j, groups)}, device_id_type=MESH
        )
    pl.semaphore_wait(barrier, shards_f - 1 + groups - 1)
    return f, z


def remote(src, dst, send_sem, recv_sem, f, z):
    return pltpu.make_async_remote_copy(
        src_ref=src,
        dst_ref=dst,
        send_sem=send_sem,
        recv_sem=recv_sem,
        device_id={"fsdp": f, "tensor": z},
        device_id_type=MESH,
    )


def inverse_factor(aug, mats, rank):
    block = 32
    wide = (mats, block, 2 * block)
    wide_row = lax.broadcasted_iota(jnp.int32, wide, 1)
    wide_col = lax.broadcasted_iota(jnp.int32, wide, 2)
    on_diagonal = wide_row == wide_col
    small = (mats, block, block)
    small_eye = (lax.broadcasted_iota(jnp.int32, small, 1) == lax.broadcasted_iota(jnp.int32, small, 2)).astype(jnp.float32)
    for start in range(0, rank, block):
        stop = start + block

        def eliminate(k, both):
            row = jnp.sum(jnp.where(wide_row == k, both, 0.0), axis=1, keepdims=True)
            column = jnp.sum(jnp.where(wide_col == k, both, 0.0), axis=2, keepdims=True)
            pivot = jnp.sum(jnp.where(wide_col[:, :1] == k, row, 0.0), axis=2, keepdims=True)
            ratio = jnp.where(wide_row[:, :, :1] > k, column * (1.0 / pivot), 0.0)
            return both - ratio * row

        both = jnp.concatenate([aug[:, start:stop, start:stop], small_eye], axis=2)
        both = lax.fori_loop(0, block, eliminate, both, unroll=4)
        diagonal = jnp.sum(jnp.where(on_diagonal, both, 0.0), axis=2, keepdims=True)
        inverse = both[:, :, block:] * lax.rsqrt(diagonal)
        for m in range(mats):
            top = jnp.dot(inverse[m], aug[m, start:stop, :], precision=HIGHEST, preferred_element_type=jnp.float32)
            aug[m, start:stop, :] = top
            if stop < rank:
                below = top[:, :rank].T[stop:]
                aug[m, stop:, :] -= jnp.dot(below, top, precision=HIGHEST, preferred_element_type=jnp.float32)


def step_kernel(
    shards_f, groups, kinds,
    own_ref, m_ref, g_ref, r_ref,
    got_out, low_out, fact_out, right_out,
    summed, sendbuf, got, pbuf, prelay, pjoin, pnear, pfar, pchunk,
    gram, gnear, gpair, ghalf, gchip, aug, wfull,
    obuf, fpart, fpair, fhalf, fchip, fchunk, fsend, lowbuf, sqbuf, sqrecv, rightbuf,
    p_send, p_recv, r_send, r_recv, x_send, x_recv, ga_send, ga_recv, gb_send, gb_recv,
    w_send, w_recv, o_send, o_recv, op_send, op_recv, fa_send, fa_recv, fb_send, fb_recv, fz_send, fz_recv,
    sq_send, sq_recv, low_send, low_recv, right_send, right_recv,
    s_send, first_recv, near_recv, second_recv, pass_send, pass_recv, out_sem,
):
    mats, rows, columns = m_ref.shape
    experts = mats // kinds
    slots = CAP * kinds
    rank = r_ref.shape[-1]
    units = 2 * mats // groups
    f, z = greet(shards_f, groups)
    core = lax.rem(f, 2)
    chip = f // 2
    chips = shards_f // 2
    pair = chip * 2 + 1 - core
    urows = rows // 2
    started = []

    def go(src, dst, send_sem, recv_sem, to_f, to_z):
        copy = remote(src, dst, send_sem, recv_sem, to_f, to_z)
        copy.start()
        started.append(copy)
        return copy

    def landed(dst, recv_sem):
        remote(dst, dst, recv_sem, recv_sem, f, z).wait_recv()

    near = z + 1 - 2 * lax.rem(z, 2)
    upper = z // 2
    inner = 2 - upper
    outer = 3 - 3 * upper
    far = 2 - 2 * upper
    is_inner = (z == 1) | (z == 2)
    is_outer = jnp.logical_not(is_inner)

    def relay(t, i, u):
        return remote(pbuf.at[u], prelay.at[t, i], r_send.at[t, i], r_recv.at[t, i], f, near)

    def across(t, i, d):
        return remote(pjoin.at[t, i], pfar.at[i], x_send.at[t, i], x_recv.at[i], f, d)

    for t, d in enumerate((outer, inner, near, z)):
        for i in range(units):
            u = d * units + i
            m = u // 2
            top = lax.rem(u, 2) * urows

            @pl.loop(0, urows // 128)
            def _(b):
                at = pl.ds(pl.multiple_of(top + b * 128, 128), 128)
                total = m_ref[m, at, :].astype(jnp.float32) + g_ref[m, at, :].astype(jnp.float32)
                low = total.astype(jnp.bfloat16)
                summed[m, at, :] = low
                pbuf[u, pl.ds(pl.multiple_of(b * 128, 128), 128), :] = jnp.dot(
                    low, r_ref[m], preferred_element_type=jnp.float32
                )

            if t < 2:
                @pl.when(is_outer)
                def _():
                    relay(t, i, u).start()

        if t == 2:
            go(pbuf.at[pl.ds(near * units, units)], pnear, p_send, p_recv, f, near)

    @pl.when(is_inner)
    def _():
        for t, d in enumerate((outer, inner)):
            for i in range(units):
                landed(prelay.at[t, i], r_recv.at[t, i])
                pjoin[t, i] = pbuf[d * units + i] + prelay[t, i]
                across(t, i, d).start()

    step = 128
    owner = [own_ref[e] for e in range(experts)]
    position = [sum(((owner[b] == owner[e]).astype(jnp.int32) for b in range(e)), jnp.int32(0)) for e in range(experts)]

    def taken(d, c):
        return sum((jnp.where((owner[e] == d) & (position[e] == c), e, 0) for e in range(experts)), jnp.int32(0))

    second = sum(
        (jnp.where((owner[e] // 2 == 1 - upper) & (position[e] == 1), e, 0) for e in range(experts)), jnp.int32(0)
    )
    picks = (second, taken(outer, 0), taken(inner, 0), taken(near, 0), taken(near, 1))
    for unit, expert in enumerate(picks):
        for k in range(kinds):
            @pl.loop(0, rows // step)
            def _(i):
                at = pl.ds(pl.multiple_of(i * step, step), step)
                sendbuf[unit, k, at, :] = summed[expert * kinds + k, at, :]
    here = pl.ds(pl.multiple_of(z * columns, columns), columns)
    for c in range(CAP):
        expert = taken(z, c)
        for k in range(kinds):
            @pl.loop(0, rows // step)
            def _(i):
                at = pl.ds(pl.multiple_of(i * step, step), step)
                got[c * kinds + k, at, here] = summed[expert * kinds + k, at, :]

    def place(c, source, k):
        return got.at[c * kinds + k, :, pl.ds(pl.multiple_of(source * columns, columns), columns)]

    def send(unit, c, recv, d, k):
        go(sendbuf.at[unit, k], place(c, z, k), s_send.at[unit, k], recv, f, d)

    def far_second(k):
        send(0, 1, second_recv.at[lax.rem(z, 2), k], inner, k)

    def far_outer(k):
        send(1, 0, first_recv.at[z, k], outer, k)

    def far_inner(k):
        send(2, 0, first_recv.at[z, k], inner, k)

    def near_first(k):
        send(3, 0, first_recv.at[z, k], near, k)

    def near_second(k):
        send(4, 1, near_recv.at[k], near, k)

    def hand_on(k):
        @pl.when(is_inner)
        def _():
            for i in range(2):
                block = place(1, far + i, k)
                landed(block, second_recv.at[i, k])
                remote(block, block, pass_send.at[i, k], pass_recv.at[i, k], f, near).start()

    odd = lax.rem(z, 2)
    landed(pnear, p_recv)
    for i in range(units):
        landed(pfar.at[i], x_recv.at[i])
        pchunk[i] = pbuf[z * units + i] + pnear[i] + pfar[i]

    def gram_of(i):
        panel = pchunk[i]
        return jnp.dot(panel.T, panel, precision=HIGHEST, preferred_element_type=jnp.float32)

    gram[2] = gram_of(2 - 2 * odd)
    shared = go(gram.at[2], gnear, ga_send.at[0], ga_recv.at[0], f, near)
    gram[0] = gram_of(odd) + gram_of(odd + 1)
    shared.wait_recv()
    gram[1] = gram[2] + gnear[...]
    far_second(0)
    near_second(0)
    far_second(1)
    near_second(1)
    near_first(0)
    near_first(1)
    far_outer(0)
    go(gram.at[1 - core], gpair, ga_send.at[1], ga_recv.at[1], pair, z).wait_recv()
    total = gram[core] + gpair[...]
    ghalf[...] = total
    for j in (2, 1, 3):
        go(
            ghalf, gchip.at[j - 1], gb_send.at[j - 1], gb_recv.at[j - 1],
            lax.rem(chip + j, chips) * 2 + core, z,
        )
    for j in range(1, chips):
        landed(gchip.at[j - 1], gb_recv.at[j - 1])
        total = total + gchip[j - 1]

    row_at = lax.broadcasted_iota(jnp.int32, (rank, rank), 0)
    col_at = lax.broadcasted_iota(jnp.int32, (rank, rank), 1)
    eye = (row_at == col_at).astype(jnp.float32)
    aug[0, :, :rank] = total + ridge_term * eye
    aug[0, :, rank:] = eye
    inverse_factor(aug, 1, rank)
    wfull[core] = aug[0, :, rank:]
    go(wfull.at[core], wfull.at[core], w_send, w_recv, pair, z)
    landed(wfull.at[1 - core], w_recv)

    for i, which in enumerate((odd, 0, 1 - odd)):
        ortho = jnp.dot(pchunk[i], wfull[which].T, precision=HIGHEST, preferred_element_type=jnp.float32)
        obuf[z * units + i] = ortho.astype(jnp.bfloat16)
    def chunk_of(source):
        return obuf.at[pl.ds(source * units, units)]

    def ortho_on(i):
        part = chunk_of(far + i)
        return remote(part, part, op_send.at[i], op_recv.at[i], f, near)

    go(chunk_of(z), chunk_of(z), o_send.at[0], o_recv.at[lax.rem(z, 2)], f, inner)
    go(chunk_of(z), chunk_of(z), o_send.at[1], o_recv.at[2], f, near)

    @pl.when(is_inner)
    def _():
        for i in range(2):
            landed(chunk_of(far + i), o_recv.at[i])
            ortho_on(i).start()

    landed(chunk_of(near), o_recv.at[2])

    @pl.when(is_outer)
    def _():
        for i in range(2):
            landed(chunk_of(far + i), op_recv.at[i])

    far_inner(0)
    hand_on(0)

    for m in range(mats):
        fpart[m] = jnp.dot(
            obuf[2 * m].T, summed[m, :urows], preferred_element_type=jnp.float32
        ) + jnp.dot(obuf[2 * m + 1].T, summed[m, urows:], preferred_element_type=jnp.float32)
        low_rows = rank // 2
        go(
            fpart.at[m, pl.ds(pl.multiple_of((1 - core) * low_rows, low_rows), low_rows), :],
            fpair.at[m], fa_send.at[m], fa_recv.at[m], pair, z,
        )
    piece = rank // shards_f
    own = pl.ds(pl.multiple_of(core * low_rows, low_rows), low_rows)
    for m in range(mats):
        landed(fpair.at[m], fa_recv.at[m])
        fhalf[m] = fpart[m, own, :] + fpair[m]
    for j in (2, 1, 3):
        other = lax.rem(chip + j, chips)
        go(
            fhalf.at[:, pl.ds(pl.multiple_of(other * piece, piece), piece), :],
            fchip.at[j - 1], fb_send.at[j - 1], fb_recv.at[j - 1], other * 2 + core, z,
        )
    total = fhalf[:, pl.ds(pl.multiple_of(chip * piece, piece), piece), :]
    for j in range(1, chips):
        landed(fchip.at[j - 1], fb_recv.at[j - 1])
        total = total + fchip[j - 1]
    square = total * total
    part_sum = square[:, :, :128]
    for lane in range(128, columns, 128):
        part_sum = part_sum + square[:, :, lane : lane + 128]
    sqbuf[...] = part_sum
    for j in (2, 3, 1):
        go(sqbuf, sqrecv.at[j - 1], sq_send.at[j - 1], sq_recv.at[j - 1], f, lax.rem(z + j, groups))
    fchunk[...] = total
    chunk = core * low_rows + chip * piece
    at = pl.ds(pl.multiple_of(chunk, piece), piece)
    for j in (2, 3, 1):
        d = lax.rem(z + j, groups)
        for c in range(CAP):
            expert = taken(d, c)
            for k in range(kinds):
                fsend[j - 1, c * kinds + k] = fchunk[expert * kinds + k].astype(jnp.bfloat16)
        go(fsend.at[j - 1], lowbuf.at[:, at, here], fz_send.at[j - 1], fz_recv.at[j - 1], f, d)
    hand_on(1)
    far_outer(1)
    far_inner(1)
    for c in range(CAP):
        expert = taken(z, c)
        for k in range(kinds):
            lowbuf[c * kinds + k, at, here] = fchunk[expert * kinds + k].astype(jnp.bfloat16)
    for j in range(1, groups):
        source = lax.rem(z + groups - j, groups)
        there = pl.ds(pl.multiple_of(source * columns, columns), columns)
        landed(lowbuf.at[:, at, there], fz_recv.at[j - 1])
    for j in (2, 1, 3):
        part = lowbuf.at[:, at, :]
        go(part, part, low_send.at[j - 1], low_recv.at[j - 1], lax.rem(chip + j, chips) * 2 + core, z)
    square = sqbuf[...]
    for j in range(1, groups):
        landed(sqrecv.at[j - 1], sq_recv.at[j - 1])
        square = square + sqrecv[j - 1]
    mean_square = jnp.sum(square, axis=2, keepdims=True) / (groups * columns)
    rightbuf[:, at, :] = fchunk[...] * lax.rsqrt(mean_square + epsilon)
    for j in (2, 1, 3):
        part = rightbuf.at[:, at, :]
        go(part, part, right_send.at[j - 1], right_recv.at[j - 1], lax.rem(chip + j, chips) * 2 + core, z)
    theirs = pl.ds(pl.multiple_of((1 - core) * low_rows, low_rows), low_rows)
    for buffer, sent, recv in ((lowbuf, low_send, low_recv), (rightbuf, right_send, right_recv)):
        for j in range(1, chips):
            start = core * low_rows + lax.rem(chip + chips - j, chips) * piece
            landed(buffer.at[:, pl.ds(pl.multiple_of(start, piece), piece), :], recv.at[j - 1])
        part = buffer.at[:, own, :]
        go(part, part, sent.at[chips - 1], recv.at[chips - 1], pair, z)
    for c in range(CAP):
        expert = taken(z, c)
        for k in range(kinds):
            low_out[c * kinds + k, :urows] = obuf[(expert * kinds + k) * 2]
            low_out[c * kinds + k, urows:] = obuf[(expert * kinds + k) * 2 + 1]

    kept = []

    def keep(c, source, k):
        there = pl.ds(pl.multiple_of(source * columns, columns), columns)
        copy = pltpu.make_async_copy(
            place(c, source, k), got_out.at[c * kinds + k, :, there], out_sem.at[len(kept)]
        )
        copy.start()
        kept.append(copy)

    for k in range(kinds):
        keep(0, z, k)
        keep(1, z, k)
    for k in range(kinds):
        landed(place(1, near, k), near_recv.at[k])
        keep(1, near, k)
    for k in range(kinds):
        for source in (near, far, far + 1):
            landed(place(0, source, k), first_recv.at[source, k])
            keep(0, source, k)

    @pl.when(is_inner)
    def _():
        for i in range(2):
            for k in range(kinds):
                block = place(1, far + i, k)
                remote(block, block, pass_send.at[i, k], pass_recv.at[i, k], f, near).wait_send()
            ortho_on(i).wait_send()
        for t, d in enumerate((outer, inner)):
            for i in range(units):
                across(t, i, d).wait_send()

    @pl.when(is_outer)
    def _():
        for t, d in enumerate((outer, inner)):
            for i in range(units):
                relay(t, i, d * units + i).wait_send()
        for i in range(2):
            for k in range(kinds):
                landed(place(1, far + i, k), pass_recv.at[i, k])

    for i in range(2):
        for k in range(kinds):
            keep(1, far + i, k)
    for buffer, recv in ((lowbuf, low_recv), (rightbuf, right_recv)):
        landed(buffer.at[:, theirs, :], recv.at[chips - 1])
    fact_out[...] = lowbuf[...]
    right_out[...] = rightbuf[...]
    for copy in started:
        copy.wait_send()
    for copy in kept:
        copy.wait()


def fresh_kernel(used_ref, got_ref, low_ref, fact_ref, state_ref, left_ref):
    m = pl.program_id(0)
    update = jnp.dot(low_ref[0], fact_ref[0], preferred_element_type=jnp.float32)
    fresh = got_ref[0].astype(jnp.float32) - feedback * update
    state_ref[0] = jnp.where(used_ref[m] > 0, fresh, 0.0).astype(jnp.bfloat16)
    left = low_ref[0].astype(jnp.float32) * math.sqrt(D)
    left_ref[0] = jnp.where(used_ref[m] > 0, left, 0.0)


def shards(momentum, gradient, right_in, owners):
    groups = lax.axis_size("tensor")
    shards_f = lax.axis_size("fsdp")
    experts, kinds, rows, columns = momentum.shape
    rank = right_in.shape[-1]
    hidden = groups * columns
    mats = CAP * kinds
    z = lax.axis_index("tensor")
    index_line = jnp.arange(experts, dtype=jnp.int32)
    same_owner = owners[:, None] == owners[None, :]
    earlier = index_line[None, :] < index_line[:, None]
    position = jnp.sum((same_owner & earlier).astype(jnp.int32), axis=1)
    slot = owners * CAP + position
    here = slot[:, None] == (z * CAP + jnp.arange(mats, dtype=jnp.int32) // kinds)[None, :]
    used = jnp.sum(here.astype(jnp.int32), axis=0)

    smem = pl.BlockSpec(memory_space=pltpu.SMEM)
    vmem = pl.BlockSpec(memory_space=pltpu.VMEM)
    hbm = pl.BlockSpec(memory_space=pl.ANY)
    f32, bf16 = jnp.float32, jnp.bfloat16
    shape = jax.ShapeDtypeStruct
    dma = pltpu.SemaphoreType.DMA
    chips = shards_f // 2
    every = experts * kinds
    units = 2 * every // groups
    piece = rank // shards_f
    near_z, near_c = groups - 1, chips - 1
    got, low, fact, right = pl.pallas_call(
        functools.partial(step_kernel, shards_f, groups, kinds),
        out_shape=(
            shape((mats, rows, hidden), bf16),
            shape((mats, rows, rank), bf16),
            shape((mats, rank, hidden), bf16),
            shape((every, rank, columns), f32),
        ),
        in_specs=[smem, vmem, vmem, vmem],
        out_specs=(hbm, vmem, vmem, vmem),
        scratch_shapes=[
            pltpu.VMEM((every, rows, columns), bf16),
            pltpu.VMEM((5, kinds, rows, columns), bf16),
            pltpu.VMEM((mats, rows, hidden), bf16),
            pltpu.VMEM((2 * every, rows // 2, rank), f32),
            pltpu.VMEM((2, units, rows // 2, rank), f32),
            pltpu.VMEM((2, units, rows // 2, rank), f32),
            pltpu.VMEM((units, rows // 2, rank), f32),
            pltpu.VMEM((units, rows // 2, rank), f32),
            pltpu.VMEM((units, rows // 2, rank), f32),
            pltpu.VMEM((3, rank, rank), f32),
            pltpu.VMEM((rank, rank), f32),
            pltpu.VMEM((rank, rank), f32),
            pltpu.VMEM((rank, rank), f32),
            pltpu.VMEM((near_c, rank, rank), f32),
            pltpu.VMEM((1, rank, 2 * rank), f32),
            pltpu.VMEM((2, rank, rank), f32),
            pltpu.VMEM((2 * every, rows // 2, rank), bf16),
            pltpu.VMEM((every, rank, columns), f32),
            pltpu.VMEM((every, rank // 2, columns), f32),
            pltpu.VMEM((every, rank // 2, columns), f32),
            pltpu.VMEM((near_c, every, piece, columns), f32),
            pltpu.VMEM((every, piece, columns), f32),
            pltpu.VMEM((near_z, mats, piece, columns), bf16),
            pltpu.VMEM((mats, rank, hidden), bf16),
            pltpu.VMEM((every, piece, 128), f32),
            pltpu.VMEM((near_z, every, piece, 128), f32),
            pltpu.VMEM((every, rank, columns), f32),
            dma, dma,
            dma((2, units)), dma((2, units)),
            dma((2, units)), dma((units,)),
            dma((2,)), dma((2,)),
            dma((near_c,)), dma((near_c,)),
            dma, dma,
            dma((2,)), dma((3,)), dma((2,)), dma((2,)),
            dma((every,)), dma((every,)),
            dma((near_c,)), dma((near_c,)),
            dma((near_z,)), dma((near_z,)),
            dma((near_z,)), dma((near_z,)),
            dma((chips,)), dma((chips,)),
            dma((chips,)), dma((chips,)),
            dma((5, kinds)), dma((groups, kinds)), dma((kinds,)),
            dma((2, kinds)), dma((2, kinds)), dma((2, kinds)), dma((groups * mats,)),
        ],
        compiler_params=pltpu.CompilerParams(
            collective_id=0, has_side_effects=True, vmem_limit_bytes=VMEM_BYTES
        ),
        name="step",
    )(
        owners,
        momentum.reshape(every, rows, columns),
        gradient.reshape(every, rows, columns),
        right_in.reshape(every, columns, rank),
    )

    band = min(rows, 256)
    state, left = pl.pallas_call(
        fresh_kernel,
        grid=(mats, rows // band),
        out_shape=(shape((mats, rows, hidden), bf16), shape((mats, rows, rank), f32)),
        in_specs=[
            smem,
            pl.BlockSpec((1, band, hidden), lambda m, i: (m, i, 0)),
            pl.BlockSpec((1, band, rank), lambda m, i: (m, i, 0)),
            pl.BlockSpec((1, rank, hidden), lambda m, i: (m, 0, 0)),
        ],
        out_specs=(
            pl.BlockSpec((1, band, hidden), lambda m, i: (m, i, 0)),
            pl.BlockSpec((1, band, rank), lambda m, i: (m, i, 0)),
        ),
        name="fresh",
    )(used, got, low, fact)
    right_new = jnp.swapaxes(right, 1, 2).reshape(experts, kinds, columns, rank)
    return (
        state.reshape(CAP, kinds, rows, hidden),
        left.reshape(CAP, kinds, rows, rank),
        right_new,
    )


def solution(mesh):
    fits = mesh.shape["fsdp"] == 8 and mesh.shape["tensor"] == 4
    return jax.shard_map(
        shards if fits else general_shards,
        mesh=mesh,
        in_specs=(
            P(None, None, "fsdp", "tensor"),
            P(None, None, "fsdp", "tensor"),
            P(None, None, "tensor", None),
            P(),
        ),
        out_specs=(
            P("tensor", None, "fsdp", None),
            P("tensor", None, "fsdp", None),
            P(None, None, "tensor", None),
        ),
        check_vma=False,
    )
```

```python
import functools
import math

import jax
import jax.numpy as jnp
from jax import lax
from jax.experimental import pallas as pl
from jax.experimental.pallas import tpu as pltpu
from jax.sharding import PartitionSpec as P

D = 4096
CAP = 2


ridge_term = 0.001
feedback = 0.1
epsilon = 1e-06


def orthonormal(panel, gram_total):
    eye_matrix = jnp.eye(gram_total.shape[-1], dtype=jnp.float32)
    lower_factor = jnp.linalg.cholesky(gram_total + ridge_term * eye_matrix)
    solved = jax.scipy.linalg.solve_triangular(
        lower_factor, jnp.swapaxes(panel, -1, -2), lower=True
    )
    return jnp.swapaxes(solved, -1, -2)


def slot_table(owners, groups, capacity):
    count = owners.shape[0]
    index_line = jnp.arange(count, dtype=jnp.int32)
    same_owner = owners[:, None] == owners[None, :]
    earlier = index_line[None, :] < index_line[:, None]
    position = jnp.sum((same_owner & earlier).astype(jnp.int32), axis=1)
    owner_hit = owners[:, None, None] == jnp.arange(groups, dtype=jnp.int32)[None, :, None]
    slot_hit = position[:, None, None] == jnp.arange(capacity, dtype=jnp.int32)[None, None, :]
    return (owner_hit & slot_hit).astype(jnp.float32)


def general_shards(momentum, gradient, right_in, owners):
    highest = lax.Precision.HIGHEST
    groups = lax.axis_size("tensor")
    rows = momentum.shape[2]
    columns = momentum.shape[3]
    owner_table = slot_table(owners, groups, CAP)
    table_low = owner_table.astype(jnp.bfloat16)
    summed = (momentum.astype(jnp.float32) + gradient.astype(jnp.float32)).astype(jnp.bfloat16)
    scale = math.sqrt(D)
    send_state = jnp.einsum(
        "edc,emrk->cmrdk", table_low, summed, preferred_element_type=jnp.float32
    ).astype(jnp.bfloat16)
    send_right = jnp.einsum(
        "edc,emkq->cmkdq", table_low, right_in, preferred_element_type=jnp.float32
    ).astype(jnp.bfloat16)
    got_state, got_right = (
        lax.all_to_all(send_state, "tensor", split_axis=3, concat_axis=3, tiled=True),
        lax.all_to_all(send_right, "tensor", split_axis=3, concat_axis=3, tiled=True),
    )
    panel = jnp.einsum(
        "cmrtk,cmktq->cmrq", got_state, got_right, preferred_element_type=jnp.float32
    )
    gram_part = jnp.einsum("cmrq,cmrs->cmqs", panel, panel, precision=highest)
    gram_total = lax.psum(gram_part, "fsdp")
    ortho = orthonormal(panel, gram_total)
    ortho_low = ortho.astype(jnp.bfloat16)
    factor_part = jnp.einsum(
        "cmrtk,cmrq->cmktq", got_state, ortho_low, preferred_element_type=jnp.float32
    )
    factor = lax.psum(factor_part, "fsdp")
    mean_square = jnp.mean(factor * factor, axis=(2, 3))
    right_new = factor * lax.rsqrt(mean_square + epsilon)[:, :, None, None, :]
    update = jnp.einsum("cmrq,cmktq->cmrtk", ortho, factor, precision=highest)
    fresh = (got_state.astype(jnp.float32) - feedback * update).astype(jnp.bfloat16)
    state_out = fresh.reshape(CAP, fresh.shape[1], rows, groups * columns)
    left_out = ortho * scale
    returned = lax.all_to_all(right_new, "tensor", split_axis=3, concat_axis=3, tiled=True)
    right_out = jnp.einsum("edc,cmkdq->emkq", owner_table, returned, precision=highest)
    return (state_out, left_out, right_out)


MESH = pl.DeviceIdType.MESH
HIGHEST = lax.Precision.HIGHEST
VMEM_BYTES = 56 * 1024 * 1024


def greet(shards_f, groups):
    f = lax.axis_index("fsdp")
    z = lax.axis_index("tensor")
    barrier = pltpu.get_barrier_semaphore()
    for j in range(1, shards_f):
        pl.semaphore_signal(
            barrier, inc=1, device_id={"fsdp": lax.rem(f + j, shards_f), "tensor": z}, device_id_type=MESH
        )
    for j in range(1, groups):
        pl.semaphore_signal(
            barrier, inc=1, device_id={"fsdp": f, "tensor": lax.rem(z + j, groups)}, device_id_type=MESH
        )
    pl.semaphore_wait(barrier, shards_f - 1 + groups - 1)
    return f, z


def remote(src, dst, send_sem, recv_sem, f, z):
    return pltpu.make_async_remote_copy(
        src_ref=src,
        dst_ref=dst,
        send_sem=send_sem,
        recv_sem=recv_sem,
        device_id={"fsdp": f, "tensor": z},
        device_id_type=MESH,
    )


def inverse_factor(aug, mats, rank):
    block = 32
    wide = (mats, block, 2 * block)
    wide_row = lax.broadcasted_iota(jnp.int32, wide, 1)
    wide_col = lax.broadcasted_iota(jnp.int32, wide, 2)
    on_diagonal = wide_row == wide_col
    small = (mats, block, block)
    small_eye = (lax.broadcasted_iota(jnp.int32, small, 1) == lax.broadcasted_iota(jnp.int32, small, 2)).astype(jnp.float32)
    for start in range(0, rank, block):
        stop = start + block

        def eliminate(k, both):
            row = jnp.sum(jnp.where(wide_row == k, both, 0.0), axis=1, keepdims=True)
            column = jnp.sum(jnp.where(wide_col == k, both, 0.0), axis=2, keepdims=True)
            pivot = jnp.sum(jnp.where(wide_col[:, :1] == k, row, 0.0), axis=2, keepdims=True)
            ratio = jnp.where(wide_row[:, :, :1] > k, column * (1.0 / pivot), 0.0)
            return both - ratio * row

        both = jnp.concatenate([aug[:, start:stop, start:stop], small_eye], axis=2)
        both = lax.fori_loop(0, block, eliminate, both, unroll=4)
        diagonal = jnp.sum(jnp.where(on_diagonal, both, 0.0), axis=2, keepdims=True)
        inverse = both[:, :, block:] * lax.rsqrt(diagonal)
        for m in range(mats):
            top = jnp.dot(inverse[m], aug[m, start:stop, :], precision=HIGHEST, preferred_element_type=jnp.float32)
            aug[m, start:stop, :] = top
            if stop < rank:
                below = top[:, :rank].T[stop:]
                aug[m, stop:, :] -= jnp.dot(below, top, precision=HIGHEST, preferred_element_type=jnp.float32)


def step_kernel(
    shards_f, groups, kinds,
    own_ref, m_ref, g_ref, r_ref,
    state_out, left_out, right_out,
    summed, sendbuf, got, pbuf, prelay, pjoin, pnear, pfar, pchunk,
    gram, gnear, gpair, ghalf, gchip, aug, wfull,
    obuf, fpart, fpair, fhalf, fchip, fchunk, fsend, lowbuf, sqbuf, sqrecv, rightbuf,
    p_send, p_recv, r_send, r_recv, x_send, x_recv, ga_send, ga_recv, gb_send, gb_recv,
    w_send, w_recv, o_send, o_recv, op_send, op_recv, fa_send, fa_recv, fb_send, fb_recv, fz_send, fz_recv,
    sq_send, sq_recv, low_send, low_recv, right_send, right_recv,
    s_send, first_recv, near_recv, second_recv, pass_send, pass_recv, out_sem,
):
    mats, rows, columns = m_ref.shape
    experts = mats // kinds
    slots = CAP * kinds
    rank = r_ref.shape[-1]
    units = 2 * mats // groups
    f, z = greet(shards_f, groups)
    core = lax.rem(f, 2)
    chip = f // 2
    chips = shards_f // 2
    pair = chip * 2 + 1 - core
    urows = rows // 2
    started = []

    def go(src, dst, send_sem, recv_sem, to_f, to_z):
        copy = remote(src, dst, send_sem, recv_sem, to_f, to_z)
        copy.start()
        started.append(copy)
        return copy

    def landed(dst, recv_sem):
        remote(dst, dst, recv_sem, recv_sem, f, z).wait_recv()

    near = z + 1 - 2 * lax.rem(z, 2)
    upper = z // 2
    inner = 2 - upper
    outer = 3 - 3 * upper
    far = 2 - 2 * upper
    is_inner = (z == 1) | (z == 2)
    is_outer = jnp.logical_not(is_inner)

    def relay(t, i, u):
        return remote(pbuf.at[u], prelay.at[t, i], r_send.at[t, i], r_recv.at[t, i], f, near)

    def across(t, i, d):
        return remote(pjoin.at[t, i], pfar.at[i], x_send.at[t, i], x_recv.at[i], f, d)

    for t, d in enumerate((outer, inner, near, z)):
        for i in range(units):
            u = d * units + i
            m = u // 2
            top = lax.rem(u, 2) * urows

            @pl.loop(0, urows // 128)
            def _(b):
                at = pl.ds(pl.multiple_of(top + b * 128, 128), 128)
                total = m_ref[m, at, :].astype(jnp.float32) + g_ref[m, at, :].astype(jnp.float32)
                low = total.astype(jnp.bfloat16)
                summed[m, at, :] = low
                pbuf[u, pl.ds(pl.multiple_of(b * 128, 128), 128), :] = jnp.dot(
                    low, r_ref[m], preferred_element_type=jnp.float32
                )

            if t < 2:
                @pl.when(is_outer)
                def _():
                    relay(t, i, u).start()

        if t == 2:
            go(pbuf.at[pl.ds(near * units, units)], pnear, p_send, p_recv, f, near)

    @pl.when(is_inner)
    def _():
        for t, d in enumerate((outer, inner)):
            for i in range(units):
                landed(prelay.at[t, i], r_recv.at[t, i])
                pjoin[t, i] = pbuf[d * units + i] + prelay[t, i]
                across(t, i, d).start()

    step = 128
    owner = [own_ref[e] for e in range(experts)]
    position = [sum(((owner[b] == owner[e]).astype(jnp.int32) for b in range(e)), jnp.int32(0)) for e in range(experts)]

    def taken(d, c):
        return sum((jnp.where((owner[e] == d) & (position[e] == c), e, 0) for e in range(experts)), jnp.int32(0))

    second = sum(
        (jnp.where((owner[e] // 2 == 1 - upper) & (position[e] == 1), e, 0) for e in range(experts)), jnp.int32(0)
    )
    picks = (second, taken(outer, 0), taken(inner, 0), taken(near, 0), taken(near, 1))
    for unit, expert in enumerate(picks):
        for k in range(kinds):
            @pl.loop(0, rows // step)
            def _(i):
                at = pl.ds(pl.multiple_of(i * step, step), step)
                sendbuf[unit, k, at, :] = summed[expert * kinds + k, at, :]
    here = pl.ds(pl.multiple_of(z * columns, columns), columns)
    for c in range(CAP):
        expert = taken(z, c)
        for k in range(kinds):
            @pl.loop(0, rows // step)
            def _(i):
                at = pl.ds(pl.multiple_of(i * step, step), step)
                got[c * kinds + k, at, here] = summed[expert * kinds + k, at, :]

    def place(c, source, k):
        return got.at[c * kinds + k, :, pl.ds(pl.multiple_of(source * columns, columns), columns)]

    def send(unit, c, recv, d, k):
        go(sendbuf.at[unit, k], place(c, z, k), s_send.at[unit, k], recv, f, d)

    def far_second(k):
        send(0, 1, second_recv.at[lax.rem(z, 2), k], inner, k)

    def far_outer(k):
        send(1, 0, first_recv.at[z, k], outer, k)

    def far_inner(k):
        send(2, 0, first_recv.at[z, k], inner, k)

    def near_first(k):
        send(3, 0, first_recv.at[z, k], near, k)

    def near_second(k):
        send(4, 1, near_recv.at[k], near, k)

    def hand_on(k):
        @pl.when(is_inner)
        def _():
            for i in range(2):
                block = place(1, far + i, k)
                landed(block, second_recv.at[i, k])
                remote(block, block, pass_send.at[i, k], pass_recv.at[i, k], f, near).start()

    odd = lax.rem(z, 2)
    landed(pnear, p_recv)
    for i in range(units):
        landed(pfar.at[i], x_recv.at[i])
        pchunk[i] = pbuf[z * units + i] + pnear[i] + pfar[i]

    def gram_of(i):
        panel = pchunk[i]
        return jnp.dot(panel.T, panel, precision=HIGHEST, preferred_element_type=jnp.float32)

    gram[2] = gram_of(2 - 2 * odd)
    shared = go(gram.at[2], gnear, ga_send.at[0], ga_recv.at[0], f, near)
    gram[0] = gram_of(odd) + gram_of(odd + 1)
    shared.wait_recv()
    gram[1] = gram[2] + gnear[...]
    far_second(0)
    near_second(0)
    far_second(1)
    near_second(1)
    near_first(0)
    near_first(1)
    far_outer(0)
    go(gram.at[1 - core], gpair, ga_send.at[1], ga_recv.at[1], pair, z).wait_recv()
    total = gram[core] + gpair[...]
    ghalf[...] = total
    for j in (2, 1, 3):
        go(
            ghalf, gchip.at[j - 1], gb_send.at[j - 1], gb_recv.at[j - 1],
            lax.rem(chip + j, chips) * 2 + core, z,
        )
    for j in range(1, chips):
        landed(gchip.at[j - 1], gb_recv.at[j - 1])
        total = total + gchip[j - 1]

    row_at = lax.broadcasted_iota(jnp.int32, (rank, rank), 0)
    col_at = lax.broadcasted_iota(jnp.int32, (rank, rank), 1)
    eye = (row_at == col_at).astype(jnp.float32)
    aug[0, :, :rank] = total + ridge_term * eye
    aug[0, :, rank:] = eye
    inverse_factor(aug, 1, rank)
    wfull[core] = aug[0, :, rank:]
    go(wfull.at[core], wfull.at[core], w_send, w_recv, pair, z)
    landed(wfull.at[1 - core], w_recv)

    for i, which in enumerate((odd, 0, 1 - odd)):
        ortho = jnp.dot(pchunk[i], wfull[which].T, precision=HIGHEST, preferred_element_type=jnp.float32)
        obuf[z * units + i] = ortho.astype(jnp.bfloat16)
    def chunk_of(source):
        return obuf.at[pl.ds(source * units, units)]

    def ortho_on(i):
        part = chunk_of(far + i)
        return remote(part, part, op_send.at[i], op_recv.at[i], f, near)

    go(chunk_of(z), chunk_of(z), o_send.at[0], o_recv.at[lax.rem(z, 2)], f, inner)
    go(chunk_of(z), chunk_of(z), o_send.at[1], o_recv.at[2], f, near)

    @pl.when(is_inner)
    def _():
        for i in range(2):
            landed(chunk_of(far + i), o_recv.at[i])
            ortho_on(i).start()

    landed(chunk_of(near), o_recv.at[2])

    @pl.when(is_outer)
    def _():
        for i in range(2):
            landed(chunk_of(far + i), op_recv.at[i])

    far_inner(0)
    hand_on(0)

    for m in range(mats):
        fpart[m] = jnp.dot(
            obuf[2 * m].T, summed[m, :urows], preferred_element_type=jnp.float32
        ) + jnp.dot(obuf[2 * m + 1].T, summed[m, urows:], preferred_element_type=jnp.float32)
        low_rows = rank // 2
        go(
            fpart.at[m, pl.ds(pl.multiple_of((1 - core) * low_rows, low_rows), low_rows), :],
            fpair.at[m], fa_send.at[m], fa_recv.at[m], pair, z,
        )
    piece = rank // shards_f
    own = pl.ds(pl.multiple_of(core * low_rows, low_rows), low_rows)
    for m in range(mats):
        landed(fpair.at[m], fa_recv.at[m])
        fhalf[m] = fpart[m, own, :] + fpair[m]
    for j in (2, 1, 3):
        other = lax.rem(chip + j, chips)
        go(
            fhalf.at[:, pl.ds(pl.multiple_of(other * piece, piece), piece), :],
            fchip.at[j - 1], fb_send.at[j - 1], fb_recv.at[j - 1], other * 2 + core, z,
        )
    total = fhalf[:, pl.ds(pl.multiple_of(chip * piece, piece), piece), :]
    for j in range(1, chips):
        landed(fchip.at[j - 1], fb_recv.at[j - 1])
        total = total + fchip[j - 1]
    square = total * total
    part_sum = square[:, :, :128]
    for lane in range(128, columns, 128):
        part_sum = part_sum + square[:, :, lane : lane + 128]
    sqbuf[...] = part_sum
    for j in (2, 3, 1):
        go(sqbuf, sqrecv.at[j - 1], sq_send.at[j - 1], sq_recv.at[j - 1], f, lax.rem(z + j, groups))
    fchunk[...] = total
    chunk = core * low_rows + chip * piece
    at = pl.ds(pl.multiple_of(chunk, piece), piece)
    for j in (2, 3, 1):
        d = lax.rem(z + j, groups)
        for c in range(CAP):
            expert = taken(d, c)
            for k in range(kinds):
                fsend[j - 1, c * kinds + k] = fchunk[expert * kinds + k].astype(jnp.bfloat16)
        go(fsend.at[j - 1], lowbuf.at[:, at, here], fz_send.at[j - 1], fz_recv.at[j - 1], f, d)
    hand_on(1)
    far_outer(1)
    far_inner(1)
    for c in range(CAP):
        expert = taken(z, c)
        for k in range(kinds):
            lowbuf[c * kinds + k, at, here] = fchunk[expert * kinds + k].astype(jnp.bfloat16)
    for j in range(1, groups):
        source = lax.rem(z + groups - j, groups)
        there = pl.ds(pl.multiple_of(source * columns, columns), columns)
        landed(lowbuf.at[:, at, there], fz_recv.at[j - 1])
    for j in (2, 1, 3):
        part = lowbuf.at[:, at, :]
        go(part, part, low_send.at[j - 1], low_recv.at[j - 1], lax.rem(chip + j, chips) * 2 + core, z)
    square = sqbuf[...]
    for j in range(1, groups):
        landed(sqrecv.at[j - 1], sq_recv.at[j - 1])
        square = square + sqrecv[j - 1]
    mean_square = jnp.sum(square, axis=2, keepdims=True) / (groups * columns)
    rightbuf[:, at, :] = fchunk[...] * lax.rsqrt(mean_square + epsilon)
    for j in (2, 1, 3):
        part = rightbuf.at[:, at, :]
        go(part, part, right_send.at[j - 1], right_recv.at[j - 1], lax.rem(chip + j, chips) * 2 + core, z)
    theirs = pl.ds(pl.multiple_of((1 - core) * low_rows, low_rows), low_rows)
    for buffer, sent, recv in ((lowbuf, low_send, low_recv), (rightbuf, right_send, right_recv)):
        for j in range(1, chips):
            start = core * low_rows + lax.rem(chip + chips - j, chips) * piece
            landed(buffer.at[:, pl.ds(pl.multiple_of(start, piece), piece), :], recv.at[j - 1])
        part = buffer.at[:, own, :]
        go(part, part, sent.at[chips - 1], recv.at[chips - 1], pair, z)
    def present(c):
        return sum(((owner[e] == z) & (position[e] == c)).astype(jnp.int32) for e in range(experts)) > 0

    for c in range(CAP):
        expert = taken(z, c)
        for k in range(kinds):
            for h in range(2):
                left = obuf[(expert * kinds + k) * 2 + h].astype(jnp.float32) * math.sqrt(D)
                left_out[c * kinds + k, h * urows : (h + 1) * urows] = jnp.where(present(c), left, 0.0)

    landed(lowbuf.at[:, theirs, :], low_recv.at[chips - 1])
    kept = []

    def keep(c, source, k):
        m = c * kinds + k
        there = pl.ds(pl.multiple_of(source * columns, columns), columns)
        expert = taken(z, c)
        used = present(c)
        for h in range(2):
            @pl.loop(0, urows // 128)
            def _(b):
                at = pl.ds(pl.multiple_of(h * urows + b * 128, 128), 128)
                low = obuf[(expert * kinds + k) * 2 + h, pl.ds(pl.multiple_of(b * 128, 128), 128), :]
                update = jnp.dot(low, lowbuf[m, :, there], preferred_element_type=jnp.float32)
                fresh = got[m, at, there].astype(jnp.float32) - feedback * update
                got[m, at, there] = jnp.where(used, fresh, 0.0).astype(jnp.bfloat16)
        copy = pltpu.make_async_copy(place(c, source, k), state_out.at[m, :, there], out_sem.at[len(kept)])
        copy.start()
        kept.append(copy)

    for c in range(CAP):
        for k in range(kinds):
            keep(c, z, k)
    landed(rightbuf.at[:, theirs, :], right_recv.at[chips - 1])
    right_out[...] = rightbuf[...]
    for k in range(kinds):
        landed(place(1, near, k), near_recv.at[k])
        keep(1, near, k)
    for k in range(kinds):
        landed(place(0, near, k), first_recv.at[near, k])
        keep(0, near, k)
    for k in range(kinds):
        for i in range(2):
            landed(place(0, far + i, k), first_recv.at[far + i, k])
            keep(0, far + i, k)

        @pl.when(is_inner)
        def _():
            for i in range(2):
                block = place(1, far + i, k)
                remote(block, block, pass_send.at[i, k], pass_recv.at[i, k], f, near).wait_send()

        @pl.when(is_outer)
        def _():
            for i in range(2):
                landed(place(1, far + i, k), pass_recv.at[i, k])

        for i in range(2):
            keep(1, far + i, k)

    @pl.when(is_inner)
    def _():
        for i in range(2):
            ortho_on(i).wait_send()
        for t, d in enumerate((outer, inner)):
            for i in range(units):
                across(t, i, d).wait_send()

    @pl.when(is_outer)
    def _():
        for t, d in enumerate((outer, inner)):
            for i in range(units):
                relay(t, i, d * units + i).wait_send()

    for copy in started:
        copy.wait_send()
    for copy in kept:
        copy.wait()


def shards(momentum, gradient, right_in, owners):
    groups = lax.axis_size("tensor")
    shards_f = lax.axis_size("fsdp")
    experts, kinds, rows, columns = momentum.shape
    rank = right_in.shape[-1]
    hidden = groups * columns
    mats = CAP * kinds
    smem = pl.BlockSpec(memory_space=pltpu.SMEM)
    vmem = pl.BlockSpec(memory_space=pltpu.VMEM)
    hbm = pl.BlockSpec(memory_space=pl.ANY)
    f32, bf16 = jnp.float32, jnp.bfloat16
    shape = jax.ShapeDtypeStruct
    dma = pltpu.SemaphoreType.DMA
    chips = shards_f // 2
    every = experts * kinds
    units = 2 * every // groups
    piece = rank // shards_f
    near_z, near_c = groups - 1, chips - 1
    state, left, right = pl.pallas_call(
        functools.partial(step_kernel, shards_f, groups, kinds),
        out_shape=(
            shape((mats, rows, hidden), bf16),
            shape((mats, rows, rank), f32),
            shape((every, rank, columns), f32),
        ),
        in_specs=[smem, vmem, vmem, vmem],
        out_specs=(hbm, vmem, vmem),
        scratch_shapes=[
            pltpu.VMEM((every, rows, columns), bf16),
            pltpu.VMEM((5, kinds, rows, columns), bf16),
            pltpu.VMEM((mats, rows, hidden), bf16),
            pltpu.VMEM((2 * every, rows // 2, rank), f32),
            pltpu.VMEM((2, units, rows // 2, rank), f32),
            pltpu.VMEM((2, units, rows // 2, rank), f32),
            pltpu.VMEM((units, rows // 2, rank), f32),
            pltpu.VMEM((units, rows // 2, rank), f32),
            pltpu.VMEM((units, rows // 2, rank), f32),
            pltpu.VMEM((3, rank, rank), f32),
            pltpu.VMEM((rank, rank), f32),
            pltpu.VMEM((rank, rank), f32),
            pltpu.VMEM((rank, rank), f32),
            pltpu.VMEM((near_c, rank, rank), f32),
            pltpu.VMEM((1, rank, 2 * rank), f32),
            pltpu.VMEM((2, rank, rank), f32),
            pltpu.VMEM((2 * every, rows // 2, rank), bf16),
            pltpu.VMEM((every, rank, columns), f32),
            pltpu.VMEM((every, rank // 2, columns), f32),
            pltpu.VMEM((every, rank // 2, columns), f32),
            pltpu.VMEM((near_c, every, piece, columns), f32),
            pltpu.VMEM((every, piece, columns), f32),
            pltpu.VMEM((near_z, mats, piece, columns), bf16),
            pltpu.VMEM((mats, rank, hidden), bf16),
            pltpu.VMEM((every, piece, 128), f32),
            pltpu.VMEM((near_z, every, piece, 128), f32),
            pltpu.VMEM((every, rank, columns), f32),
            dma, dma,
            dma((2, units)), dma((2, units)),
            dma((2, units)), dma((units,)),
            dma((2,)), dma((2,)),
            dma((near_c,)), dma((near_c,)),
            dma, dma,
            dma((2,)), dma((3,)), dma((2,)), dma((2,)),
            dma((every,)), dma((every,)),
            dma((near_c,)), dma((near_c,)),
            dma((near_z,)), dma((near_z,)),
            dma((near_z,)), dma((near_z,)),
            dma((chips,)), dma((chips,)),
            dma((chips,)), dma((chips,)),
            dma((5, kinds)), dma((groups, kinds)), dma((kinds,)),
            dma((2, kinds)), dma((2, kinds)), dma((2, kinds)), dma((groups * mats,)),
        ],
        compiler_params=pltpu.CompilerParams(
            collective_id=0, has_side_effects=True, vmem_limit_bytes=VMEM_BYTES
        ),
        name="step",
    )(
        owners,
        momentum.reshape(every, rows, columns),
        gradient.reshape(every, rows, columns),
        right_in.reshape(every, columns, rank),
    )

    right_new = jnp.swapaxes(right, 1, 2).reshape(experts, kinds, columns, rank)
    return (
        state.reshape(CAP, kinds, rows, hidden),
        left.reshape(CAP, kinds, rows, rank),
        right_new,
    )


def solution(mesh):
    fits = mesh.shape["fsdp"] == 8 and mesh.shape["tensor"] == 4
    return jax.shard_map(
        shards if fits else general_shards,
        mesh=mesh,
        in_specs=(
            P(None, None, "fsdp", "tensor"),
            P(None, None, "fsdp", "tensor"),
            P(None, None, "tensor", None),
            P(),
        ),
        out_specs=(
            P("tensor", None, "fsdp", None),
            P("tensor", None, "fsdp", None),
            P(None, None, "tensor", None),
        ),
        check_vma=False,
    )
```

```python
import functools
import math

import jax
import jax.numpy as jnp
from jax import lax
from jax.experimental import pallas as pl
from jax.experimental.pallas import tpu as pltpu
from jax.sharding import PartitionSpec as P

D = 4096
CAP = 2


ridge_term = 0.001
feedback = 0.1
epsilon = 1e-06


def orthonormal(panel, gram_total):
    eye_matrix = jnp.eye(gram_total.shape[-1], dtype=jnp.float32)
    lower_factor = jnp.linalg.cholesky(gram_total + ridge_term * eye_matrix)
    solved = jax.scipy.linalg.solve_triangular(
        lower_factor, jnp.swapaxes(panel, -1, -2), lower=True
    )
    return jnp.swapaxes(solved, -1, -2)


def slot_table(owners, groups, capacity):
    count = owners.shape[0]
    index_line = jnp.arange(count, dtype=jnp.int32)
    same_owner = owners[:, None] == owners[None, :]
    earlier = index_line[None, :] < index_line[:, None]
    position = jnp.sum((same_owner & earlier).astype(jnp.int32), axis=1)
    owner_hit = owners[:, None, None] == jnp.arange(groups, dtype=jnp.int32)[None, :, None]
    slot_hit = position[:, None, None] == jnp.arange(capacity, dtype=jnp.int32)[None, None, :]
    return (owner_hit & slot_hit).astype(jnp.float32)


def general_shards(momentum, gradient, right_in, owners):
    highest = lax.Precision.HIGHEST
    groups = lax.axis_size("tensor")
    rows = momentum.shape[2]
    columns = momentum.shape[3]
    owner_table = slot_table(owners, groups, CAP)
    table_low = owner_table.astype(jnp.bfloat16)
    summed = (momentum.astype(jnp.float32) + gradient.astype(jnp.float32)).astype(jnp.bfloat16)
    scale = math.sqrt(D)
    send_state = jnp.einsum(
        "edc,emrk->cmrdk", table_low, summed, preferred_element_type=jnp.float32
    ).astype(jnp.bfloat16)
    send_right = jnp.einsum(
        "edc,emkq->cmkdq", table_low, right_in, preferred_element_type=jnp.float32
    ).astype(jnp.bfloat16)
    got_state, got_right = (
        lax.all_to_all(send_state, "tensor", split_axis=3, concat_axis=3, tiled=True),
        lax.all_to_all(send_right, "tensor", split_axis=3, concat_axis=3, tiled=True),
    )
    panel = jnp.einsum(
        "cmrtk,cmktq->cmrq", got_state, got_right, preferred_element_type=jnp.float32
    )
    gram_part = jnp.einsum("cmrq,cmrs->cmqs", panel, panel, precision=highest)
    gram_total = lax.psum(gram_part, "fsdp")
    ortho = orthonormal(panel, gram_total)
    ortho_low = ortho.astype(jnp.bfloat16)
    factor_part = jnp.einsum(
        "cmrtk,cmrq->cmktq", got_state, ortho_low, preferred_element_type=jnp.float32
    )
    factor = lax.psum(factor_part, "fsdp")
    mean_square = jnp.mean(factor * factor, axis=(2, 3))
    right_new = factor * lax.rsqrt(mean_square + epsilon)[:, :, None, None, :]
    update = jnp.einsum("cmrq,cmktq->cmrtk", ortho, factor, precision=highest)
    fresh = (got_state.astype(jnp.float32) - feedback * update).astype(jnp.bfloat16)
    state_out = fresh.reshape(CAP, fresh.shape[1], rows, groups * columns)
    left_out = ortho * scale
    returned = lax.all_to_all(right_new, "tensor", split_axis=3, concat_axis=3, tiled=True)
    right_out = jnp.einsum("edc,cmkdq->emkq", owner_table, returned, precision=highest)
    return (state_out, left_out, right_out)


MESH = pl.DeviceIdType.MESH
HIGHEST = lax.Precision.HIGHEST
VMEM_BYTES = 48 * 1024 * 1024


def greet(shards_f, groups):
    f = lax.axis_index("fsdp")
    z = lax.axis_index("tensor")
    barrier = pltpu.get_barrier_semaphore()
    for j in range(1, shards_f):
        pl.semaphore_signal(
            barrier, inc=1, device_id={"fsdp": lax.rem(f + j, shards_f), "tensor": z}, device_id_type=MESH
        )
    for j in range(1, groups):
        pl.semaphore_signal(
            barrier, inc=1, device_id={"fsdp": f, "tensor": lax.rem(z + j, groups)}, device_id_type=MESH
        )
    pl.semaphore_wait(barrier, shards_f - 1 + groups - 1)
    return f, z


def remote(src, dst, send_sem, recv_sem, f, z):
    return pltpu.make_async_remote_copy(
        src_ref=src,
        dst_ref=dst,
        send_sem=send_sem,
        recv_sem=recv_sem,
        device_id={"fsdp": f, "tensor": z},
        device_id_type=MESH,
    )


def inverse_factor(aug, mats, rank):
    block = 32
    wide = (mats, block, 2 * block)
    wide_row = lax.broadcasted_iota(jnp.int32, wide, 1)
    wide_col = lax.broadcasted_iota(jnp.int32, wide, 2)
    on_diagonal = wide_row == wide_col
    small = (mats, block, block)
    small_eye = (lax.broadcasted_iota(jnp.int32, small, 1) == lax.broadcasted_iota(jnp.int32, small, 2)).astype(jnp.float32)
    for start in range(0, rank, block):
        stop = start + block

        def eliminate(k, both):
            row = jnp.sum(jnp.where(wide_row == k, both, 0.0), axis=1, keepdims=True)
            column = jnp.sum(jnp.where(wide_col == k, both, 0.0), axis=2, keepdims=True)
            pivot = jnp.sum(jnp.where(wide_col[:, :1] == k, row, 0.0), axis=2, keepdims=True)
            ratio = jnp.where(wide_row[:, :, :1] > k, column * (1.0 / pivot), 0.0)
            return both - ratio * row

        both = jnp.concatenate([aug[:, start:stop, start:stop], small_eye], axis=2)
        both = lax.fori_loop(0, block, eliminate, both, unroll=4)
        diagonal = jnp.sum(jnp.where(on_diagonal, both, 0.0), axis=2, keepdims=True)
        inverse = both[:, :, block:] * lax.rsqrt(diagonal)
        for m in range(mats):
            top = jnp.dot(inverse[m], aug[m, start:stop, :], precision=HIGHEST, preferred_element_type=jnp.float32)
            aug[m, start:stop, :] = top
            if stop < rank:
                below = top[:, :rank].T[stop:]
                aug[m, stop:, :] -= jnp.dot(below, top, precision=HIGHEST, preferred_element_type=jnp.float32)


def step_kernel(
    shards_f, groups, kinds,
    own_ref, m_ref, g_ref, r_ref,
    state_out, left_out, right_out,
    summed, sendbuf, got, pbuf, prelay, pjoin, pnear, pfar, pchunk,
    gram, gnear, gpair, ghalf, gchip, aug, wfull,
    obuf, fpart, fpair, fhalf, fchip, fchunk, fsend, lowbuf, sqbuf, sqrecv, rightbuf,
    p_send, p_recv, r_send, r_recv, x_send, x_recv, ga_send, ga_recv, gb_send, gb_recv,
    w_send, w_recv, o_send, o_recv, op_send, op_recv, fa_send, fa_recv, fb_send, fb_recv, fz_send, fz_recv,
    sq_send, sq_recv, low_send, low_recv, right_send, right_recv,
    s_send, first_recv, near_recv, second_recv, pass_send, pass_recv, out_sem,
):
    mats, rows, columns = m_ref.shape
    experts = mats // kinds
    slots = CAP * kinds
    rank = r_ref.shape[-1]
    units = 2 * mats // groups
    f, z = greet(shards_f, groups)
    core = lax.rem(f, 2)
    chip = f // 2
    chips = shards_f // 2
    pair = chip * 2 + 1 - core
    urows = rows // 2
    started = []

    def go(src, dst, send_sem, recv_sem, to_f, to_z):
        copy = remote(src, dst, send_sem, recv_sem, to_f, to_z)
        copy.start()
        started.append(copy)
        return copy

    def landed(dst, recv_sem):
        remote(dst, dst, recv_sem, recv_sem, f, z).wait_recv()

    near = z + 1 - 2 * lax.rem(z, 2)
    upper = z // 2
    inner = 2 - upper
    outer = 3 - 3 * upper
    far = 2 - 2 * upper
    is_inner = (z == 1) | (z == 2)
    is_outer = jnp.logical_not(is_inner)

    def relay(t, i, u):
        return remote(pbuf.at[u], prelay.at[t, i], r_send.at[t, i], r_recv.at[t, i], f, near)

    def across(t, i, d):
        return remote(pjoin.at[t, i], pfar.at[i], x_send.at[t, i], x_recv.at[i], f, d)

    for t, d in enumerate((outer, inner, near, z)):
        for i in range(units):
            u = d * units + i
            m = u // 2
            top = lax.rem(u, 2) * urows

            @pl.loop(0, urows // 128)
            def _(b):
                at = pl.ds(pl.multiple_of(top + b * 128, 128), 128)
                total = m_ref[m, at, :].astype(jnp.float32) + g_ref[m, at, :].astype(jnp.float32)
                low = total.astype(jnp.bfloat16)
                summed[m, at, :] = low
                pbuf[u, pl.ds(pl.multiple_of(b * 128, 128), 128), :] = jnp.dot(
                    low, r_ref[m], preferred_element_type=jnp.float32
                )

            if t < 2:
                @pl.when(is_outer)
                def _():
                    relay(t, i, u).start()

        if t == 2:
            go(pbuf.at[pl.ds(near * units, units)], pnear, p_send, p_recv, f, near)

    @pl.when(is_inner)
    def _():
        for t, d in enumerate((outer, inner)):
            for i in range(units):
                landed(prelay.at[t, i], r_recv.at[t, i])
                pjoin[t, i] = pbuf[d * units + i] + prelay[t, i]
                across(t, i, d).start()

    step = 128
    owner = [own_ref[e] for e in range(experts)]
    position = [sum(((owner[b] == owner[e]).astype(jnp.int32) for b in range(e)), jnp.int32(0)) for e in range(experts)]

    def taken(d, c):
        return sum((jnp.where((owner[e] == d) & (position[e] == c), e, 0) for e in range(experts)), jnp.int32(0))

    second = sum(
        (jnp.where((owner[e] // 2 == 1 - upper) & (position[e] == 1), e, 0) for e in range(experts)), jnp.int32(0)
    )
    picks = (second, taken(outer, 0), taken(inner, 0), taken(near, 0), taken(near, 1))
    for unit, expert in enumerate(picks):
        for k in range(kinds):
            @pl.loop(0, rows // step)
            def _(i):
                at = pl.ds(pl.multiple_of(i * step, step), step)
                sendbuf[unit, k, at, :] = summed[expert * kinds + k, at, :]
    here = pl.ds(pl.multiple_of(z * columns, columns), columns)
    for c in range(CAP):
        expert = taken(z, c)
        for k in range(kinds):
            @pl.loop(0, rows // step)
            def _(i):
                at = pl.ds(pl.multiple_of(i * step, step), step)
                got[c * kinds + k, at, here] = summed[expert * kinds + k, at, :]

    def place(c, source, k):
        return got.at[c * kinds + k, :, pl.ds(pl.multiple_of(source * columns, columns), columns)]

    def send(unit, c, recv, d, k):
        go(sendbuf.at[unit, k], place(c, z, k), s_send.at[unit, k], recv, f, d)

    def far_second(k):
        send(0, 1, second_recv.at[lax.rem(z, 2), k], inner, k)

    def far_outer(k):
        send(1, 0, first_recv.at[z, k], outer, k)

    def far_inner(k):
        send(2, 0, first_recv.at[z, k], inner, k)

    def near_first(k):
        send(3, 0, first_recv.at[z, k], near, k)

    def near_second(k):
        send(4, 1, near_recv.at[k], near, k)

    def hand_on(k):
        @pl.when(is_inner)
        def _():
            for i in range(2):
                block = place(1, far + i, k)
                landed(block, second_recv.at[i, k])
                remote(block, block, pass_send.at[i, k], pass_recv.at[i, k], f, near).start()

    odd = lax.rem(z, 2)
    landed(pnear, p_recv)
    for i in range(units):
        landed(pfar.at[i], x_recv.at[i])
        pchunk[i] = pbuf[z * units + i] + pnear[i] + pfar[i]

    def gram_of(i):
        panel = pchunk[i]
        return jnp.dot(panel.T, panel, precision=HIGHEST, preferred_element_type=jnp.float32)

    gram[2] = gram_of(2 - 2 * odd)
    shared = go(gram.at[2], gnear, ga_send.at[0], ga_recv.at[0], f, near)
    gram[0] = gram_of(odd) + gram_of(odd + 1)
    shared.wait_recv()
    gram[1] = gram[2] + gnear[...]
    far_second(0)
    near_second(0)
    far_second(1)
    near_second(1)
    near_first(0)
    near_first(1)
    far_outer(0)
    go(gram.at[1 - core], gpair, ga_send.at[1], ga_recv.at[1], pair, z).wait_recv()
    total = gram[core] + gpair[...]
    ghalf[...] = total
    for j in (2, 1, 3):
        go(
            ghalf, gchip.at[j - 1], gb_send.at[j - 1], gb_recv.at[j - 1],
            lax.rem(chip + j, chips) * 2 + core, z,
        )
    for j in range(1, chips):
        landed(gchip.at[j - 1], gb_recv.at[j - 1])
        total = total + gchip[j - 1]

    row_at = lax.broadcasted_iota(jnp.int32, (rank, rank), 0)
    col_at = lax.broadcasted_iota(jnp.int32, (rank, rank), 1)
    eye = (row_at == col_at).astype(jnp.float32)
    aug[0, :, :rank] = total + ridge_term * eye
    aug[0, :, rank:] = eye
    inverse_factor(aug, 1, rank)
    wfull[core] = aug[0, :, rank:]
    go(wfull.at[core], wfull.at[core], w_send, w_recv, pair, z)
    landed(wfull.at[1 - core], w_recv)

    for i, which in enumerate((odd, 0, 1 - odd)):
        ortho = jnp.dot(pchunk[i], wfull[which].T, precision=HIGHEST, preferred_element_type=jnp.float32)
        obuf[z * units + i] = ortho.astype(jnp.bfloat16)
    def chunk_of(source):
        return obuf.at[pl.ds(source * units, units)]

    def ortho_on(i):
        part = chunk_of(far + i)
        return remote(part, part, op_send.at[i], op_recv.at[i], f, near)

    go(chunk_of(z), chunk_of(z), o_send.at[0], o_recv.at[lax.rem(z, 2)], f, inner)
    go(chunk_of(z), chunk_of(z), o_send.at[1], o_recv.at[2], f, near)

    @pl.when(is_inner)
    def _():
        for i in range(2):
            landed(chunk_of(far + i), o_recv.at[i])
            ortho_on(i).start()

    landed(chunk_of(near), o_recv.at[2])

    @pl.when(is_outer)
    def _():
        for i in range(2):
            landed(chunk_of(far + i), op_recv.at[i])

    far_inner(0)
    hand_on(0)

    for m in range(mats):
        fpart[m] = jnp.dot(
            obuf[2 * m].T, summed[m, :urows], preferred_element_type=jnp.float32
        ) + jnp.dot(obuf[2 * m + 1].T, summed[m, urows:], preferred_element_type=jnp.float32)
        low_rows = rank // 2
        go(
            fpart.at[m, pl.ds(pl.multiple_of((1 - core) * low_rows, low_rows), low_rows), :],
            fpair.at[m], fa_send.at[m], fa_recv.at[m], pair, z,
        )
    piece = rank // shards_f
    own = pl.ds(pl.multiple_of(core * low_rows, low_rows), low_rows)
    for m in range(mats):
        landed(fpair.at[m], fa_recv.at[m])
        fhalf[m] = fpart[m, own, :] + fpair[m]
    for j in (2, 1, 3):
        other = lax.rem(chip + j, chips)
        go(
            fhalf.at[:, pl.ds(pl.multiple_of(other * piece, piece), piece), :],
            fchip.at[j - 1], fb_send.at[j - 1], fb_recv.at[j - 1], other * 2 + core, z,
        )
    total = fhalf[:, pl.ds(pl.multiple_of(chip * piece, piece), piece), :]
    for j in range(1, chips):
        landed(fchip.at[j - 1], fb_recv.at[j - 1])
        total = total + fchip[j - 1]
    square = total * total
    part_sum = square[:, :, :128]
    for lane in range(128, columns, 128):
        part_sum = part_sum + square[:, :, lane : lane + 128]
    sqbuf[...] = part_sum
    for j in (2, 3, 1):
        go(sqbuf, sqrecv.at[j - 1], sq_send.at[j - 1], sq_recv.at[j - 1], f, lax.rem(z + j, groups))
    fchunk[...] = total
    chunk = core * low_rows + chip * piece
    at = pl.ds(pl.multiple_of(chunk, piece), piece)
    for j in (2, 3, 1):
        d = lax.rem(z + j, groups)
        for c in range(CAP):
            expert = taken(d, c)
            for k in range(kinds):
                fsend[j - 1, c * kinds + k] = fchunk[expert * kinds + k].astype(jnp.bfloat16)
        go(fsend.at[j - 1], lowbuf.at[:, at, here], fz_send.at[j - 1], fz_recv.at[j - 1], f, d)
    hand_on(1)
    far_outer(1)
    far_inner(1)
    for c in range(CAP):
        expert = taken(z, c)
        for k in range(kinds):
            lowbuf[c * kinds + k, at, here] = fchunk[expert * kinds + k].astype(jnp.bfloat16)
    for j in range(1, groups):
        source = lax.rem(z + groups - j, groups)
        there = pl.ds(pl.multiple_of(source * columns, columns), columns)
        landed(lowbuf.at[:, at, there], fz_recv.at[j - 1])
    for j in (2, 1, 3):
        part = lowbuf.at[:, at, :]
        go(part, part, low_send.at[j - 1], low_recv.at[j - 1], lax.rem(chip + j, chips) * 2 + core, z)
    square = sqbuf[...]
    for j in range(1, groups):
        landed(sqrecv.at[j - 1], sq_recv.at[j - 1])
        square = square + sqrecv[j - 1]
    mean_square = jnp.sum(square, axis=2, keepdims=True) / (groups * columns)
    rightbuf[:, at, :] = fchunk[...] * lax.rsqrt(mean_square + epsilon)
    for j in (2, 1, 3):
        part = rightbuf.at[:, at, :]
        go(part, part, right_send.at[j - 1], right_recv.at[j - 1], lax.rem(chip + j, chips) * 2 + core, z)
    theirs = pl.ds(pl.multiple_of((1 - core) * low_rows, low_rows), low_rows)
    for buffer, sent, recv in ((lowbuf, low_send, low_recv), (rightbuf, right_send, right_recv)):
        for j in range(1, chips):
            start = core * low_rows + lax.rem(chip + chips - j, chips) * piece
            landed(buffer.at[:, pl.ds(pl.multiple_of(start, piece), piece), :], recv.at[j - 1])
        part = buffer.at[:, own, :]
        go(part, part, sent.at[chips - 1], recv.at[chips - 1], pair, z)
    def present(c):
        return sum(((owner[e] == z) & (position[e] == c)).astype(jnp.int32) for e in range(experts)) > 0

    for c in range(CAP):
        expert = taken(z, c)
        for k in range(kinds):
            for h in range(2):
                left = obuf[(expert * kinds + k) * 2 + h].astype(jnp.float32) * math.sqrt(D)
                left_out[c * kinds + k, h * urows : (h + 1) * urows] = jnp.where(present(c), left, 0.0)

    landed(lowbuf.at[:, theirs, :], low_recv.at[chips - 1])
    kept = []

    def keep(c, source, k):
        m = c * kinds + k
        there = pl.ds(pl.multiple_of(source * columns, columns), columns)
        expert = taken(z, c)
        used = present(c)
        for h in range(2):
            @pl.loop(0, urows // 128)
            def _(b):
                at = pl.ds(pl.multiple_of(h * urows + b * 128, 128), 128)
                low = obuf[(expert * kinds + k) * 2 + h, pl.ds(pl.multiple_of(b * 128, 128), 128), :]
                update = jnp.dot(low, lowbuf[m, :, there], preferred_element_type=jnp.float32)
                fresh = got[m, at, there].astype(jnp.float32) - feedback * update
                got[m, at, there] = jnp.where(used, fresh, 0.0).astype(jnp.bfloat16)
        copy = pltpu.make_async_copy(place(c, source, k), state_out.at[m, :, there], out_sem.at[len(kept)])
        copy.start()
        kept.append(copy)

    for c in range(CAP):
        for k in range(kinds):
            keep(c, z, k)
    landed(rightbuf.at[:, theirs, :], right_recv.at[chips - 1])
    for m in range(mats):
        right_out[m] = rightbuf[m].T
    for k in range(kinds):
        landed(place(1, near, k), near_recv.at[k])
        keep(1, near, k)
    for k in range(kinds):
        landed(place(0, near, k), first_recv.at[near, k])
        keep(0, near, k)
    for k in range(kinds):
        for i in range(2):
            landed(place(0, far + i, k), first_recv.at[far + i, k])
            keep(0, far + i, k)

        @pl.when(is_inner)
        def _():
            for i in range(2):
                block = place(1, far + i, k)
                remote(block, block, pass_send.at[i, k], pass_recv.at[i, k], f, near).wait_send()

        @pl.when(is_outer)
        def _():
            for i in range(2):
                landed(place(1, far + i, k), pass_recv.at[i, k])

        for i in range(2):
            keep(1, far + i, k)

    @pl.when(is_inner)
    def _():
        for i in range(2):
            ortho_on(i).wait_send()
        for t, d in enumerate((outer, inner)):
            for i in range(units):
                across(t, i, d).wait_send()

    @pl.when(is_outer)
    def _():
        for t, d in enumerate((outer, inner)):
            for i in range(units):
                relay(t, i, d * units + i).wait_send()

    for copy in started:
        copy.wait_send()
    for copy in kept:
        copy.wait()


def shards(momentum, gradient, right_in, owners):
    groups = lax.axis_size("tensor")
    shards_f = lax.axis_size("fsdp")
    experts, kinds, rows, columns = momentum.shape
    rank = right_in.shape[-1]
    hidden = groups * columns
    mats = CAP * kinds
    smem = pl.BlockSpec(memory_space=pltpu.SMEM)
    vmem = pl.BlockSpec(memory_space=pltpu.VMEM)
    hbm = pl.BlockSpec(memory_space=pl.ANY)
    f32, bf16 = jnp.float32, jnp.bfloat16
    shape = jax.ShapeDtypeStruct
    dma = pltpu.SemaphoreType.DMA
    chips = shards_f // 2
    every = experts * kinds
    units = 2 * every // groups
    piece = rank // shards_f
    near_z, near_c = groups - 1, chips - 1
    state, left, right = pl.pallas_call(
        functools.partial(step_kernel, shards_f, groups, kinds),
        out_shape=(
            pltpu.VMEM((mats, rows, hidden), bf16),
            pltpu.VMEM((mats, rows, rank), f32),
            pltpu.VMEM((every, columns, rank), f32),
        ),
        in_specs=[smem, vmem, vmem, vmem],
        out_specs=(vmem, vmem, vmem),
        scratch_shapes=[
            pltpu.VMEM((every, rows, columns), bf16),
            pltpu.VMEM((5, kinds, rows, columns), bf16),
            pltpu.VMEM((mats, rows, hidden), bf16),
            pltpu.VMEM((2 * every, rows // 2, rank), f32),
            pltpu.VMEM((2, units, rows // 2, rank), f32),
            pltpu.VMEM((2, units, rows // 2, rank), f32),
            pltpu.VMEM((units, rows // 2, rank), f32),
            pltpu.VMEM((units, rows // 2, rank), f32),
            pltpu.VMEM((units, rows // 2, rank), f32),
            pltpu.VMEM((3, rank, rank), f32),
            pltpu.VMEM((rank, rank), f32),
            pltpu.VMEM((rank, rank), f32),
            pltpu.VMEM((rank, rank), f32),
            pltpu.VMEM((near_c, rank, rank), f32),
            pltpu.VMEM((1, rank, 2 * rank), f32),
            pltpu.VMEM((2, rank, rank), f32),
            pltpu.VMEM((2 * every, rows // 2, rank), bf16),
            pltpu.VMEM((every, rank, columns), f32),
            pltpu.VMEM((every, rank // 2, columns), f32),
            pltpu.VMEM((every, rank // 2, columns), f32),
            pltpu.VMEM((near_c, every, piece, columns), f32),
            pltpu.VMEM((every, piece, columns), f32),
            pltpu.VMEM((near_z, mats, piece, columns), bf16),
            pltpu.VMEM((mats, rank, hidden), bf16),
            pltpu.VMEM((every, piece, 128), f32),
            pltpu.VMEM((near_z, every, piece, 128), f32),
            pltpu.VMEM((every, rank, columns), f32),
            dma, dma,
            dma((2, units)), dma((2, units)),
            dma((2, units)), dma((units,)),
            dma((2,)), dma((2,)),
            dma((near_c,)), dma((near_c,)),
            dma, dma,
            dma((2,)), dma((3,)), dma((2,)), dma((2,)),
            dma((every,)), dma((every,)),
            dma((near_c,)), dma((near_c,)),
            dma((near_z,)), dma((near_z,)),
            dma((near_z,)), dma((near_z,)),
            dma((chips,)), dma((chips,)),
            dma((chips,)), dma((chips,)),
            dma((5, kinds)), dma((groups, kinds)), dma((kinds,)),
            dma((2, kinds)), dma((2, kinds)), dma((2, kinds)), dma((groups * mats,)),
        ],
        compiler_params=pltpu.CompilerParams(
            collective_id=0, has_side_effects=True, vmem_limit_bytes=VMEM_BYTES
        ),
        name="step",
    )(
        owners,
        momentum.reshape(every, rows, columns),
        gradient.reshape(every, rows, columns),
        right_in.reshape(every, columns, rank),
    )

    right_new = right.reshape(experts, kinds, columns, rank)
    return (
        state.reshape(CAP, kinds, rows, hidden),
        left.reshape(CAP, kinds, rows, rank),
        right_new,
    )


def solution(mesh):
    fits = mesh.shape["fsdp"] == 8 and mesh.shape["tensor"] == 4
    return jax.shard_map(
        shards if fits else general_shards,
        mesh=mesh,
        in_specs=(
            P(None, None, "fsdp", "tensor"),
            P(None, None, "fsdp", "tensor"),
            P(None, None, "tensor", None),
            P(),
        ),
        out_specs=(
            P("tensor", None, "fsdp", None),
            P("tensor", None, "fsdp", None),
            P(None, None, "tensor", None),
        ),
        check_vma=False,
    )
```

```python
import functools
import math

import jax
import jax.numpy as jnp
from jax import lax
from jax.experimental import pallas as pl
from jax.experimental.pallas import tpu as pltpu
from jax.sharding import PartitionSpec as P

D = 4096
CAP = 2


ridge_term = 0.001
feedback = 0.1
epsilon = 1e-06


def orthonormal(panel, gram_total):
    eye_matrix = jnp.eye(gram_total.shape[-1], dtype=jnp.float32)
    lower_factor = jnp.linalg.cholesky(gram_total + ridge_term * eye_matrix)
    solved = jax.scipy.linalg.solve_triangular(
        lower_factor, jnp.swapaxes(panel, -1, -2), lower=True
    )
    return jnp.swapaxes(solved, -1, -2)


def slot_table(owners, groups, capacity):
    count = owners.shape[0]
    index_line = jnp.arange(count, dtype=jnp.int32)
    same_owner = owners[:, None] == owners[None, :]
    earlier = index_line[None, :] < index_line[:, None]
    position = jnp.sum((same_owner & earlier).astype(jnp.int32), axis=1)
    owner_hit = owners[:, None, None] == jnp.arange(groups, dtype=jnp.int32)[None, :, None]
    slot_hit = position[:, None, None] == jnp.arange(capacity, dtype=jnp.int32)[None, None, :]
    return (owner_hit & slot_hit).astype(jnp.float32)


def general_shards(momentum, gradient, right_in, owners):
    highest = lax.Precision.HIGHEST
    groups = lax.axis_size("tensor")
    rows = momentum.shape[2]
    columns = momentum.shape[3]
    owner_table = slot_table(owners, groups, CAP)
    table_low = owner_table.astype(jnp.bfloat16)
    summed = (momentum.astype(jnp.float32) + gradient.astype(jnp.float32)).astype(jnp.bfloat16)
    scale = math.sqrt(D)
    send_state = jnp.einsum(
        "edc,emrk->cmrdk", table_low, summed, preferred_element_type=jnp.float32
    ).astype(jnp.bfloat16)
    send_right = jnp.einsum(
        "edc,emkq->cmkdq", table_low, right_in, preferred_element_type=jnp.float32
    ).astype(jnp.bfloat16)
    got_state, got_right = (
        lax.all_to_all(send_state, "tensor", split_axis=3, concat_axis=3, tiled=True),
        lax.all_to_all(send_right, "tensor", split_axis=3, concat_axis=3, tiled=True),
    )
    panel = jnp.einsum(
        "cmrtk,cmktq->cmrq", got_state, got_right, preferred_element_type=jnp.float32
    )
    gram_part = jnp.einsum("cmrq,cmrs->cmqs", panel, panel, precision=highest)
    gram_total = lax.psum(gram_part, "fsdp")
    ortho = orthonormal(panel, gram_total)
    ortho_low = ortho.astype(jnp.bfloat16)
    factor_part = jnp.einsum(
        "cmrtk,cmrq->cmktq", got_state, ortho_low, preferred_element_type=jnp.float32
    )
    factor = lax.psum(factor_part, "fsdp")
    mean_square = jnp.mean(factor * factor, axis=(2, 3))
    right_new = factor * lax.rsqrt(mean_square + epsilon)[:, :, None, None, :]
    update = jnp.einsum("cmrq,cmktq->cmrtk", ortho, factor, precision=highest)
    fresh = (got_state.astype(jnp.float32) - feedback * update).astype(jnp.bfloat16)
    state_out = fresh.reshape(CAP, fresh.shape[1], rows, groups * columns)
    left_out = ortho * scale
    returned = lax.all_to_all(right_new, "tensor", split_axis=3, concat_axis=3, tiled=True)
    right_out = jnp.einsum("edc,cmkdq->emkq", owner_table, returned, precision=highest)
    return (state_out, left_out, right_out)


MESH = pl.DeviceIdType.MESH
HIGHEST = lax.Precision.HIGHEST
VMEM_BYTES = 48 * 1024 * 1024


def greet(shards_f, groups):
    f = lax.axis_index("fsdp")
    z = lax.axis_index("tensor")
    barrier = pltpu.get_barrier_semaphore()
    for j in range(1, shards_f):
        pl.semaphore_signal(
            barrier, inc=1, device_id={"fsdp": lax.rem(f + j, shards_f), "tensor": z}, device_id_type=MESH
        )
    for j in range(1, groups):
        pl.semaphore_signal(
            barrier, inc=1, device_id={"fsdp": f, "tensor": lax.rem(z + j, groups)}, device_id_type=MESH
        )
    pl.semaphore_wait(barrier, shards_f - 1 + groups - 1)
    return f, z


def remote(src, dst, send_sem, recv_sem, f, z):
    return pltpu.make_async_remote_copy(
        src_ref=src,
        dst_ref=dst,
        send_sem=send_sem,
        recv_sem=recv_sem,
        device_id={"fsdp": f, "tensor": z},
        device_id_type=MESH,
    )


def inverse_factor(aug, mats, rank):
    block = 32
    wide = (mats, block, 2 * block)
    wide_row = lax.broadcasted_iota(jnp.int32, wide, 1)
    wide_col = lax.broadcasted_iota(jnp.int32, wide, 2)
    on_diagonal = wide_row == wide_col
    small = (mats, block, block)
    small_eye = (lax.broadcasted_iota(jnp.int32, small, 1) == lax.broadcasted_iota(jnp.int32, small, 2)).astype(jnp.float32)
    for start in range(0, rank, block):
        stop = start + block

        def eliminate(k, both):
            row = jnp.sum(jnp.where(wide_row == k, both, 0.0), axis=1, keepdims=True)
            column = jnp.sum(jnp.where(wide_col == k, both, 0.0), axis=2, keepdims=True)
            pivot = jnp.sum(jnp.where(wide_col[:, :1] == k, row, 0.0), axis=2, keepdims=True)
            ratio = jnp.where(wide_row[:, :, :1] > k, column * (1.0 / pivot), 0.0)
            return both - ratio * row

        both = jnp.concatenate([aug[:, start:stop, start:stop], small_eye], axis=2)
        both = lax.fori_loop(0, block, eliminate, both, unroll=4)
        diagonal = jnp.sum(jnp.where(on_diagonal, both, 0.0), axis=2, keepdims=True)
        inverse = both[:, :, block:] * lax.rsqrt(diagonal)
        for m in range(mats):
            top = jnp.dot(inverse[m], aug[m, start:stop, :], precision=HIGHEST, preferred_element_type=jnp.float32)
            aug[m, start:stop, :] = top
            if stop < rank:
                below = top[:, :rank].T[stop:]
                aug[m, stop:, :] -= jnp.dot(below, top, precision=HIGHEST, preferred_element_type=jnp.float32)


def step_kernel(
    shards_f, groups, kinds,
    own_ref, m_ref, g_ref, r_ref,
    state_out, left_out, right_out,
    summed, sendbuf, got, pbuf, prelay, pjoin, pnear, pfar, pchunk,
    gram, gnear, gpair, ghalf, gchip, aug, wfull,
    obuf, fpart, fpair, fhalf, fchip, fchunk, fsend, lowbuf, sqbuf, sqrecv, rightbuf,
    p_send, p_recv, r_send, r_recv, x_send, x_recv, ga_send, ga_recv, gb_send, gb_recv,
    w_send, w_recv, o_send, o_recv, op_send, op_recv, fa_send, fa_recv, fb_send, fb_recv, fz_send, fz_recv,
    sq_send, sq_recv, low_send, low_recv, right_send, right_recv,
    s_send, first_recv, near_recv, second_recv, pass_send, pass_recv, out_sem,
):
    mats, rows, columns = m_ref.shape
    experts = mats // kinds
    slots = CAP * kinds
    rank = r_ref.shape[-1]
    units = 2 * mats // groups
    f, z = greet(shards_f, groups)
    core = lax.rem(f, 2)
    chip = f // 2
    chips = shards_f // 2
    pair = chip * 2 + 1 - core
    urows = rows // 2
    started = []

    def go(src, dst, send_sem, recv_sem, to_f, to_z):
        copy = remote(src, dst, send_sem, recv_sem, to_f, to_z)
        copy.start()
        started.append(copy)
        return copy

    def landed(dst, recv_sem):
        remote(dst, dst, recv_sem, recv_sem, f, z).wait_recv()

    near = z + 1 - 2 * lax.rem(z, 2)
    upper = z // 2
    inner = 2 - upper
    outer = 3 - 3 * upper
    far = 2 - 2 * upper
    is_inner = (z == 1) | (z == 2)
    is_outer = jnp.logical_not(is_inner)

    def relay(t, i, u):
        return remote(pbuf.at[u], prelay.at[t, i], r_send.at[t, i], r_recv.at[t, i], f, near)

    def across(t, i, d):
        return remote(pjoin.at[t, i], pfar.at[i], x_send.at[t, i], x_recv.at[i], f, d)

    for t, d in enumerate((outer, inner, near, z)):
        for i in range(units):
            u = d * units + i
            m = u // 2
            top = lax.rem(u, 2) * urows

            @pl.loop(0, urows // 128)
            def _(b):
                at = pl.ds(pl.multiple_of(top + b * 128, 128), 128)
                total = m_ref[m, at, :].astype(jnp.float32) + g_ref[m, at, :].astype(jnp.float32)
                low = total.astype(jnp.bfloat16)
                summed[m, at, :] = low
                pbuf[u, pl.ds(pl.multiple_of(b * 128, 128), 128), :] = jnp.dot(
                    low, r_ref[m], preferred_element_type=jnp.float32
                )

            if t < 2:
                @pl.when(is_outer)
                def _():
                    relay(t, i, u).start()

        if t == 2:
            go(pbuf.at[pl.ds(near * units, units)], pnear, p_send, p_recv, f, near)

    @pl.when(is_inner)
    def _():
        for t, d in enumerate((outer, inner)):
            for i in range(units):
                landed(prelay.at[t, i], r_recv.at[t, i])
                pjoin[t, i] = pbuf[d * units + i] + prelay[t, i]
                across(t, i, d).start()

    step = 128
    owner = [own_ref[e] for e in range(experts)]
    position = [sum(((owner[b] == owner[e]).astype(jnp.int32) for b in range(e)), jnp.int32(0)) for e in range(experts)]

    def taken(d, c):
        return sum((jnp.where((owner[e] == d) & (position[e] == c), e, 0) for e in range(experts)), jnp.int32(0))

    second = sum(
        (jnp.where((owner[e] // 2 == 1 - upper) & (position[e] == 1), e, 0) for e in range(experts)), jnp.int32(0)
    )
    picks = (second, taken(outer, 0), taken(inner, 0), taken(near, 0), taken(near, 1))
    for unit, expert in enumerate(picks):
        for k in range(kinds):
            @pl.loop(0, rows // step)
            def _(i):
                at = pl.ds(pl.multiple_of(i * step, step), step)
                sendbuf[unit, k, at, :] = summed[expert * kinds + k, at, :]
    here = pl.ds(pl.multiple_of(z * columns, columns), columns)
    for c in range(CAP):
        expert = taken(z, c)
        for k in range(kinds):
            @pl.loop(0, rows // step)
            def _(i):
                at = pl.ds(pl.multiple_of(i * step, step), step)
                got[c * kinds + k, at, here] = summed[expert * kinds + k, at, :]

    def place(c, source, k):
        return got.at[c * kinds + k, :, pl.ds(pl.multiple_of(source * columns, columns), columns)]

    def send(unit, c, recv, d, k):
        go(sendbuf.at[unit, k], place(c, z, k), s_send.at[unit, k], recv, f, d)

    def far_second(k):
        send(0, 1, second_recv.at[lax.rem(z, 2), k], inner, k)

    def far_outer(k):
        send(1, 0, first_recv.at[z, k], outer, k)

    def far_inner(k):
        send(2, 0, first_recv.at[z, k], inner, k)

    def near_first(k):
        send(3, 0, first_recv.at[z, k], near, k)

    def near_second(k):
        send(4, 1, near_recv.at[k], near, k)

    def hand_on(k):
        @pl.when(is_inner)
        def _():
            for i in range(2):
                block = place(1, far + i, k)
                landed(block, second_recv.at[i, k])
                remote(block, block, pass_send.at[i, k], pass_recv.at[i, k], f, near).start()

    odd = lax.rem(z, 2)
    landed(pnear, p_recv)
    for i in range(units):
        landed(pfar.at[i], x_recv.at[i])
        pchunk[i] = pbuf[z * units + i] + pnear[i] + pfar[i]

    def gram_of(i):
        panel = pchunk[i]
        return jnp.dot(panel.T, panel, precision=HIGHEST, preferred_element_type=jnp.float32)

    gram[2] = gram_of(2 - 2 * odd)
    shared = go(gram.at[2], gnear, ga_send.at[0], ga_recv.at[0], f, near)
    gram[0] = gram_of(odd) + gram_of(odd + 1)
    shared.wait_recv()
    gram[1] = gram[2] + gnear[...]
    go(gram.at[1 - core], gpair, ga_send.at[1], ga_recv.at[1], pair, z).wait_recv()
    total = gram[core] + gpair[...]
    ghalf[...] = total
    for j in (2, 1, 3):
        go(
            ghalf, gchip.at[j - 1], gb_send.at[j - 1], gb_recv.at[j - 1],
            lax.rem(chip + j, chips) * 2 + core, z,
        )
    far_second(0)
    near_second(0)
    far_second(1)
    near_second(1)
    near_first(0)
    near_first(1)
    far_outer(0)
    for j in range(1, chips):
        landed(gchip.at[j - 1], gb_recv.at[j - 1])
        total = total + gchip[j - 1]

    row_at = lax.broadcasted_iota(jnp.int32, (rank, rank), 0)
    col_at = lax.broadcasted_iota(jnp.int32, (rank, rank), 1)
    eye = (row_at == col_at).astype(jnp.float32)
    aug[0, :, :rank] = total + ridge_term * eye
    aug[0, :, rank:] = eye
    inverse_factor(aug, 1, rank)
    wfull[core] = aug[0, :, rank:]
    go(wfull.at[core], wfull.at[core], w_send, w_recv, pair, z)
    landed(wfull.at[1 - core], w_recv)

    for i, which in enumerate((odd, 0, 1 - odd)):
        ortho = jnp.dot(pchunk[i], wfull[which].T, precision=HIGHEST, preferred_element_type=jnp.float32)
        obuf[z * units + i] = ortho.astype(jnp.bfloat16)
    def chunk_of(source):
        return obuf.at[pl.ds(source * units, units)]

    def ortho_on(i):
        part = chunk_of(far + i)
        return remote(part, part, op_send.at[i], op_recv.at[i], f, near)

    go(chunk_of(z), chunk_of(z), o_send.at[0], o_recv.at[lax.rem(z, 2)], f, inner)
    go(chunk_of(z), chunk_of(z), o_send.at[1], o_recv.at[2], f, near)

    @pl.when(is_inner)
    def _():
        for i in range(2):
            landed(chunk_of(far + i), o_recv.at[i])
            ortho_on(i).start()

    landed(chunk_of(near), o_recv.at[2])

    @pl.when(is_outer)
    def _():
        for i in range(2):
            landed(chunk_of(far + i), op_recv.at[i])

    for m in range(mats):
        fpart[m] = jnp.dot(
            obuf[2 * m].T, summed[m, :urows], preferred_element_type=jnp.float32
        ) + jnp.dot(obuf[2 * m + 1].T, summed[m, urows:], preferred_element_type=jnp.float32)
        low_rows = rank // 2
        go(
            fpart.at[m, pl.ds(pl.multiple_of((1 - core) * low_rows, low_rows), low_rows), :],
            fpair.at[m], fa_send.at[m], fa_recv.at[m], pair, z,
        )
    piece = rank // shards_f
    own = pl.ds(pl.multiple_of(core * low_rows, low_rows), low_rows)
    for m in range(mats):
        landed(fpair.at[m], fa_recv.at[m])
        fhalf[m] = fpart[m, own, :] + fpair[m]
    for j in (2, 1, 3):
        other = lax.rem(chip + j, chips)
        go(
            fhalf.at[:, pl.ds(pl.multiple_of(other * piece, piece), piece), :],
            fchip.at[j - 1], fb_send.at[j - 1], fb_recv.at[j - 1], other * 2 + core, z,
        )
    total = fhalf[:, pl.ds(pl.multiple_of(chip * piece, piece), piece), :]
    far_inner(0)
    hand_on(0)
    for j in range(1, chips):
        landed(fchip.at[j - 1], fb_recv.at[j - 1])
        total = total + fchip[j - 1]
    square = total * total
    part_sum = square[:, :, :128]
    for lane in range(128, columns, 128):
        part_sum = part_sum + square[:, :, lane : lane + 128]
    sqbuf[...] = part_sum
    for j in (2, 3, 1):
        go(sqbuf, sqrecv.at[j - 1], sq_send.at[j - 1], sq_recv.at[j - 1], f, lax.rem(z + j, groups))
    fchunk[...] = total
    chunk = core * low_rows + chip * piece
    at = pl.ds(pl.multiple_of(chunk, piece), piece)
    for j in (2, 3, 1):
        d = lax.rem(z + j, groups)
        for c in range(CAP):
            expert = taken(d, c)
            for k in range(kinds):
                fsend[j - 1, c * kinds + k] = fchunk[expert * kinds + k].astype(jnp.bfloat16)
        go(fsend.at[j - 1], lowbuf.at[:, at, here], fz_send.at[j - 1], fz_recv.at[j - 1], f, d)
    hand_on(1)
    far_outer(1)
    far_inner(1)
    for c in range(CAP):
        expert = taken(z, c)
        for k in range(kinds):
            lowbuf[c * kinds + k, at, here] = fchunk[expert * kinds + k].astype(jnp.bfloat16)
    for j in range(1, groups):
        source = lax.rem(z + groups - j, groups)
        there = pl.ds(pl.multiple_of(source * columns, columns), columns)
        landed(lowbuf.at[:, at, there], fz_recv.at[j - 1])
    for j in (2, 1, 3):
        part = lowbuf.at[:, at, :]
        go(part, part, low_send.at[j - 1], low_recv.at[j - 1], lax.rem(chip + j, chips) * 2 + core, z)
    square = sqbuf[...]
    for j in range(1, groups):
        landed(sqrecv.at[j - 1], sq_recv.at[j - 1])
        square = square + sqrecv[j - 1]
    mean_square = jnp.sum(square, axis=2, keepdims=True) / (groups * columns)
    rightbuf[:, at, :] = fchunk[...] * lax.rsqrt(mean_square + epsilon)
    for j in (2, 1, 3):
        part = rightbuf.at[:, at, :]
        go(part, part, right_send.at[j - 1], right_recv.at[j - 1], lax.rem(chip + j, chips) * 2 + core, z)
    theirs = pl.ds(pl.multiple_of((1 - core) * low_rows, low_rows), low_rows)
    for buffer, sent, recv in ((lowbuf, low_send, low_recv), (rightbuf, right_send, right_recv)):
        for j in range(1, chips):
            start = core * low_rows + lax.rem(chip + chips - j, chips) * piece
            landed(buffer.at[:, pl.ds(pl.multiple_of(start, piece), piece), :], recv.at[j - 1])
        part = buffer.at[:, own, :]
        go(part, part, sent.at[chips - 1], recv.at[chips - 1], pair, z)
    def present(c):
        return sum(((owner[e] == z) & (position[e] == c)).astype(jnp.int32) for e in range(experts)) > 0

    for c in range(CAP):
        expert = taken(z, c)
        for k in range(kinds):
            for h in range(2):
                left = obuf[(expert * kinds + k) * 2 + h].astype(jnp.float32) * math.sqrt(D)
                left_out[c * kinds + k, h * urows : (h + 1) * urows] = jnp.where(present(c), left, 0.0)

    landed(lowbuf.at[:, theirs, :], low_recv.at[chips - 1])
    kept = []

    def keep(c, source, k):
        m = c * kinds + k
        there = pl.ds(pl.multiple_of(source * columns, columns), columns)
        expert = taken(z, c)
        used = present(c)
        for h in range(2):
            @pl.loop(0, urows // 128)
            def _(b):
                at = pl.ds(pl.multiple_of(h * urows + b * 128, 128), 128)
                low = obuf[(expert * kinds + k) * 2 + h, pl.ds(pl.multiple_of(b * 128, 128), 128), :]
                update = jnp.dot(low, lowbuf[m, :, there], preferred_element_type=jnp.float32)
                fresh = got[m, at, there].astype(jnp.float32) - feedback * update
                got[m, at, there] = jnp.where(used, fresh, 0.0).astype(jnp.bfloat16)
        copy = pltpu.make_async_copy(place(c, source, k), state_out.at[m, :, there], out_sem.at[len(kept)])
        copy.start()
        kept.append(copy)

    for c in range(CAP):
        for k in range(kinds):
            keep(c, z, k)
    landed(rightbuf.at[:, theirs, :], right_recv.at[chips - 1])
    for m in range(mats):
        right_out[m] = rightbuf[m].T
    for k in range(kinds):
        landed(place(1, near, k), near_recv.at[k])
        keep(1, near, k)
    for k in range(kinds):
        landed(place(0, near, k), first_recv.at[near, k])
        keep(0, near, k)
    for k in range(kinds):
        for i in range(2):
            landed(place(0, far + i, k), first_recv.at[far + i, k])
            keep(0, far + i, k)

        @pl.when(is_inner)
        def _():
            for i in range(2):
                block = place(1, far + i, k)
                remote(block, block, pass_send.at[i, k], pass_recv.at[i, k], f, near).wait_send()

        @pl.when(is_outer)
        def _():
            for i in range(2):
                landed(place(1, far + i, k), pass_recv.at[i, k])

        for i in range(2):
            keep(1, far + i, k)

    @pl.when(is_inner)
    def _():
        for i in range(2):
            ortho_on(i).wait_send()
        for t, d in enumerate((outer, inner)):
            for i in range(units):
                across(t, i, d).wait_send()

    @pl.when(is_outer)
    def _():
        for t, d in enumerate((outer, inner)):
            for i in range(units):
                relay(t, i, d * units + i).wait_send()

    for copy in started:
        copy.wait_send()
    for copy in kept:
        copy.wait()


def shards(momentum, gradient, right_in, owners):
    groups = lax.axis_size("tensor")
    shards_f = lax.axis_size("fsdp")
    experts, kinds, rows, columns = momentum.shape
    rank = right_in.shape[-1]
    hidden = groups * columns
    mats = CAP * kinds
    smem = pl.BlockSpec(memory_space=pltpu.SMEM)
    vmem = pl.BlockSpec(memory_space=pltpu.VMEM)
    hbm = pl.BlockSpec(memory_space=pl.ANY)
    f32, bf16 = jnp.float32, jnp.bfloat16
    shape = jax.ShapeDtypeStruct
    dma = pltpu.SemaphoreType.DMA
    chips = shards_f // 2
    every = experts * kinds
    units = 2 * every // groups
    piece = rank // shards_f
    near_z, near_c = groups - 1, chips - 1
    state, left, right = pl.pallas_call(
        functools.partial(step_kernel, shards_f, groups, kinds),
        out_shape=(
            pltpu.VMEM((mats, rows, hidden), bf16),
            pltpu.VMEM((mats, rows, rank), f32),
            pltpu.VMEM((every, columns, rank), f32),
        ),
        in_specs=[smem, vmem, vmem, vmem],
        out_specs=(vmem, vmem, vmem),
        scratch_shapes=[
            pltpu.VMEM((every, rows, columns), bf16),
            pltpu.VMEM((5, kinds, rows, columns), bf16),
            pltpu.VMEM((mats, rows, hidden), bf16),
            pltpu.VMEM((2 * every, rows // 2, rank), f32),
            pltpu.VMEM((2, units, rows // 2, rank), f32),
            pltpu.VMEM((2, units, rows // 2, rank), f32),
            pltpu.VMEM((units, rows // 2, rank), f32),
            pltpu.VMEM((units, rows // 2, rank), f32),
            pltpu.VMEM((units, rows // 2, rank), f32),
            pltpu.VMEM((3, rank, rank), f32),
            pltpu.VMEM((rank, rank), f32),
            pltpu.VMEM((rank, rank), f32),
            pltpu.VMEM((rank, rank), f32),
            pltpu.VMEM((near_c, rank, rank), f32),
            pltpu.VMEM((1, rank, 2 * rank), f32),
            pltpu.VMEM((2, rank, rank), f32),
            pltpu.VMEM((2 * every, rows // 2, rank), bf16),
            pltpu.VMEM((every, rank, columns), f32),
            pltpu.VMEM((every, rank // 2, columns), f32),
            pltpu.VMEM((every, rank // 2, columns), f32),
            pltpu.VMEM((near_c, every, piece, columns), f32),
            pltpu.VMEM((every, piece, columns), f32),
            pltpu.VMEM((near_z, mats, piece, columns), bf16),
            pltpu.VMEM((mats, rank, hidden), bf16),
            pltpu.VMEM((every, piece, 128), f32),
            pltpu.VMEM((near_z, every, piece, 128), f32),
            pltpu.VMEM((every, rank, columns), f32),
            dma, dma,
            dma((2, units)), dma((2, units)),
            dma((2, units)), dma((units,)),
            dma((2,)), dma((2,)),
            dma((near_c,)), dma((near_c,)),
            dma, dma,
            dma((2,)), dma((3,)), dma((2,)), dma((2,)),
            dma((every,)), dma((every,)),
            dma((near_c,)), dma((near_c,)),
            dma((near_z,)), dma((near_z,)),
            dma((near_z,)), dma((near_z,)),
            dma((chips,)), dma((chips,)),
            dma((chips,)), dma((chips,)),
            dma((5, kinds)), dma((groups, kinds)), dma((kinds,)),
            dma((2, kinds)), dma((2, kinds)), dma((2, kinds)), dma((groups * mats,)),
        ],
        compiler_params=pltpu.CompilerParams(
            collective_id=0, has_side_effects=True, vmem_limit_bytes=VMEM_BYTES
        ),
        name="step",
    )(
        owners,
        momentum.reshape(every, rows, columns),
        gradient.reshape(every, rows, columns),
        right_in.reshape(every, columns, rank),
    )

    right_new = right.reshape(experts, kinds, columns, rank)
    return (
        state.reshape(CAP, kinds, rows, hidden),
        left.reshape(CAP, kinds, rows, rank),
        right_new,
    )


def solution(mesh):
    fits = mesh.shape["fsdp"] == 8 and mesh.shape["tensor"] == 4
    return jax.shard_map(
        shards if fits else general_shards,
        mesh=mesh,
        in_specs=(
            P(None, None, "fsdp", "tensor"),
            P(None, None, "fsdp", "tensor"),
            P(None, None, "tensor", None),
            P(),
        ),
        out_specs=(
            P("tensor", None, "fsdp", None),
            P("tensor", None, "fsdp", None),
            P(None, None, "tensor", None),
        ),
        check_vma=False,
    )
```
